32 devices in a mesh: dp: 8 (over y, x, core), tensor: 4 (over z).
Axes of the slice: x: 2, y: 2, z: 4, core: 2. Of those that a mesh axis runs over, the one named last changes fastest.
Arguments:
- hidden_in: bfloat16 [4096, 2048], P(('dp', 'tensor')), may hold values from -6 to 6
- ln1_gain: float32 [2048], replicated, may hold values from 0.5 to 1.5
- ln1_bias: float32 [2048], replicated, may hold values from -1.8 to 1.8
- qkv_weight: bfloat16 [2048, 6144], P('dp', 'tensor'), may hold values from -0.125 to 0.125
- joined_bias: float32 [6144], P('tensor'), may hold values from -1.8 to 1.8
- out_weight: bfloat16 [2048, 2048], P('tensor', 'dp'), may hold values from -0.5 to 0.5
- output_bias: float32 [2048], replicated, may hold values from -1.8 to 1.8
- ln2_gain: float32 [2048], replicated, may hold values from 0.5 to 1.5
- ln2_bias: float32 [2048], replicated, may hold values from -1.8 to 1.8
- fc1_weight: bfloat16 [2048, 8192], P('dp', 'tensor'), may hold values from -0.125 to 0.125
- first_feed_bias: float32 [8192], P('tensor'), may hold values from -1.8 to 1.8
- fc2_weight: bfloat16 [8192, 2048], P('tensor', 'dp'), may hold values from -0.0625 to 0.0625
- second_feed_bias: float32 [2048], replicated, may hold values from -1.8 to 1.8
- qkv_down: bfloat16 [8, 16, 2048], replicated, may hold values from -0.125 to 0.125
- qkv_up: bfloat16 [8, 16, 6144], replicated, may hold values from -1.5 to 1.5
- out_down: bfloat16 [8, 16, 2048], replicated, may hold values from -0.125 to 0.125
- out_up: bfloat16 [8, 16, 2048], replicated, may hold values from -1.5 to 1.5
- fc1_down: bfloat16 [8, 16, 2048], replicated, may hold values from -0.125 to 0.125
- fc1_up: bfloat16 [8, 16, 8192], replicated, may hold values from -1.5 to 1.5
- fc2_down: bfloat16 [8, 16, 8192], replicated, may hold values from -0.0625 to 0.0625
- fc2_up: bfloat16 [8, 16, 2048], replicated, may hold values from -1.5 to 1.5
- seq_adapter: int32 [2], replicated, may hold values from 0 to 7, as said below
- span_starts: int32 [2, 3], replicated, may hold values from 0 to 1790, as said below
- cotangent: bfloat16 [4096, 2048], P(('dp', 'tensor')), may hold values from -6 to 6
Outputs:
- layer_output: bfloat16 [4096, 2048], P(('dp', 'tensor'))
- hidden_grad: float32 [4096, 2048], P(('dp', 'tensor'))
- qkv_down_grad: float32 [8, 16, 2048], P(None, None, ('dp', 'tensor'))
- qkv_up_grad: float32 [8, 16, 6144], P(None, None, ('dp', 'tensor'))
- out_down_grad: float32 [8, 16, 2048], P(None, None, ('dp', 'tensor'))
- out_up_grad: float32 [8, 16, 2048], P(None, None, ('dp', 'tensor'))
- fc1_down_grad: float32 [8, 16, 2048], P(None, None, ('dp', 'tensor'))
- fc1_up_grad: float32 [8, 16, 8192], P(None, None, ('dp', 'tensor'))
- fc2_down_grad: float32 [8, 16, 8192], P(None, None, ('dp', 'tensor'))
- fc2_up_grad: float32 [8, 16, 2048], P(None, None, ('dp', 'tensor'))
The draws below stay inside these ranges and needn't reach their ends.
Inputs may be any that keep to these rules, and one draw needn't show every extreme that they name: `span_starts`: in every sequence, picture span j starts between j times the floor of 2048 / 3 and that plus the floor of 2048 / 3 minus 256, so spans never intersect. `seq_adapter`: two sequences use the same adapter only if their numbers differ by a multiple of 8.
All inputs are finite; a program needn't handle non-finite values.
Results may differ from the reference program's by a relative error of at most 0.02.
Values may be sent and summed in bfloat16 or wider, within the bound.
No kernel may reach another device: no remote copies, remote signals or barrier semaphores. Data moves between devices by JAX's collectives and lax.ppermute only.
A program may use at most 88 MiB of HBM per device.

```python
import jax
import jax.numpy as jnp
from jax import lax

D = 2048
H = 32
HD = 64
FF = 8192
R = 16
ADAPTERS = 8
SPANS = 3
PIC = 256
LENGTH = 2048
SEQS = 2
TOKENS = 4096


def draw_seq_adapter(key, part):
    order = jax.random.permutation(jax.random.fold_in(key, 21), ADAPTERS).astype(jnp.int32)
    seq_index = jnp.arange(SEQS, dtype=jnp.int32) % ADAPTERS
    return order[seq_index].astype(jnp.int32)


def draw_span_starts(key, part):
    region = LENGTH // SPANS
    offsets = jax.random.randint(jax.random.fold_in(key, 11), (SEQS, SPANS), 0, region - PIC + 1)
    first_seq = jax.random.randint(jax.random.fold_in(key, 12), (), 0, SEQS)
    final_seq = jax.random.randint(jax.random.fold_in(key, 13), (), 0, SEQS)
    seq_index = jnp.arange(SEQS, dtype=jnp.int32)[:, None]
    span_index = jnp.arange(SPANS, dtype=jnp.int32)[None, :]
    offsets = jnp.where((seq_index == first_seq) & (span_index == 0), 0, offsets)
    offsets = jnp.where((seq_index == final_seq) & (span_index == SPANS - 1), region - PIC, offsets)
    return (span_index * region + offsets).astype(jnp.int32)


def steps_of(rng, dims, pieces, smallest, largest):
    def one(position, blocks):
        steps = jax.random.uniform(jax.random.fold_in(jax.random.fold_in(rng, 6), position), (blocks,), jnp.float32, smallest / len(pieces), largest / len(pieces))
        return jnp.repeat(jnp.exp(steps), dims[position] // blocks).reshape((-1,) + (1,) * (len(dims) - position - 1))

    level = one(*pieces[0])
    for cut in pieces[1:]:
        level = level * one(*cut)
    return level


def bell_draw(stream_key, dims, scale, most, cuts=(), held_as=jnp.bfloat16):
    gain = steps_of(stream_key, dims, cuts, -0.22, 0.18) if cuts else 1.0
    values = jax.random.normal(stream_key, dims, jnp.float32) * scale * gain
    return jnp.minimum(jnp.maximum(values, -most), most).astype(held_as)


def setup_inputs(seed: int = 0) -> dict:
    key_list = jax.random.split(jax.random.key(seed), 25)
    hidden_in = bell_draw(key_list[0], (TOKENS, D), 1.0, 6.0, ((0, 32),))
    ln1_gain = jnp.clip(1.0 + 0.1 * jax.random.normal(key_list[1], (D,), jnp.float32), 0.5, 1.5)
    ln1_bias = bell_draw(key_list[2], (D,), 0.3, 1.8, (), jnp.float32)
    qkv_weight = bell_draw(key_list[3], (D, 3 * D), D ** -0.5, 0.125, ((0, 8), (1, 4)))
    joined_bias = bell_draw(key_list[4], (3 * D,), 0.3, 1.8, ((0, 4),), jnp.float32)
    out_weight = bell_draw(key_list[5], (D, D), (D // 16) ** -0.5, 0.5, ((0, 4), (1, 8)))
    output_bias = bell_draw(key_list[6], (D,), 0.3, 1.8, (), jnp.float32)
    ln2_gain = jnp.clip(1.0 + 0.1 * jax.random.normal(key_list[7], (D,), jnp.float32), 0.5, 1.5)
    ln2_bias = bell_draw(key_list[8], (D,), 0.3, 1.8, (), jnp.float32)
    fc1_weight = bell_draw(key_list[9], (D, FF), D ** -0.5, 0.125, ((0, 8), (1, 4)))
    first_feed_bias = bell_draw(key_list[10], (FF,), 0.3, 1.8, ((0, 4),), jnp.float32)
    fc2_weight = bell_draw(key_list[11], (FF, D), FF ** -0.5, 0.0625, ((0, 4), (1, 8)))
    second_feed_bias = bell_draw(key_list[12], (D,), 0.3, 1.8, (), jnp.float32)
    qkv_down = bell_draw(key_list[13], (ADAPTERS, R, D), D ** -0.5, 0.125)
    qkv_up = bell_draw(key_list[14], (ADAPTERS, R, 3 * D), R ** -0.5, 1.5)
    out_down = bell_draw(key_list[15], (ADAPTERS, R, D), D ** -0.5, 0.125)
    out_up = bell_draw(key_list[16], (ADAPTERS, R, D), R ** -0.5, 1.5)
    fc1_down = bell_draw(key_list[17], (ADAPTERS, R, D), D ** -0.5, 0.125)
    fc1_up = bell_draw(key_list[18], (ADAPTERS, R, FF), R ** -0.5, 1.5)
    fc2_down = bell_draw(key_list[19], (ADAPTERS, R, FF), FF ** -0.5, 0.0625)
    fc2_up = bell_draw(key_list[20], (ADAPTERS, R, D), R ** -0.5, 1.5)
    seq_adapter = draw_seq_adapter(jax.random.fold_in(key_list[24], 71), 0)
    span_starts = draw_span_starts(jax.random.fold_in(key_list[24], 71), 0)
    cotangent = bell_draw(key_list[23], (TOKENS, D), 1.0, 6.0, ((0, 32),))
    return dict(hidden_in=hidden_in, ln1_gain=ln1_gain, ln1_bias=ln1_bias, qkv_weight=qkv_weight, joined_bias=joined_bias, out_weight=out_weight, output_bias=output_bias, ln2_gain=ln2_gain, ln2_bias=ln2_bias, fc1_weight=fc1_weight, first_feed_bias=first_feed_bias, fc2_weight=fc2_weight, second_feed_bias=second_feed_bias, qkv_down=qkv_down, qkv_up=qkv_up, out_down=out_down, out_up=out_up, fc1_down=fc1_down, fc1_up=fc1_up, fc2_down=fc2_down, fc2_up=fc2_up, seq_adapter=seq_adapter, span_starts=span_starts, cotangent=cotangent)


@jax.custom_vjp
def reduced_rows(v):
    return lax.optimization_barrier(v.astype(jnp.bfloat16)).astype(jnp.float32)

@jax.custom_vjp
def reduced_backward(v):
    return v

def low_keep(v):
    return (reduced_rows(v), None)

def low_pass(kept, grad):
    return (grad,)

def back_keep(v):
    return (v, None)

def back_low(kept, grad):
    return (reduced_rows(grad),)
reduced_rows.defvjp(low_keep, low_pass)
reduced_backward.defvjp(back_keep, back_low)
EPS = 1e-05
ADAPTER_FACTOR = 0.5

def dense_product(left_side, right_side):
    return jnp.dot(left_side, right_side, precision=lax.Precision.HIGHEST, preferred_element_type=jnp.float32)

def norm_layer(values, norm_gain, norm_shift):
    centred = values - lax.optimization_barrier(jnp.mean(values, axis=-1, keepdims=True))
    spread = lax.optimization_barrier(jnp.mean(centred * centred, axis=-1, keepdims=True))
    return centred * lax.rsqrt(spread + EPS) * norm_gain + norm_shift

def span_label(positions, starts):
    inside = (positions[:, None] >= starts[None, :]) & (positions[:, None] < starts[None, :] + PIC)
    span_order = jnp.arange(1, SPANS + 1, dtype=jnp.int32)
    return lax.optimization_barrier(jnp.sum(jnp.where(inside, span_order[None, :], 0), axis=1)).astype(jnp.int32) - 1

def attend(queries, key_all, values, starts):
    positions = jnp.arange(LENGTH, dtype=jnp.int32)
    labels = span_label(positions, starts)
    slopes = jnp.exp2(-8.0 * (jnp.arange(H, dtype=jnp.int32).astype(jnp.float32) + 1.0) / H)
    row_block = min(512, LENGTH)

    def one_block(block_index):
        row_start = block_index * row_block
        query_rows = lax.dynamic_slice_in_dim(queries, row_start, row_block, 0)
        row_pos = row_start + jnp.arange(row_block, dtype=jnp.int32)
        row_label = lax.dynamic_slice_in_dim(labels, row_start, row_block, 0)
        raw_scores = jnp.einsum('qhd,khd->hqk', query_rows, key_all, precision=lax.Precision.HIGHEST)
        offset = (positions[None, :] - row_pos[:, None]).astype(jnp.float32)
        scores = reduced_backward((raw_scores + slopes[:, None, None] * offset[None]) * 0.125)
        allowed = (positions[None, :] <= row_pos[:, None]) | (row_label[:, None] == labels[None, :]) & (row_label[:, None] >= 0)
        scores = jnp.where(allowed[None], scores, -1e+30)
        row_top = lax.optimization_barrier(jnp.max(scores, axis=-1, keepdims=True))
        exponent = jnp.exp(scores - row_top)
        probability = reduced_rows(exponent / lax.optimization_barrier(jnp.sum(exponent, axis=-1, keepdims=True)))
        return jnp.einsum('hqk,khd->qhd', probability, values, precision=lax.Precision.HIGHEST)
    blocks = lax.map(jax.checkpoint(one_block), jnp.arange(LENGTH // row_block, dtype=jnp.int32))
    return blocks.reshape(LENGTH, H * HD)

def reference(hidden_in, ln1_gain, ln1_bias, qkv_weight, joined_bias, out_weight, output_bias, ln2_gain, ln2_bias, fc1_weight, first_feed_bias, fc2_weight, second_feed_bias, qkv_down, qkv_up, out_down, out_up, fc1_down, fc1_up, fc2_down, fc2_up, seq_adapter, span_starts, cotangent):
    joined_matrix = qkv_weight.astype(jnp.float32)
    output_matrix = out_weight.astype(jnp.float32)
    first_feed_matrix = fc1_weight.astype(jnp.float32)
    second_feed_matrix = fc2_weight.astype(jnp.float32)
    stacks = (qkv_down.astype(jnp.float32), qkv_up.astype(jnp.float32), out_down.astype(jnp.float32), out_up.astype(jnp.float32), fc1_down.astype(jnp.float32), fc1_up.astype(jnp.float32), fc2_down.astype(jnp.float32), fc2_up.astype(jnp.float32))

    def layer(input_rows, picked, starts):
        down_qkv, joined_raise, down_out, output_raise, down_fc1, first_feed_raise, down_fc2, second_feed_raise = picked
        normalized_rows = reduced_rows(norm_layer(input_rows, ln1_gain, ln1_bias))
        adapter_product = reduced_rows(reduced_backward(dense_product(normalized_rows, down_qkv.T)))
        joined_projection = reduced_rows(reduced_backward(dense_product(normalized_rows, joined_matrix) + ADAPTER_FACTOR * dense_product(adapter_product, joined_raise) + joined_bias))
        grouped = joined_projection.reshape(LENGTH, H, 3, HD)
        attended_context = attend(grouped[:, :, 0], grouped[:, :, 1], grouped[:, :, 2], starts)
        attended_context = reduced_rows(reduced_backward(attended_context))
        adapter_product = reduced_rows(reduced_backward(dense_product(attended_context, down_out.T)))
        middle_activation = input_rows + reduced_backward(dense_product(attended_context, output_matrix) + ADAPTER_FACTOR * dense_product(adapter_product, output_raise) + output_bias)
        normalized_rows = reduced_rows(norm_layer(middle_activation, ln2_gain, ln2_bias))
        adapter_product = reduced_rows(reduced_backward(dense_product(normalized_rows, down_fc1.T)))
        preactivation = reduced_backward(dense_product(normalized_rows, first_feed_matrix) + ADAPTER_FACTOR * dense_product(adapter_product, first_feed_raise) + first_feed_bias)
        activated_rows = reduced_rows(jax.nn.gelu(preactivation, approximate=False))
        adapter_product = reduced_rows(reduced_backward(dense_product(activated_rows, down_fc2.T)))
        return middle_activation + reduced_backward(dense_product(activated_rows, second_feed_matrix) + ADAPTER_FACTOR * dense_product(adapter_product, second_feed_raise) + second_feed_bias)
    layer_saved = jax.checkpoint(layer)

    def forward(rows_all, stack_set):

        def one_seq(scan_carry, inputs):
            seq_rows, adapter_slot, starts = inputs
            picked = tuple((lax.dynamic_index_in_dim(one_stack, adapter_slot, 0, keepdims=False) for one_stack in stack_set))
            return (scan_carry, layer_saved(seq_rows, picked, starts))
        unused, outputs = lax.scan(one_seq, jnp.zeros((), jnp.float32), (rows_all.reshape(SEQS, LENGTH, D), seq_adapter, span_starts))
        return outputs.reshape(TOKENS, D)
    result, pullback = jax.vjp(forward, hidden_in.astype(jnp.float32), stacks)
    input_grad, stack_grads = pullback(cotangent.astype(jnp.float32))
    return (result.astype(jnp.bfloat16), input_grad, stack_grads[0], stack_grads[1], stack_grads[2], stack_grads[3], stack_grads[4], stack_grads[5], stack_grads[6], stack_grads[7])
```

```python
import functools

import jax
import jax.numpy as jnp
from jax import lax
from jax.experimental import pallas as pl
from jax.experimental.pallas import tpu as pltpu
from jax.sharding import PartitionSpec as P

H = 32
HD = 64
ADAPTERS = 8
SEQ_DEVS = 4
PIC = 256
EPS = 1e-05
FACTOR = 0.5
BF = jnp.bfloat16
F32 = jnp.float32
BLOCK = 256
VMEM_BYTES = 56 * 1024 * 1024


def dot(a, b):
    return jnp.dot(a, b, preferred_element_type=F32)


def dot_nt(a, b):
    return lax.dot_general(a, b, (((1,), (1,)), ((), ())), preferred_element_type=F32)


def dot_tn(a, b):
    return lax.dot_general(a, b, (((0,), (0,)), ((), ())), preferred_element_type=F32)


def gelu_and_slope(f):
    phi = 0.5 * (1.0 + lax.erf(f * (0.5**0.5)))
    density = jnp.exp(-0.5 * f * f) * (0.5 / jnp.pi) ** 0.5
    return f * phi, phi + f * density


def norm_forward(values, gain, shift):
    centred = values - jnp.mean(values, axis=-1, keepdims=True)
    inverse = lax.rsqrt(jnp.mean(centred * centred, axis=-1, keepdims=True) + EPS)
    unit = centred * inverse
    return unit * gain + shift, unit, inverse


def norm_backward(upstream, unit, inverse, gain):
    scaled = upstream * gain
    return inverse * (
        scaled
        - jnp.mean(scaled, axis=-1, keepdims=True)
        - unit * jnp.mean(scaled * unit, axis=-1, keepdims=True)
    )


def shift_one(array, axis):
    n = lax.axis_size(axis)
    return lax.ppermute(array, axis, [(i, (i + 1) % n) for i in range(n)])


def ring_gather(array, axis):
    pieces = [array]
    for _ in range(lax.axis_size(axis) - 1):
        pieces.append(shift_one(pieces[-1], axis))
    return pieces


def ring_scatter(pieces, axis):
    total = pieces[1].astype(BF)
    for piece in pieces[2:] + pieces[:1]:
        total = shift_one(total, axis).astype(F32) + piece.astype(F32)
        if piece is not pieces[0]:
            total = total.astype(BF)
    return total


def exchange(array, distance):
    n = lax.axis_size("dp")
    return lax.ppermute(array, "dp", [(i, i ^ distance) for i in range(n)])


def span_of(positions, meta_ref, spans, outside):
    label = jnp.full(positions.shape, outside, jnp.int32)
    for j in range(spans):
        start = meta_ref[2 + j]
        label = jnp.where((positions >= start) & (positions < start + PIC), j, label)
    return label


def allowed_block(i, j, meta_ref, spans):
    key_pos = j * BLOCK + lax.broadcasted_iota(jnp.int32, (BLOCK, BLOCK), 0)
    row_pos = i * BLOCK + lax.broadcasted_iota(jnp.int32, (BLOCK, BLOCK), 1)
    key_label = span_of(key_pos, meta_ref, spans, -1)
    row_label = span_of(row_pos, meta_ref, spans, -2)
    return (key_pos <= row_pos) | (key_label == row_label)


def crosses(i, meta_ref, spans):
    edge = (i + 1) * BLOCK
    found = jnp.bool_(False)
    for j in range(spans):
        start = meta_ref[2 + j]
        found = found | ((start < edge) & (edge < start + PIC))
    return found


def block_rows(i):
    return pl.ds(pl.multiple_of(i * BLOCK, BLOCK), BLOCK)


def reorder_starts(meta_ref, parts, ring, rows):
    part, spot = meta_ref[0], meta_ref[1]
    for e in range(parts):
        for k in range(ring):
            back = spot - k
            back = jnp.where(back < 0, back + ring, back)
            true_start = ((part ^ e) * ring + back) * rows
            yield e, k, pl.ds(pl.multiple_of(true_start, rows), rows)


def prepare_block(b, heads, qkv_ref, slope_ref, kaug_ref, qaug_ref):
    rows = block_rows(b)
    lane = lax.broadcasted_iota(jnp.int32, (BLOCK, HD), 1)
    pos = b * BLOCK + lax.broadcasted_iota(jnp.int32, (BLOCK, HD), 0)
    ones = jnp.where(lane < 3, 1.0, 0.0).astype(BF)
    for h in range(heads):
        at = h * 3 * HD
        query = qkv_ref[rows, at : at + HD] * jnp.asarray(0.125, BF)
        key = qkv_ref[rows, at + HD : at + 2 * HD]
        offset = pos.astype(F32) * (slope_ref[h] * 0.125)
        high = offset.astype(BF).astype(F32)
        middle = (offset - high).astype(BF).astype(F32)
        low = offset - high - middle
        extra = jnp.where(
            lane == 0, high, jnp.where(lane == 1, middle, jnp.where(lane == 2, low, 0.0))
        ).astype(BF)
        qaug_ref[h, rows, :] = jnp.concatenate([query, ones], axis=1)
        kaug_ref[h, rows, :] = jnp.concatenate([key, extra], axis=1)


def forward_kernel(heads, parts, ring, rows, spans, meta_ref, slope_ref, *refs):
    piece_refs = refs[:parts]
    ctx_ref, qkv_ref, out_t_ref, log_ref, kaug_ref, qaug_ref, vt_ref = refs[parts:]
    length = qkv_ref.shape[0]
    blocks = length // BLOCK
    for e, k, dst in reorder_starts(meta_ref, parts, ring, rows):
        qkv_ref[dst, :] = piece_refs[e][k * rows : (k + 1) * rows, :]
    eye = (
        lax.broadcasted_iota(jnp.int32, (HD, HD), 0) == lax.broadcasted_iota(jnp.int32, (HD, HD), 1)
    ).astype(BF)

    def prepare(b, unused):
        prepare_block(b, heads, qkv_ref, slope_ref, kaug_ref, qaug_ref)
        cols = block_rows(b)
        for h in range(heads):
            at = h * 3 * HD + 2 * HD
            value = qkv_ref[cols, at : at + HD]
            vt_ref[h, :HD, cols] = dot_nt(eye, value).astype(BF)
            row = lax.broadcasted_iota(jnp.int32, (16, BLOCK), 0)
            vt_ref[h, HD:, cols] = jnp.where(row == 0, 1.0, 0.0).astype(BF)
        return unused

    lax.fori_loop(0, blocks, prepare, 0)

    def one_row_block(i, unused):
        rows_i = block_rows(i)
        queries = [qaug_ref[h, rows_i, :] for h in range(heads)]

        def step(j, state, allowed=None):
            cols = block_rows(j)
            new_state = []
            for h in range(heads):
                scores = dot_nt(kaug_ref[h, cols, :], queries[h])
                if allowed is not None:
                    scores = jnp.where(allowed, scores, -1e30)
                top = jnp.max(scores, axis=0, keepdims=True)
                if state is not None:
                    old_top, old_sum = state[h]
                    top = jnp.maximum(top, old_top)
                weight = jnp.exp(scores - top).astype(BF)
                total = dot(vt_ref[h, :, cols], weight)
                if state is not None:
                    total = total + old_sum * jnp.exp(old_top - top)
                new_state.append((top, total))
            return tuple(new_state)

        state = step(i, None, allowed_block(i, i, meta_ref, spans))
        state = lax.fori_loop(0, i, step, state)
        state = lax.cond(
            crosses(i, meta_ref, spans),
            lambda s: step(i + 1, s, allowed_block(i, i + 1, meta_ref, spans)),
            lambda s: s,
            state,
        )
        outs = []
        for h in range(heads):
            top, total = state[h]
            amount = total[HD : HD + 1]
            outs.append(total[:HD] / amount)
            log_ref[h : h + 1, rows_i] = top + jnp.log(amount)
        if heads * HD < 128:
            outs.append(jnp.zeros((128 - heads * HD, BLOCK), F32))
        out_t = jnp.concatenate(outs, axis=0)
        out_t_ref[:, rows_i] = out_t
        turned = out_t.T.astype(BF)[:, : heads * HD]
        for part in range(BLOCK // rows):
            block = i * (BLOCK // rows) + part
            e = (block // ring) ^ meta_ref[0]
            k = meta_ref[1] - block % ring
            k = jnp.where(k < 0, k + ring, k)
            start = pl.multiple_of((e * ring + k) * rows, rows)
            ctx_ref[pl.ds(start, rows), :] = turned[part * rows : (part + 1) * rows]
        return unused

    lax.fori_loop(0, blocks, one_row_block, 0)


def backward_kernel(heads, parts, ring, rows, spans, meta_ref, slope_ref, *refs):
    piece_refs = refs[:parts]
    (
        qkv_ref,
        out_t_ref,
        log_ref,
        grad_ref,
        g_ref,
        kaug_ref,
        qaug_ref,
        kt_ref,
        gq_ref,
        gg_ref,
        delta_ref,
        dqt_ref,
        dkv_ref,
    ) = refs[parts:]
    length = qkv_ref.shape[0]
    blocks = length // BLOCK
    for e, k, dst in reorder_starts(meta_ref, parts, ring, rows):
        g_ref[dst, :] = piece_refs[e][k * rows : (k + 1) * rows, :]
    eye = (
        lax.broadcasted_iota(jnp.int32, (HD, HD), 0) == lax.broadcasted_iota(jnp.int32, (HD, HD), 1)
    ).astype(BF)

    def prepare(b, unused):
        prepare_block(b, heads, qkv_ref, slope_ref, kaug_ref, qaug_ref)
        cols = block_rows(b)
        blank = jnp.zeros((BLOCK, HD), BF)
        grad_t = g_ref[cols, :].astype(F32)
        if heads * HD < 128:
            grad_t = jnp.concatenate([grad_t, jnp.zeros((BLOCK, 128 - heads * HD), F32)], axis=1)
        product = grad_t.T * out_t_ref[:, cols]
        for h in range(heads):
            at = h * 3 * HD
            kt_ref[h, :, cols] = dot_nt(eye, qkv_ref[cols, at + HD : at + 2 * HD]).astype(BF)
            query = qkv_ref[cols, at : at + HD] * jnp.asarray(0.125, BF)
            gq_ref[h, cols, :] = jnp.concatenate([blank, query], axis=1)
            gg_ref[h, cols, :] = jnp.concatenate([g_ref[cols, h * HD : (h + 1) * HD], blank], axis=1)
            delta_ref[h : h + 1, cols] = jnp.sum(
                product[h * HD : (h + 1) * HD], axis=0, keepdims=True
            )
            dkv_ref[h, cols, :] = jnp.zeros((BLOCK, 2 * HD), F32)
        return unused

    lax.fori_loop(0, blocks, prepare, 0)

    def one_row_block(i, unused):
        rows_i = block_rows(i)

        def step(j, state, allowed=None):
            cols = block_rows(j)
            new_state = []
            for h in range(heads):
                at = h * 3 * HD + 2 * HD
                scores = dot_nt(kaug_ref[h, cols, :], qaug_ref[h, rows_i, :])
                if allowed is not None:
                    scores = jnp.where(allowed, scores, -1e30)
                weight = jnp.exp(scores - log_ref[h : h + 1, rows_i])
                grad_weight = dot_nt(
                    qkv_ref[cols, at : at + HD], g_ref[rows_i, h * HD : (h + 1) * HD]
                )
                grad_score = (weight * (grad_weight - delta_ref[h : h + 1, rows_i])).astype(BF)
                dkv_ref[h, cols, :] += dot(weight.astype(BF), gg_ref[h, rows_i, :]) + dot(
                    grad_score, gq_ref[h, rows_i, :]
                )
                new_state.append(state[h] + dot(kt_ref[h, :, cols], grad_score))
            return tuple(new_state)

        state = tuple(jnp.zeros((HD, BLOCK), F32) for _ in range(heads))
        state = step(i, state, allowed_block(i, i, meta_ref, spans))
        state = lax.fori_loop(0, i, step, state)
        state = lax.cond(
            crosses(i, meta_ref, spans),
            lambda s: step(i + 1, s, allowed_block(i, i + 1, meta_ref, spans)),
            lambda s: s,
            state,
        )
        outs = list(state)
        if heads * HD < 128:
            outs.append(jnp.zeros((128 - heads * HD, BLOCK), F32))
        dqt_ref[rows_i, :] = jnp.concatenate(outs, axis=0).T * 0.125
        return unused

    lax.fori_loop(0, blocks, one_row_block, 0)

    def write(b, unused):
        cols = block_rows(b)
        columns = []
        for h in range(heads):
            dkv = dkv_ref[h, cols, :]
            columns += [dqt_ref[cols, h * HD : (h + 1) * HD], dkv[:, HD:], dkv[:, :HD]]
        whole = jnp.concatenate(columns, axis=1).astype(BF)
        for part in range(BLOCK // rows):
            block = b * (BLOCK // rows) + part
            e = (block // ring) ^ meta_ref[0]
            k = meta_ref[1] - block % ring
            k = jnp.where(k < 0, k + ring, k)
            start = pl.multiple_of((e * ring + k) * rows, rows)
            grad_ref[pl.ds(start, rows), :] = whole[part * rows : (part + 1) * rows]
        return unused

    lax.fori_loop(0, blocks, write, 0)


def specs(count_smem, count_vmem):
    return [pl.BlockSpec(memory_space=pltpu.SMEM)] * count_smem + [
        pl.BlockSpec(memory_space=pltpu.VMEM)
    ] * count_vmem


def attend_forward(pieces, meta, slopes, ring, rows):
    heads = slopes.shape[0]
    parts = len(pieces)
    length = parts * pieces[0].shape[0]
    wide = max(128, heads * HD)
    return pl.pallas_call(
        functools.partial(forward_kernel, heads, parts, ring, rows, meta.shape[0] - 2),
        out_shape=(
            jax.ShapeDtypeStruct((length, heads * HD), BF),
            jax.ShapeDtypeStruct((length, heads * 3 * HD), BF),
            jax.ShapeDtypeStruct((wide, length), F32),
            jax.ShapeDtypeStruct((8, length), F32),
        ),
        in_specs=specs(2, parts),
        out_specs=tuple(specs(0, 4)),
        scratch_shapes=[
            pltpu.VMEM((heads, length, 128), BF),
            pltpu.VMEM((heads, length, 128), BF),
            pltpu.VMEM((heads, HD + 16, length), BF),
        ],
        compiler_params=pltpu.CompilerParams(vmem_limit_bytes=VMEM_BYTES),
        cost_estimate=pl.CostEstimate(
            flops=heads * length * length * HD * 8,
            bytes_accessed=length * heads * HD * 20,
            transcendentals=heads * length * length // 2,
        ),
    )(meta, slopes, *pieces)


def attend_backward(pieces, qkv, out_t, logs, meta, slopes, ring, rows):
    heads = slopes.shape[0]
    parts = len(pieces)
    length = qkv.shape[0]
    wide = max(128, heads * HD)
    return pl.pallas_call(
        functools.partial(backward_kernel, heads, parts, ring, rows, meta.shape[0] - 2),
        out_shape=jax.ShapeDtypeStruct((length, heads * 3 * HD), BF),
        in_specs=specs(2, parts + 3),
        out_specs=specs(0, 1)[0],
        scratch_shapes=[
            pltpu.VMEM((length, heads * HD), BF),
            pltpu.VMEM((heads, length, 128), BF),
            pltpu.VMEM((heads, length, 128), BF),
            pltpu.VMEM((heads, HD, length), BF),
            pltpu.VMEM((heads, length, 128), BF),
            pltpu.VMEM((heads, length, 128), BF),
            pltpu.VMEM((8, length), F32),
            pltpu.VMEM((length, wide), F32),
            pltpu.VMEM((heads, length, 128), F32),
        ],
        compiler_params=pltpu.CompilerParams(vmem_limit_bytes=VMEM_BYTES),
        cost_estimate=pl.CostEstimate(
            flops=heads * length * length * HD * 16,
            bytes_accessed=length * heads * HD * 20,
            transcendentals=heads * length * length // 2,
        ),
    )(meta, slopes, *pieces, qkv, out_t, logs)


def reduce_full_width(stacks, groups):
    ring, n = lax.axis_size("tensor"), lax.axis_size("dp")
    spot, data = lax.axis_index("tensor"), lax.axis_index("dp")
    group, part = data // SEQ_DEVS, data % SEQ_DEVS
    widths = [s.shape[1] // (ring * n) for s in stacks]
    rank = stacks[0].shape[0]
    joined = jnp.concatenate(
        [s.reshape(rank, groups, SEQ_DEVS, ring, w) for s, w in zip(stacks, widths)], axis=4
    )
    joined = jnp.transpose(joined, (3, 2, 1, 0, 4))

    def spot_block(k):
        return lax.dynamic_index_in_dim(joined, (spot + k) % ring, 0, keepdims=False)

    total = spot_block(0)
    for k in range(1, ring):
        moved = lax.ppermute(
            spot_block(k).astype(BF), "tensor", [(i, (i + k) % ring) for i in range(ring)]
        )
        total = total + moved.astype(F32)

    own = lax.dynamic_index_in_dim(total, part, 0, keepdims=False)
    for e in range(1, SEQ_DEVS):
        block = lax.dynamic_index_in_dim(total, part ^ e, 0, keepdims=False)
        own = own + exchange(block.astype(BF), e).astype(F32)
    pieces = [lax.dynamic_index_in_dim(own, group, 0, keepdims=False)]
    for k in range(1, groups):
        block = lax.dynamic_index_in_dim(own, (group + k) % groups, 0, keepdims=False)
        pieces.append(
            lax.ppermute(
                block.astype(BF), "dp", [(i, (i + k * SEQ_DEVS) % n) for i in range(n)]
            ).astype(F32)
        )
    return [(piece, (group - k) % groups) for k, piece in enumerate(pieces)], widths


def reduce_own_columns(stacks, groups):
    ring, n = lax.axis_size("tensor"), lax.axis_size("dp")
    spot, data = lax.axis_index("tensor"), lax.axis_index("dp")
    group, part = data // SEQ_DEVS, data % SEQ_DEVS
    widths = [s.shape[1] // n for s in stacks]
    rank = stacks[0].shape[0]
    joined = jnp.concatenate(
        [s.reshape(rank, SEQ_DEVS, groups, w) for s, w in zip(stacks, widths)], axis=3
    )
    joined = jnp.transpose(joined, (1, 2, 0, 3))
    own = lax.dynamic_index_in_dim(joined, part, 0, keepdims=False)
    for e in range(1, SEQ_DEVS):
        block = lax.dynamic_index_in_dim(joined, part ^ e, 0, keepdims=False)
        own = own + exchange(block.astype(BF), e).astype(F32)
    pieces = []
    mine = (data * ring + spot) % groups
    for k in range(groups):
        pairs = []
        for i in range(n):
            for z in range(ring):
                r = (i // SEQ_DEVS + k) % groups
                pairs.append((i * ring + z, z * n + (i % SEQ_DEVS) * groups + r))
        block = lax.dynamic_index_in_dim(own, (group + k) % groups, 0, keepdims=False)
        moved = lax.ppermute(block.astype(BF), ("dp", "tensor"), pairs).astype(F32)
        pieces.append((moved, (mine - k) % groups))
    return pieces, widths


def place(pieces, widths, seq_adapter):
    slots = jnp.arange(ADAPTERS, dtype=jnp.int32)
    whole = 0.0
    for piece, sequence in pieces:
        slot = lax.dynamic_index_in_dim(seq_adapter, sequence, 0, keepdims=False)
        whole = whole + jnp.where((slots == slot)[:, None, None], piece[None], 0.0)
    outs, at = [], 0
    for width in widths:
        outs.append(whole[:, :, at : at + width])
        at += width
    return outs


def local(
    hidden_in,
    ln1_gain,
    ln1_bias,
    qkv_weight,
    joined_bias,
    out_weight,
    output_bias,
    ln2_gain,
    ln2_bias,
    fc1_weight,
    first_feed_bias,
    fc2_weight,
    second_feed_bias,
    qkv_down,
    qkv_up,
    out_down,
    out_up,
    fc1_down,
    fc1_up,
    fc2_down,
    fc2_up,
    seq_adapter,
    span_starts,
    cotangent,
):
    spot = lax.axis_index("tensor")
    data = lax.axis_index("dp")
    ring = lax.axis_size("tensor")
    groups = lax.axis_size("dp") // SEQ_DEVS
    group, part = data // SEQ_DEVS, data % SEQ_DEVS
    rows = hidden_in.shape[0]
    slot = lax.dynamic_index_in_dim(seq_adapter, group, 0, keepdims=False)
    starts = lax.dynamic_index_in_dim(span_starts, group, 0, keepdims=False)
    qkv_cols, ctx_cols, hidden_cols = qkv_weight.shape[1], out_weight.shape[0], fc1_weight.shape[1]
    heads = qkv_cols // (3 * HD) // SEQ_DEVS
    meta = jnp.concatenate([jnp.stack([part, spot]), starts]).astype(jnp.int32)
    first_head = (spot * SEQ_DEVS + part) * heads
    slopes = jnp.exp2(
        -8.0 * ((first_head + jnp.arange(heads, dtype=jnp.int32)).astype(F32) + 1.0) / H
    )

    def pick(stack):
        return lax.dynamic_index_in_dim(stack, slot, 0, keepdims=False)

    def own_cols(matrix, count):
        return lax.dynamic_slice_in_dim(matrix, spot * count, count, 1)

    a_q, b_q = pick(qkv_down), own_cols(pick(qkv_up), qkv_cols)
    a_o, b_o = own_cols(pick(out_down), ctx_cols), pick(out_up)
    a_1, b_1 = pick(fc1_down), own_cols(pick(fc1_up), hidden_cols)
    a_2, b_2 = own_cols(pick(fc2_down), hidden_cols), pick(fc2_up)

    w_qkv = lax.all_gather(qkv_weight, "dp", axis=0, tiled=True)
    w_out = lax.all_gather(out_weight, "dp", axis=1, tiled=True)
    w_fc1 = lax.all_gather(fc1_weight, "dp", axis=0, tiled=True)
    w_fc2 = lax.all_gather(fc2_weight, "dp", axis=1, tiled=True)

    def split(array):
        return [array[k * rows : (k + 1) * rows] for k in range(ring)]

    def up(low, matrix):
        return FACTOR * dot(low.astype(BF), matrix)

    x = hidden_in.astype(F32)
    normed1, unit1, inverse1 = norm_forward(x, ln1_gain, ln1_bias)
    n1 = jnp.concatenate(ring_gather(normed1.astype(BF), "tensor"), axis=0)
    gy = jnp.concatenate(ring_gather(cotangent, "tensor"), axis=0)
    u1 = dot_nt(n1, a_q).astype(BF)
    qkv = (dot(n1, w_qkv) + up(u1, b_q) + joined_bias).astype(BF)
    pieces = []
    for e in range(SEQ_DEVS):
        piece = lax.dynamic_slice_in_dim(qkv, (part ^ e) * (heads * 3 * HD), heads * 3 * HD, 1)
        pieces.append(exchange(piece, e) if e else piece)
    ctx_rel, qkv_true, out_t, logs = attend_forward(pieces, meta, slopes, ring, rows)
    count = ring * rows
    ctx = jnp.zeros((count, ctx_cols), BF)
    for e in range(SEQ_DEVS):
        piece = ctx_rel[e * count : (e + 1) * count]
        piece = exchange(piece, e) if e else piece
        ctx = lax.dynamic_update_slice_in_dim(ctx, piece, (part ^ e) * (heads * HD), 1)
    u2 = dot_nt(ctx, a_o).astype(BF)
    part_out = (dot(ctx, w_out) + up(u2, b_o)).astype(BF)
    mid = x + (ring_scatter(split(part_out), "tensor") + output_bias)

    normed2, unit2, inverse2 = norm_forward(mid, ln2_gain, ln2_bias)
    n2 = jnp.concatenate(ring_gather(normed2.astype(BF), "tensor"), axis=0)
    u3 = dot_nt(n2, a_1).astype(BF)
    act, slope = gelu_and_slope(dot(n2, w_fc1) + up(u3, b_1) + first_feed_bias)
    act = act.astype(BF)
    u4 = dot_nt(act, a_2).astype(BF)
    part_mlp = (dot(act, w_fc2) + up(u4, b_2)).astype(BF)

    gu4 = (FACTOR * dot_nt(gy, b_2)).astype(BF)
    gact = dot_nt(gy, w_fc2) + dot(gu4, a_2)
    gf = (gact * slope).astype(BF)
    gu3 = (FACTOR * dot_nt(gf, b_1)).astype(BF)
    part_in2 = (dot_nt(gf, w_fc1) + dot(gu3, a_1)).astype(BF)
    grad_n2 = ring_scatter(split(part_in2), "tensor")
    grad_mid = cotangent.astype(F32) + norm_backward(grad_n2, unit2, inverse2, ln2_gain)
    gm = jnp.concatenate(ring_gather(grad_mid.astype(BF), "tensor"), axis=0)
    layer_output = (mid + (ring_scatter(split(part_mlp), "tensor") + second_feed_bias)).astype(BF)

    gu2 = (FACTOR * dot_nt(gm, b_o)).astype(BF)
    gctx = (dot_nt(gm, w_out) + dot(gu2, a_o)).astype(BF)
    pieces = []
    for e in range(SEQ_DEVS):
        piece = lax.dynamic_slice_in_dim(gctx, (part ^ e) * (heads * HD), heads * HD, 1)
        pieces.append(exchange(piece, e) if e else piece)
    grad_rel = attend_backward(pieces, qkv_true, out_t, logs, meta, slopes, ring, rows)
    gqkv = jnp.zeros((count, qkv_cols), BF)
    for e in range(SEQ_DEVS):
        piece = grad_rel[e * count : (e + 1) * count]
        piece = exchange(piece, e) if e else piece
        gqkv = lax.dynamic_update_slice_in_dim(gqkv, piece, (part ^ e) * (heads * 3 * HD), 1)
    gu1 = (FACTOR * dot_nt(gqkv, b_q)).astype(BF)
    part_in1 = (dot_nt(gqkv, w_qkv) + dot(gu1, a_q)).astype(BF)
    grad_n1 = ring_scatter(split(part_in1), "tensor")
    hidden_grad = grad_mid + norm_backward(grad_n1, unit1, inverse1, ln1_gain)

    full_pieces, full_widths = reduce_full_width(
        [dot_tn(gu1, n1), FACTOR * dot_tn(u2, gm), dot_tn(gu3, n2), FACTOR * dot_tn(u4, gy)], groups
    )
    g_aq, g_bo, g_a1, g_b2 = place(full_pieces, full_widths, seq_adapter)
    col_pieces, col_widths = reduce_own_columns(
        [FACTOR * dot_tn(u1, gqkv), dot_tn(gu2, ctx), FACTOR * dot_tn(u3, gf), dot_tn(gu4, act)],
        groups,
    )
    g_bq, g_ao, g_b1, g_a2 = place(col_pieces, col_widths, seq_adapter)
    return (layer_output, hidden_grad, g_aq, g_bq, g_ao, g_bo, g_a1, g_b1, g_a2, g_b2)


def solution(mesh):
    rows, cols = P(("dp", "tensor"), None), P(None, None, ("dp", "tensor"))
    placed = (
        rows,
        P(),
        P(),
        P("dp", "tensor"),
        P("tensor"),
        P("tensor", "dp"),
        P(),
        P(),
        P(),
        P("dp", "tensor"),
        P("tensor"),
        P("tensor", "dp"),
    ) + (P(),) * 11 + (rows,)
    return jax.shard_map(
        local,
        mesh=mesh,
        in_specs=placed,
        out_specs=(rows, rows) + (cols,) * 8,
        check_vma=False,
    )
```

```python
import functools

import jax
import jax.numpy as jnp
from jax import lax
from jax.experimental import pallas as pl
from jax.experimental.pallas import tpu as pltpu
from jax.sharding import PartitionSpec as P

H = 32
HD = 64
ADAPTERS = 8
SEQ_DEVS = 4
PIC = 256
EPS = 1e-05
FACTOR = 0.5
BF = jnp.bfloat16
F32 = jnp.float32
BLOCK = 256
VMEM_BYTES = 56 * 1024 * 1024
SMALL_VMEM_BYTES = 28 * 1024 * 1024
US = 10**9


def dot(a, b):
    return jnp.dot(a, b, preferred_element_type=F32)


def dot_nt(a, b):
    return lax.dot_general(a, b, (((1,), (1,)), ((), ())), preferred_element_type=F32)


def dot_tn(a, b):
    return lax.dot_general(a, b, (((0,), (0,)), ((), ())), preferred_element_type=F32)


def hold(value, *until):
    return lax.optimization_barrier((value,) + until)[0]


def gelu_and_slope(f):
    phi = 0.5 * (1.0 + lax.erf(f * (0.5**0.5)))
    density = jnp.exp(-0.5 * f * f) * (0.5 / jnp.pi) ** 0.5
    return f * phi, phi + f * density


def norm_forward(values, gain, shift):
    centred = values - jnp.mean(values, axis=-1, keepdims=True)
    inverse = lax.rsqrt(jnp.mean(centred * centred, axis=-1, keepdims=True) + EPS)
    unit = centred * inverse
    return unit * gain + shift, unit, inverse


def norm_backward(upstream, unit, inverse, gain):
    scaled = upstream * gain
    return inverse * (
        scaled
        - jnp.mean(scaled, axis=-1, keepdims=True)
        - unit * jnp.mean(scaled * unit, axis=-1, keepdims=True)
    )


def shift_one(array, axis):
    n = lax.axis_size(axis)
    return lax.ppermute(array, axis, [(i, (i + 1) % n) for i in range(n)])


def ring_gather(array, axis, hops=None):
    pieces = [array]
    for _ in range(lax.axis_size(axis) - 1 if hops is None else hops):
        pieces.append(shift_one(pieces[-1], axis))
    return pieces


class Side:
    def __init__(self, stages):
        self.stages, self.result = stages, None
        self.flying = next(stages)

    def step(self, beside):
        if self.flying is None:
            return beside
        unused, *landed = lax.optimization_barrier((beside,) + tuple(self.flying))
        try:
            self.flying = self.stages.send(landed)
        except StopIteration as stop:
            self.flying, self.result = None, stop.value
        return beside


def ring_scatter(pieces, axis, side=(), first=False):
    total = pieces[1].astype(BF)
    following = pieces[2:] + pieces[:1]
    if first:
        total = (total.astype(F32) + following[0].astype(F32)).astype(BF)
        following = following[1:]
    for i, piece in enumerate(following):
        moved = shift_one(total, axis)
        for work in side:
            moved = work.step(moved) if isinstance(work, Side) else work(moved)
        total = moved.astype(F32) + piece.astype(F32)
        if i < len(following) - 1:
            total = total.astype(BF)
    return total


def exchange(array, distance):
    n = lax.axis_size("dp")
    return lax.ppermute(array, "dp", [(i, i ^ distance) for i in range(n)])


def span_of(positions, meta_ref, spans, outside):
    label = jnp.full(positions.shape, outside, jnp.int32)
    for j in range(spans):
        start = meta_ref[2 + j]
        label = jnp.where((positions >= start) & (positions < start + PIC), j, label)
    return label


def allowed_block(i, j, meta_ref, spans):
    key_pos = j * BLOCK + lax.broadcasted_iota(jnp.int32, (BLOCK, BLOCK), 0)
    row_pos = i * BLOCK + lax.broadcasted_iota(jnp.int32, (BLOCK, BLOCK), 1)
    key_label = span_of(key_pos, meta_ref, spans, -1)
    row_label = span_of(row_pos, meta_ref, spans, -2)
    return (key_pos <= row_pos) | (key_label == row_label)


def crosses(i, meta_ref, spans):
    edge = (i + 1) * BLOCK
    found = jnp.bool_(False)
    for j in range(spans):
        start = meta_ref[2 + j]
        found = found | ((start < edge) & (edge < start + PIC))
    return found


def block_rows(i):
    return pl.ds(pl.multiple_of(i * BLOCK, BLOCK), BLOCK)


def reorder_starts(meta_ref, parts, ring, rows):
    part, spot = meta_ref[0], meta_ref[1]
    for e in range(parts):
        for k in range(ring):
            back = spot - k
            back = jnp.where(back < 0, back + ring, back)
            true_start = ((part ^ e) * ring + back) * rows
            yield e, k, pl.ds(pl.multiple_of(true_start, rows), rows)


def prepare_block(b, heads, qkv_ref, slope_ref, kaug_ref, qaug_ref):
    rows = block_rows(b)
    lane = lax.broadcasted_iota(jnp.int32, (BLOCK, HD), 1)
    pos = b * BLOCK + lax.broadcasted_iota(jnp.int32, (BLOCK, HD), 0)
    ones = jnp.where(lane < 3, 1.0, 0.0).astype(BF)
    for h in range(heads):
        at = h * 3 * HD
        query = qkv_ref[rows, at : at + HD] * jnp.asarray(0.125, BF)
        key = qkv_ref[rows, at + HD : at + 2 * HD]
        offset = pos.astype(F32) * (slope_ref[h] * 0.125)
        high = offset.astype(BF).astype(F32)
        middle = (offset - high).astype(BF).astype(F32)
        low = offset - high - middle
        extra = jnp.where(
            lane == 0, high, jnp.where(lane == 1, middle, jnp.where(lane == 2, low, 0.0))
        ).astype(BF)
        qaug_ref[h, rows, :] = jnp.concatenate([query, ones], axis=1)
        kaug_ref[h, rows, :] = jnp.concatenate([key, extra], axis=1)


def forward_kernel(heads, parts, ring, rows, spans, meta_ref, slope_ref, *refs):
    piece_refs = refs[:parts]
    ctx_ref, qkv_ref, out_t_ref, log_ref, kaug_ref, qaug_ref, vt_ref = refs[parts:]
    length = qkv_ref.shape[0]
    blocks = length // BLOCK
    for e, k, dst in reorder_starts(meta_ref, parts, ring, rows):
        qkv_ref[dst, :] = piece_refs[e][k * rows : (k + 1) * rows, :]
    eye = (
        lax.broadcasted_iota(jnp.int32, (HD, HD), 0) == lax.broadcasted_iota(jnp.int32, (HD, HD), 1)
    ).astype(BF)

    def prepare(b, unused):
        prepare_block(b, heads, qkv_ref, slope_ref, kaug_ref, qaug_ref)
        cols = block_rows(b)
        for h in range(heads):
            at = h * 3 * HD + 2 * HD
            value = qkv_ref[cols, at : at + HD]
            vt_ref[h, :HD, cols] = dot_nt(eye, value).astype(BF)
            row = lax.broadcasted_iota(jnp.int32, (16, BLOCK), 0)
            vt_ref[h, HD:, cols] = jnp.where(row == 0, 1.0, 0.0).astype(BF)
        return unused

    lax.fori_loop(0, blocks, prepare, 0)

    def one_row_block(i, unused):
        rows_i = block_rows(i)
        queries = [qaug_ref[h, rows_i, :] for h in range(heads)]

        def step(j, state, allowed=None):
            cols = block_rows(j)
            new_state = []
            for h in range(heads):
                scores = dot_nt(kaug_ref[h, cols, :], queries[h])
                if allowed is not None:
                    scores = jnp.where(allowed, scores, -1e30)
                top = jnp.max(scores, axis=0, keepdims=True)
                if state is not None:
                    old_top, old_sum = state[h]
                    top = jnp.maximum(top, old_top)
                weight = jnp.exp(scores - top).astype(BF)
                total = dot(vt_ref[h, :, cols], weight)
                if state is not None:
                    total = total + old_sum * jnp.exp(old_top - top)
                new_state.append((top, total))
            return tuple(new_state)

        state = step(i, None, allowed_block(i, i, meta_ref, spans))
        state = lax.fori_loop(0, i, step, state)
        state = lax.cond(
            crosses(i, meta_ref, spans),
            lambda s: step(i + 1, s, allowed_block(i, i + 1, meta_ref, spans)),
            lambda s: s,
            state,
        )
        outs = []
        for h in range(heads):
            top, total = state[h]
            amount = total[HD : HD + 1]
            outs.append(total[:HD] / amount)
            log_ref[h : h + 1, rows_i] = top + jnp.log(amount)
        if heads * HD < 128:
            outs.append(jnp.zeros((128 - heads * HD, BLOCK), F32))
        out_t = jnp.concatenate(outs, axis=0)
        out_t_ref[:, rows_i] = out_t
        turned = out_t.T.astype(BF)[:, : heads * HD]
        for part in range(BLOCK // rows):
            block = i * (BLOCK // rows) + part
            e = (block // ring) ^ meta_ref[0]
            k = meta_ref[1] - block % ring
            k = jnp.where(k < 0, k + ring, k)
            start = pl.multiple_of((e * ring + k) * rows, rows)
            ctx_ref[pl.ds(start, rows), :] = turned[part * rows : (part + 1) * rows]
        return unused

    lax.fori_loop(0, blocks, one_row_block, 0)


def backward_kernel(heads, parts, ring, rows, spans, meta_ref, slope_ref, *refs):
    piece_refs = refs[:parts]
    (
        qkv_ref,
        out_t_ref,
        log_ref,
        grad_ref,
        g_ref,
        kaug_ref,
        qaug_ref,
        kt_ref,
        gq_ref,
        gg_ref,
        delta_ref,
        dqt_ref,
        dkv_ref,
    ) = refs[parts:]
    length = qkv_ref.shape[0]
    blocks = length // BLOCK
    for e, k, dst in reorder_starts(meta_ref, parts, ring, rows):
        g_ref[dst, :] = piece_refs[e][k * rows : (k + 1) * rows, :]
    eye = (
        lax.broadcasted_iota(jnp.int32, (HD, HD), 0) == lax.broadcasted_iota(jnp.int32, (HD, HD), 1)
    ).astype(BF)

    def prepare(b, unused):
        prepare_block(b, heads, qkv_ref, slope_ref, kaug_ref, qaug_ref)
        cols = block_rows(b)
        blank = jnp.zeros((BLOCK, HD), BF)
        grad_t = g_ref[cols, :].astype(F32)
        if heads * HD < 128:
            grad_t = jnp.concatenate([grad_t, jnp.zeros((BLOCK, 128 - heads * HD), F32)], axis=1)
        product = grad_t.T * out_t_ref[:, cols]
        for h in range(heads):
            at = h * 3 * HD
            kt_ref[h, :, cols] = dot_nt(eye, qkv_ref[cols, at + HD : at + 2 * HD]).astype(BF)
            query = qkv_ref[cols, at : at + HD] * jnp.asarray(0.125, BF)
            gq_ref[h, cols, :] = jnp.concatenate([blank, query], axis=1)
            gg_ref[h, cols, :] = jnp.concatenate([g_ref[cols, h * HD : (h + 1) * HD], blank], axis=1)
            delta_ref[h : h + 1, cols] = jnp.sum(
                product[h * HD : (h + 1) * HD], axis=0, keepdims=True
            )
            dkv_ref[h, cols, :] = jnp.zeros((BLOCK, 2 * HD), F32)
        return unused

    lax.fori_loop(0, blocks, prepare, 0)

    def one_row_block(i, unused):
        rows_i = block_rows(i)

        def step(j, state, allowed=None):
            cols = block_rows(j)
            new_state = []
            for h in range(heads):
                at = h * 3 * HD + 2 * HD
                scores = dot_nt(kaug_ref[h, cols, :], qaug_ref[h, rows_i, :])
                if allowed is not None:
                    scores = jnp.where(allowed, scores, -1e30)
                weight = jnp.exp(scores - log_ref[h : h + 1, rows_i])
                grad_weight = dot_nt(
                    qkv_ref[cols, at : at + HD], g_ref[rows_i, h * HD : (h + 1) * HD]
                )
                grad_score = (weight * (grad_weight - delta_ref[h : h + 1, rows_i])).astype(BF)
                dkv_ref[h, cols, :] += dot(weight.astype(BF), gg_ref[h, rows_i, :]) + dot(
                    grad_score, gq_ref[h, rows_i, :]
                )
                new_state.append(state[h] + dot(kt_ref[h, :, cols], grad_score))
            return tuple(new_state)

        state = tuple(jnp.zeros((HD, BLOCK), F32) for _ in range(heads))
        state = step(i, state, allowed_block(i, i, meta_ref, spans))
        state = lax.fori_loop(0, i, step, state)
        state = lax.cond(
            crosses(i, meta_ref, spans),
            lambda s: step(i + 1, s, allowed_block(i, i + 1, meta_ref, spans)),
            lambda s: s,
            state,
        )
        outs = list(state)
        if heads * HD < 128:
            outs.append(jnp.zeros((128 - heads * HD, BLOCK), F32))
        dqt_ref[rows_i, :] = jnp.concatenate(outs, axis=0).T * 0.125
        return unused

    lax.fori_loop(0, blocks, one_row_block, 0)

    def write(b, unused):
        cols = block_rows(b)
        columns = []
        for h in range(heads):
            dkv = dkv_ref[h, cols, :]
            columns += [dqt_ref[cols, h * HD : (h + 1) * HD], dkv[:, HD:], dkv[:, :HD]]
        whole = jnp.concatenate(columns, axis=1).astype(BF)
        for part in range(BLOCK // rows):
            block = b * (BLOCK // rows) + part
            e = (block // ring) ^ meta_ref[0]
            k = meta_ref[1] - block % ring
            k = jnp.where(k < 0, k + ring, k)
            start = pl.multiple_of((e * ring + k) * rows, rows)
            grad_ref[pl.ds(start, rows), :] = whole[part * rows : (part + 1) * rows]
        return unused

    lax.fori_loop(0, blocks, write, 0)


def specs(count_smem, count_vmem):
    return [pl.BlockSpec(memory_space=pltpu.SMEM)] * count_smem + [
        pl.BlockSpec(memory_space=pltpu.VMEM)
    ] * count_vmem


def attend_forward(pieces, meta, slopes, ring, rows):
    heads = slopes.shape[0]
    parts = len(pieces)
    length = parts * pieces[0].shape[0]
    wide = max(128, heads * HD)
    return pl.pallas_call(
        functools.partial(forward_kernel, heads, parts, ring, rows, meta.shape[0] - 2),
        out_shape=(
            jax.ShapeDtypeStruct((length, heads * HD), BF),
            jax.ShapeDtypeStruct((length, heads * 3 * HD), BF),
            jax.ShapeDtypeStruct((wide, length), F32),
            jax.ShapeDtypeStruct((8, length), F32),
        ),
        in_specs=specs(2, parts),
        out_specs=tuple(specs(0, 4)),
        scratch_shapes=[
            pltpu.VMEM((heads, length, 128), BF),
            pltpu.VMEM((heads, length, 128), BF),
            pltpu.VMEM((heads, HD + 16, length), BF),
        ],
        compiler_params=pltpu.CompilerParams(vmem_limit_bytes=VMEM_BYTES),
        cost_estimate=pl.CostEstimate(
            flops=2 * US, bytes_accessed=length * heads * HD * 20, transcendentals=0
        ),
    )(meta, slopes, *pieces)


def attend_backward(pieces, qkv, out_t, logs, meta, slopes, ring, rows):
    heads = slopes.shape[0]
    parts = len(pieces)
    length = qkv.shape[0]
    wide = max(128, heads * HD)
    return pl.pallas_call(
        functools.partial(backward_kernel, heads, parts, ring, rows, meta.shape[0] - 2),
        out_shape=jax.ShapeDtypeStruct((length, heads * 3 * HD), BF),
        in_specs=specs(2, parts + 3),
        out_specs=specs(0, 1)[0],
        scratch_shapes=[
            pltpu.VMEM((length, heads * HD), BF),
            pltpu.VMEM((heads, length, 128), BF),
            pltpu.VMEM((heads, length, 128), BF),
            pltpu.VMEM((heads, HD, length), BF),
            pltpu.VMEM((heads, length, 128), BF),
            pltpu.VMEM((heads, length, 128), BF),
            pltpu.VMEM((8, length), F32),
            pltpu.VMEM((length, wide), F32),
            pltpu.VMEM((heads, length, 128), F32),
        ],
        compiler_params=pltpu.CompilerParams(vmem_limit_bytes=VMEM_BYTES),
        cost_estimate=pl.CostEstimate(
            flops=2 * US, bytes_accessed=length * heads * HD * 20, transcendentals=0
        ),
    )(meta, slopes, *pieces, qkv, out_t, logs)


def take_columns(ref, part, e, width):
    def each(use):
        if width % 128 == 0:
            start = pl.multiple_of((part ^ e) * width, width)
            use(ref.at[:, pl.ds(start, width)])
        else:
            for p in range(SEQ_DEVS):

                @pl.when(part == p)
                def _():
                    use(ref.at[:, pl.ds((p ^ e) * width, width)])

    return each


def column_loop(total, body):
    step = min(256, total)

    def one(i, unused):
        body(pl.ds(pl.multiple_of(i * step, step), step))
        return unused

    lax.fori_loop(0, total // step, one, 0)


def load_weights(w_pieces, w_ref, sems, starts_ref):
    copies = []
    for i, piece in enumerate(w_pieces):
        count = piece.shape[0]
        start = pl.multiple_of(starts_ref[i], min(128, count))
        copy = pltpu.make_async_copy(piece, w_ref.at[pl.ds(start, count), :], sems.at[i])
        copy.start()
        copies.append(copy)
    return copies


def qkv_kernel(ring, n_w, meta_ref, starts_ref, *refs):
    h_pieces = refs[:ring]
    gain_ref, shift_ref, a_ref, b_ref, bias_ref = refs[ring : ring + 5]
    w_pieces = refs[ring + 5 : ring + 5 + n_w]
    outs = refs[ring + 5 + n_w :]
    q_refs, u_ref, x_ref = outs[:SEQ_DEVS], outs[SEQ_DEVS], outs[SEQ_DEVS + 1]
    o_ref, w_ref, sems = outs[SEQ_DEVS + 2 :]
    copies = load_weights(w_pieces, w_ref, sems, starts_ref)
    rows = h_pieces[0].shape[0]
    for k in range(ring):
        normed, unused, unused = norm_forward(
            h_pieces[k][...].astype(F32), gain_ref[...], shift_ref[...]
        )
        x_ref[k * rows : (k + 1) * rows, :] = normed.astype(BF)
    u_ref[...] = dot_nt(x_ref[...], a_ref[...]).astype(BF)
    for copy in copies:
        copy.wait()

    def body(cols):
        total = dot(x_ref[...], w_ref[:, cols])
        total = total + FACTOR * dot(u_ref[...], b_ref[:, cols]) + bias_ref[:, cols]
        o_ref[:, cols] = total.astype(BF)

    column_loop(o_ref.shape[1], body)
    for e in range(SEQ_DEVS):

        def store(src, e=e):
            q_refs[e][...] = src[...]

        take_columns(o_ref, meta_ref[0], e, q_refs[e].shape[1])(store)


def qkv_product(h_pieces, gain, shift, a, b, bias, w_pieces, starts, meta):
    ring, n_w = len(h_pieces), len(w_pieces)
    rows, depth = h_pieces[0].shape
    cols = b.shape[1]
    outs = pl.pallas_call(
        functools.partial(qkv_kernel, ring, n_w),
        out_shape=tuple(
            [jax.ShapeDtypeStruct((ring * rows, cols // SEQ_DEVS), BF)] * SEQ_DEVS
            + [
                jax.ShapeDtypeStruct((ring * rows, a.shape[0]), BF),
                jax.ShapeDtypeStruct((ring * rows, depth), BF),
            ]
        ),
        in_specs=specs(2, ring + 5) + [pl.BlockSpec(memory_space=pl.ANY)] * n_w,
        out_specs=tuple(specs(0, SEQ_DEVS + 2)),
        scratch_shapes=[
            pltpu.VMEM((ring * rows, cols), BF),
            pltpu.VMEM((depth, cols), BF),
            pltpu.SemaphoreType.DMA((n_w,)),
        ],
        compiler_params=pltpu.CompilerParams(vmem_limit_bytes=VMEM_BYTES),
        cost_estimate=pl.CostEstimate(
            flops=2 * US, bytes_accessed=2**20, transcendentals=0
        ),
    )(meta, starts, *h_pieces, gain, shift, a, b, bias, *w_pieces)
    return list(outs[:SEQ_DEVS]), outs[SEQ_DEVS], outs[SEQ_DEVS + 1]


def load_kernel(src_ref, dst_ref, sems):
    count = src_ref.shape[0]
    copies = [
        pltpu.make_async_copy(src_ref.at[i], dst_ref.at[i], sems.at[i]) for i in range(count)
    ]
    for copy in copies:
        copy.start()
    for copy in copies:
        copy.wait()


def load_to_vmem(array):
    return pl.pallas_call(
        load_kernel,
        out_shape=pltpu.VMEM(array.shape, array.dtype),
        in_specs=[pl.BlockSpec(memory_space=pl.ANY)],
        out_specs=pl.BlockSpec(memory_space=pltpu.VMEM),
        scratch_shapes=[pltpu.SemaphoreType.DMA((array.shape[0],))],
        compiler_params=pltpu.CompilerParams(vmem_limit_bytes=2 * 1024 * 1024),
        cost_estimate=pl.CostEstimate(
            flops=5 * US, bytes_accessed=2 * array.size, transcendentals=0
        ),
    )(pltpu.with_memory_space_constraint(array, pltpu.HBM))


def out_kernel(ring, meta_ref, *refs):
    c_pieces = refs[:SEQ_DEVS]
    a_ref, b_ref, w_ref = refs[SEQ_DEVS : SEQ_DEVS + 3]
    p_refs = refs[SEQ_DEVS + 3 : SEQ_DEVS + 3 + ring]
    ctx_ref, u_ref = refs[SEQ_DEVS + 3 + ring :]
    rows = p_refs[0].shape[0]
    width = c_pieces[0].shape[1]
    for e in range(SEQ_DEVS):

        def store(dst, e=e):
            dst[...] = c_pieces[e][...]

        take_columns(ctx_ref, meta_ref[0], e, width)(store)
    u_ref[...] = dot_nt(ctx_ref[...], a_ref[...]).astype(BF)
    shards, unused, wide = w_ref.shape
    for j in range(shards):
        cols = slice(j * wide, (j + 1) * wide)
        total = dot(ctx_ref[...], w_ref[j]) + FACTOR * dot(u_ref[...], b_ref[:, cols])
        total = total.astype(BF)
        for k in range(ring):
            p_refs[k][:, cols] = total[k * rows : (k + 1) * rows]


def out_product(c_pieces, a, b, w, meta, ring):
    count, width = c_pieces[0].shape
    rank, depth = b.shape
    outs = pl.pallas_call(
        functools.partial(out_kernel, ring),
        out_shape=tuple(
            [jax.ShapeDtypeStruct((count // ring, depth), BF)] * ring
            + [
                jax.ShapeDtypeStruct((count, width * SEQ_DEVS), BF),
                jax.ShapeDtypeStruct((count, rank), BF),
            ]
        ),
        in_specs=specs(1, SEQ_DEVS + 3),
        out_specs=tuple(specs(0, ring + 2)),
        compiler_params=pltpu.CompilerParams(vmem_limit_bytes=VMEM_BYTES),
        cost_estimate=pl.CostEstimate(
            flops=2 * count * depth * width * SEQ_DEVS,
            bytes_accessed=8 * depth * width * SEQ_DEVS,
            transcendentals=0,
        ),
    )(meta, *c_pieces, a, b, w)
    return list(outs[:ring]), outs[ring], outs[ring + 1]


def mlp_kernel(count, add, *refs):
    n2_refs, gy_refs = refs[:count], refs[count : 2 * count]
    refs = refs[2 * count :]
    a1_ref, b2_ref, b1_ref, a2_ref, bias_ref, w_ref = refs[:6]
    before, refs = refs[6 : 6 + add], refs[6 + add :]
    p_refs, m_refs, grads = refs[:count], refs[count : 2 * count], refs[2 * count : 2 * count + 4]
    x_ref, g_ref, act_ref, slope_ref, gf_ref = refs[2 * count + 4 :]
    shards, double, depth, wide = w_ref.shape
    chunks = double // 2
    rows = n2_refs[0].shape[0]
    for k in range(count):
        x_ref[k * rows : (k + 1) * rows, :] = n2_refs[k][...]
        g_ref[k * rows : (k + 1) * rows, :] = gy_refs[k][...]
    u3 = dot_nt(x_ref[...], a1_ref[...]).astype(BF)
    gu4 = (FACTOR * dot_nt(g_ref[...], b2_ref[...])).astype(BF)
    for h in range(chunks):
        cols = slice(h * wide, (h + 1) * wide)
        f = dot(x_ref[...], w_ref[:, h].reshape(shards * depth, wide))
        f = f + FACTOR * dot(u3, b1_ref[:, cols]) + bias_ref[:, cols]
        act, slope = gelu_and_slope(f)
        act_ref[:, cols] = act.astype(BF)
        slope_ref[:, cols] = slope
    for h in range(chunks):
        cols = slice(h * wide, (h + 1) * wide)
        gact = dot(gu4, a2_ref[:, cols])
        for j in range(shards):
            gact = gact + dot_nt(g_ref[:, j * wide : (j + 1) * wide], w_ref[j, chunks + h])
        gf_ref[:, cols] = (gact * slope_ref[:, cols]).astype(BF)
    gu3 = (FACTOR * dot_nt(gf_ref[...], b1_ref[...])).astype(BF)
    for j in range(shards):
        cols = slice(j * depth, (j + 1) * depth)
        total = dot(gu3, a1_ref[:, cols])
        for h in range(chunks):
            total = total + dot_nt(gf_ref[:, h * wide : (h + 1) * wide], w_ref[j, h])
        total = total.astype(BF)
        for k in range(count):
            p_refs[k][:, cols] = total[k * rows : (k + 1) * rows]
    u4 = dot_nt(act_ref[...], a2_ref[...]).astype(BF)
    for j in range(shards):
        cols = slice(j * wide, (j + 1) * wide)
        total = dot(act_ref[...], w_ref[j, chunks:].reshape(chunks * depth, wide))
        total = (total + FACTOR * dot(u4, b2_ref[:, cols])).astype(BF)
        for k in range(count):
            m_refs[k][:, cols] = total[k * rows : (k + 1) * rows]
    products = [
        FACTOR * dot_tn(u3, gf_ref[...]),
        dot_tn(gu4, act_ref[...]),
        dot_tn(gu3, x_ref[...]),
        FACTOR * dot_tn(u4, g_ref[...]),
    ]
    for i, product in enumerate(products):
        grads[i][...] = product + before[i][...] if add else product


def mlp_both_ways(n2_pieces, gy_pieces, a1, b1, a2, b2, bias, w_fc, before):
    count = len(n2_pieces)
    rows, depth = n2_pieces[0].shape
    rank, hidden = b1.shape
    total = count * rows
    outs = pl.pallas_call(
        functools.partial(mlp_kernel, count, len(before)),
        out_shape=(
            [jax.ShapeDtypeStruct((rows, depth), BF)] * (2 * count)
            + [jax.ShapeDtypeStruct((rank, hidden), F32)] * 2
            + [jax.ShapeDtypeStruct((rank, depth), F32)] * 2
        ),
        in_specs=specs(0, 2 * count + 6 + len(before)),
        out_specs=specs(0, 2 * count + 4),
        scratch_shapes=[
            pltpu.VMEM((total, depth), BF),
            pltpu.VMEM((total, depth), BF),
            pltpu.VMEM((total, hidden), BF),
            pltpu.VMEM((total, hidden), F32),
            pltpu.VMEM((total, hidden), BF),
        ],
        compiler_params=pltpu.CompilerParams(vmem_limit_bytes=SMALL_VMEM_BYTES),
        cost_estimate=pl.CostEstimate(
            flops=10 * US, bytes_accessed=4 * depth * hidden, transcendentals=0
        ),
    )(*n2_pieces, *gy_pieces, a1, b2, b1, a2, bias, w_fc, *before)
    return list(outs[:count]), list(outs[count : 2 * count]), list(outs[2 * count :])


def gctx_kernel(ring, meta_ref, *refs):
    g_pieces = refs[:ring]
    a_ref, b_ref, w_ref, ctx_ref, u2_ref = refs[ring : ring + 5]
    c_refs = refs[ring + 5 : ring + 5 + SEQ_DEVS]
    gb_ref, ga_ref, g_ref, o_ref = refs[ring + 5 + SEQ_DEVS :]
    rows = g_pieces[0].shape[0]
    for k in range(ring):
        g_ref[k * rows : (k + 1) * rows, :] = g_pieces[k][...]
    gu2 = (FACTOR * dot_nt(g_ref[...], b_ref[...])).astype(BF)
    shards, unused, wide = w_ref.shape
    total = dot(gu2, a_ref[...])
    for j in range(shards):
        total = total + dot_nt(g_ref[:, j * wide : (j + 1) * wide], w_ref[j])
    o_ref[...] = total.astype(BF)
    for e in range(SEQ_DEVS):

        def store(src, e=e):
            c_refs[e][...] = src[...]

        take_columns(o_ref, meta_ref[0], e, c_refs[e].shape[1])(store)
    gb_ref[...] = FACTOR * dot_tn(u2_ref[...], g_ref[...])
    ga_ref[...] = dot_tn(gu2, ctx_ref[...])


def gctx_product(g_pieces, a, b, w, ctx, u2, meta):
    ring = len(g_pieces)
    rows, depth = g_pieces[0].shape
    count, cols = ctx.shape
    rank = a.shape[0]
    outs = pl.pallas_call(
        functools.partial(gctx_kernel, ring),
        out_shape=tuple(
            [jax.ShapeDtypeStruct((count, cols // SEQ_DEVS), BF)] * SEQ_DEVS
            + [jax.ShapeDtypeStruct((rank, depth), F32), jax.ShapeDtypeStruct((rank, cols), F32)]
        ),
        in_specs=specs(1, ring + 5),
        out_specs=tuple(specs(0, SEQ_DEVS + 2)),
        scratch_shapes=[pltpu.VMEM((count, depth), BF), pltpu.VMEM((count, cols), BF)],
        compiler_params=pltpu.CompilerParams(vmem_limit_bytes=VMEM_BYTES),
        cost_estimate=pl.CostEstimate(
            flops=2 * count * depth * cols, bytes_accessed=8 * depth * cols, transcendentals=0
        ),
    )(meta, *g_pieces, a, b, w, ctx, u2)
    return list(outs[:SEQ_DEVS]), outs[SEQ_DEVS], outs[SEQ_DEVS + 1]


def joined_kernel(meta_ref, *refs):
    q_pieces = refs[:SEQ_DEVS]
    x_ref, b_ref, u1_ref, gb_ref, ga_ref, gu_ref, q_ref = refs[SEQ_DEVS:]
    for e in range(SEQ_DEVS):

        def store(dst, e=e):
            dst[...] = q_pieces[e][...]

        take_columns(q_ref, meta_ref[0], e, q_pieces[e].shape[1])(store)
    gu1 = (FACTOR * dot_nt(q_ref[...], b_ref[...])).astype(BF)
    gu_ref[...] = gu1
    gb_ref[...] = FACTOR * dot_tn(u1_ref[...], q_ref[...])
    ga_ref[...] = dot_tn(gu1, x_ref[...])


def joined_gradients(q_pieces, n1, b, u1, meta):
    rank, cols = b.shape
    count, depth = n1.shape
    return pl.pallas_call(
        joined_kernel,
        out_shape=(
            jax.ShapeDtypeStruct((rank, cols), F32),
            jax.ShapeDtypeStruct((rank, depth), F32),
            jax.ShapeDtypeStruct((count, rank), BF),
            jax.ShapeDtypeStruct((count, cols), BF),
        ),
        in_specs=specs(1, SEQ_DEVS + 3),
        out_specs=tuple(specs(0, 4)),
        compiler_params=pltpu.CompilerParams(vmem_limit_bytes=VMEM_BYTES),
        cost_estimate=pl.CostEstimate(
            flops=4 * US, bytes_accessed=2 * count * (cols + depth), transcendentals=0
        ),
    )(meta, *q_pieces, n1, b, u1)


def gn1_kernel(ring, n_w, starts_ref, q_ref, gu_ref, a_ref, *refs):
    w_pieces, p_refs = refs[:n_w], refs[n_w : n_w + ring]
    w_ref, sems = refs[n_w + ring :]
    copies = load_weights(w_pieces, w_ref, sems, starts_ref)
    rows = p_refs[0].shape[0]
    for copy in copies:
        copy.wait()

    def body(cols):
        total = dot_nt(q_ref[...], w_ref[cols, :]) + dot(gu_ref[...], a_ref[:, cols])
        total = total.astype(BF)
        for k in range(ring):
            p_refs[k][:, cols] = total[k * rows : (k + 1) * rows]

    column_loop(w_ref.shape[0], body)


def gn1_product(gqkv, gu1, a, w_pieces, starts, ring):
    n_w = len(w_pieces)
    count, cols = gqkv.shape
    rank, depth = a.shape
    return list(
        pl.pallas_call(
            functools.partial(gn1_kernel, ring, n_w),
            out_shape=tuple([jax.ShapeDtypeStruct((count // ring, depth), BF)] * ring),
            in_specs=specs(1, 3) + [pl.BlockSpec(memory_space=pl.ANY)] * n_w,
            out_specs=tuple(specs(0, ring)),
            scratch_shapes=[pltpu.VMEM((depth, cols), BF), pltpu.SemaphoreType.DMA((n_w,))],
            compiler_params=pltpu.CompilerParams(vmem_limit_bytes=VMEM_BYTES),
            cost_estimate=pl.CostEstimate(
                flops=6 * US, bytes_accessed=2 * depth * cols, transcendentals=0
            ),
        )(starts, gqkv, gu1, a, *w_pieces)
    )


def pack_kernel(n_full, ring, groups, meta_ref, *refs):
    stacks, (full_ref, cols_ref) = refs[:-2], refs[-2:]
    part, spot = meta_ref[0], meta_ref[1]
    at = 0
    for ref in stacks[:n_full]:
        width = ref.shape[1] // (ring * SEQ_DEVS * groups)
        for g in range(groups):
            for p in range(SEQ_DEVS):
                for z in range(ring):
                    k = z - spot
                    k = jnp.where(k < 0, k + ring, k)
                    column = ((g * SEQ_DEVS + p) * ring + z) * width
                    full_ref[k, part ^ p, g, :, at : at + width] = ref[
                        :, column : column + width
                    ].astype(BF)
        at += width
    at = 0
    for ref in stacks[n_full:]:
        width = ref.shape[1] // (SEQ_DEVS * groups)
        for p in range(SEQ_DEVS):
            for r in range(groups):
                column = (p * groups + r) * width
                cols_ref[part ^ p, r, :, at : at + width] = ref[:, column : column + width].astype(
                    BF
                )
        at += width


def pack(full, own, meta, groups):
    ring, n = lax.axis_size("tensor"), lax.axis_size("dp")
    rank = full[0].shape[0]
    full_widths = [g.shape[1] // (ring * n) for g in full]
    own_widths = [g.shape[1] // n for g in own]
    packed, packed_own = pl.pallas_call(
        functools.partial(pack_kernel, len(full), ring, groups),
        out_shape=(
            jax.ShapeDtypeStruct((ring, SEQ_DEVS, groups, rank, sum(full_widths)), BF),
            jax.ShapeDtypeStruct((SEQ_DEVS, groups, rank, sum(own_widths)), BF),
        ),
        in_specs=specs(1, len(full) + len(own)),
        out_specs=tuple(specs(0, 2)),
        compiler_params=pltpu.CompilerParams(vmem_limit_bytes=VMEM_BYTES),
        cost_estimate=pl.CostEstimate(flops=2 * US, bytes_accessed=2**20, transcendentals=0),
    )(meta, *full, *own)
    return Side(reduce_stages(packed, packed_own, full_widths, own_widths, groups))


def reduce_stages(packed, packed_own, full_widths, own_widths, groups):
    ring, n = lax.axis_size("tensor"), lax.axis_size("dp")
    spot, data = lax.axis_index("tensor"), lax.axis_index("dp")
    group = data // SEQ_DEVS
    wide = sum(full_widths)
    landed = yield [
        lax.ppermute(packed[k], "tensor", [(i, (i + k) % ring) for i in range(ring)])
        for k in range(1, ring)
    ]
    total = sum([x.astype(F32) for x in landed], packed[0].astype(F32)).astype(BF)
    total = jnp.concatenate([total, packed_own], axis=3)
    landed = yield [exchange(total[e], e) for e in range(1, SEQ_DEVS)]
    own = sum([x.astype(F32) for x in landed], total[0].astype(F32)).astype(BF)

    def block(k):
        return lax.dynamic_index_in_dim(own, (group + k) % groups, 0, keepdims=False)

    flying = []
    for k in range(1, groups):
        pairs = [(i, (i + k * SEQ_DEVS) % n) for i in range(n)]
        flying.append(lax.ppermute(block(k)[:, :wide], "dp", pairs))
    for k in range(groups):
        pairs = []
        for i in range(n):
            for z in range(ring):
                r = (i // SEQ_DEVS + k) % groups
                pairs.append((i * ring + z, z * n + (i % SEQ_DEVS) * groups + r))
        flying.append(lax.ppermute(block(k)[:, wide:], ("dp", "tensor"), pairs))
    landed = yield flying
    full = [block(0)[:, :wide]] + list(landed[: groups - 1])
    full = [(piece, (group - k) % groups) for k, piece in enumerate(full)]
    mine = (data * ring + spot) % groups
    cols = [(piece, (mine - k) % groups) for k, piece in enumerate(landed[groups - 1 :])]
    return (full, full_widths), (cols, own_widths)


def place(pieces, widths, seq_adapter):
    slots = jnp.arange(ADAPTERS, dtype=jnp.int32)
    whole = 0.0
    for piece, sequence in pieces:
        slot = lax.dynamic_index_in_dim(seq_adapter, sequence, 0, keepdims=False)
        whole = whole + jnp.where((slots == slot)[:, None, None], piece[None].astype(F32), 0.0)
    outs, at = [], 0
    for width in widths:
        outs.append(whole[:, :, at : at + width])
        at += width
    return outs


def gather_first(shard, rows_in, data, small):
    n, count = lax.axis_size("dp"), shard.shape[0]
    if n != 8 or lax.axis_size("tensor") != 4:
        whole = lax.all_gather(shard, "dp", axis=0, tiled=True)
        return [whole], [0 * data], ring_gather(rows_in, "tensor"), (), small
    half = count // 2
    by_x, by_y, by_c = exchange(shard, 2), exchange(shard, 4), exchange(shard, 1)
    ring = [rows_in, shift_one(rows_in, "tensor")]
    by_x, by_y, by_c, ring[1], *small = lax.optimization_barrier(
        (by_x, by_y, by_c, ring[1]) + small
    )
    corner_a, corner_b = exchange(by_x[:half], 4), exchange(by_y[half:], 2)
    by_xc, by_yc = exchange(by_x, 1), exchange(by_y, 1)
    ring.append(shift_one(ring[1], "tensor"))
    corner_a, corner_b, by_xc, by_yc, ring[2] = lax.optimization_barrier(
        (corner_a, corner_b, by_xc, by_yc, ring[2])
    )
    far_a, far_b = exchange(corner_a, 1), exchange(corner_b, 1)
    ring.append(shift_one(ring[2], "tensor"))
    pieces = [shard, by_c, by_x, by_xc, by_y, by_yc, corner_a, far_a, corner_b, far_b]
    starts = [(data ^ e) * count for e in range(8)]
    starts += [(data ^ e) * count + half for e in (6, 7)]
    return pieces, starts, ring, (corner_a, corner_b), small


def swap_heads(pieces):
    across, far, near = exchange(pieces[2], 2), exchange(pieces[3], 2), exchange(pieces[1], 1)
    across, far, near = lax.optimization_barrier((across, far, near))
    return [pieces[0], near, across, exchange(far, 1)]


def local(
    hidden_in,
    ln1_gain,
    ln1_bias,
    qkv_weight,
    joined_bias,
    out_weight,
    output_bias,
    ln2_gain,
    ln2_bias,
    fc1_weight,
    first_feed_bias,
    fc2_weight,
    second_feed_bias,
    qkv_down,
    qkv_up,
    out_down,
    out_up,
    fc1_down,
    fc1_up,
    fc2_down,
    fc2_up,
    seq_adapter,
    span_starts,
    cotangent,
):
    spot = lax.axis_index("tensor")
    data = lax.axis_index("dp")
    ring = lax.axis_size("tensor")
    groups = lax.axis_size("dp") // SEQ_DEVS
    group, part = data // SEQ_DEVS, data % SEQ_DEVS
    rows = hidden_in.shape[0]
    slot = lax.dynamic_index_in_dim(seq_adapter, group, 0, keepdims=False)
    starts = lax.dynamic_index_in_dim(span_starts, group, 0, keepdims=False)
    qkv_cols, ctx_cols, hidden_cols = qkv_weight.shape[1], out_weight.shape[0], fc1_weight.shape[1]
    heads = qkv_cols // (3 * HD) // SEQ_DEVS
    meta = jnp.concatenate([jnp.stack([part, spot]), starts]).astype(jnp.int32)
    first_head = (spot * SEQ_DEVS + part) * heads
    slopes = jnp.exp2(
        -8.0 * ((first_head + jnp.arange(heads, dtype=jnp.int32)).astype(F32) + 1.0) / H
    )

    def pick(stack):
        return lax.dynamic_index_in_dim(stack, slot, 0, keepdims=False)

    def own_cols(matrix, count):
        return lax.dynamic_slice_in_dim(matrix, spot * count, count, 1)

    a_q, b_q = pick(qkv_down), own_cols(pick(qkv_up), qkv_cols)
    a_o, b_o = own_cols(pick(out_down), ctx_cols), pick(out_up)
    a_1, b_1 = pick(fc1_down), own_cols(pick(fc1_up), hidden_cols)
    a_2, b_2 = own_cols(pick(fc2_down), hidden_cols), pick(fc2_up)

    n = lax.axis_size("dp")
    shard = fc1_weight.shape[0]
    chunks = hidden_cols // shard
    fc_shard = jnp.concatenate(
        [
            jnp.transpose(fc1_weight.reshape(shard, chunks, shard), (1, 0, 2)).reshape(-1, shard),
            fc2_weight,
        ],
        axis=0,
    )
    w_qkv, w_starts, h_pieces, corners, small = gather_first(
        qkv_weight, hidden_in, data, (fc_shard, a_q, b_q, a_o, b_o, a_1, b_1, a_2, b_2, slopes)
    )
    fc_shard, a_q, b_q, a_o, b_o, a_1, b_1, a_2, b_2, slopes = small
    w_starts = jnp.stack(w_starts).astype(jnp.int32)
    held_out, *unused = lax.optimization_barrier((out_weight,) + corners)
    w_out = lax.all_gather(held_out, "dp", axis=0, tiled=False)

    x = hidden_in.astype(F32)
    unused, unit1, inverse1 = norm_forward(x, ln1_gain, ln1_bias)
    h_pieces[-1], cotangent_held = lax.optimization_barrier((h_pieces[-1], cotangent))
    gy = [cotangent, shift_one(cotangent_held, "tensor")]
    pieces, u1, n1 = qkv_product(
        h_pieces, ln1_gain[None], ln1_bias[None], a_q, b_q, joined_bias[None], w_qkv, w_starts, meta
    )
    pieces, gy = lax.optimization_barrier((pieces, gy))
    gy.append(shift_one(gy[-1], "tensor"))
    pieces = swap_heads(pieces)
    fc_shard, pieces, gy = lax.optimization_barrier((fc_shard, pieces, gy))
    gy += ring_gather(gy[-1], "tensor", ring - 3)[1:]
    w_fc = lax.all_gather(fc_shard, "dp", axis=0, tiled=True)
    w_fc = w_fc.reshape(n, 2 * chunks, shard, shard)
    ctx_rel, qkv_true, out_t, logs = attend_forward(pieces, meta, slopes, ring, rows)
    ctx_rel, gy = lax.optimization_barrier((ctx_rel, gy))
    count = ring * rows
    pieces = swap_heads([ctx_rel[e * count : (e + 1) * count] for e in range(SEQ_DEVS)])
    part_out, ctx, u2 = out_product(pieces, a_o, b_o, w_out, meta, ring)
    loads = []

    def load_beside(moved):
        loads.append(moved)
        if len(loads) == ring - 1:
            moved, loads[-1] = lax.optimization_barrier(
                (moved, load_to_vmem(hold(w_fc, loads[-2])))
            )
        return moved

    mid = x + (ring_scatter(part_out, "tensor", (load_beside,)) + output_bias)
    w_near = loads[-1]

    normed2, unit2, inverse2 = norm_forward(mid, ln2_gain, ln2_bias)
    n2 = ring_gather(normed2.astype(BF), "tensor")
    part_in2, part_mlp, fc_grads = [], [], []
    for k in range(ring):
        grad_pieces, out_pieces, fc_grads = mlp_both_ways(
            n2[k : k + 1],
            gy[k : k + 1],
            a_1,
            b_1,
            a_2,
            b_2,
            first_feed_bias[None],
            w_near,
            fc_grads,
        )
        part_in2 += grad_pieces
        part_mlp += out_pieces
    g_b1, g_a2, g_a1, g_b2 = fc_grads
    grad_n2 = ring_scatter(part_in2, "tensor")
    grad_mid = cotangent.astype(F32) + norm_backward(grad_n2, unit2, inverse2, ln2_gain)
    gm = ring_gather(grad_mid.astype(BF), "tensor")

    mlp_total, gm = lax.optimization_barrier((part_mlp[1], gm))
    mlp_total = shift_one(mlp_total, "tensor")
    pieces, g_bo, g_ao = gctx_product(gm, a_o, b_o, w_out, ctx, u2, meta)
    early = pack([g_a1, g_b2, g_bo], [g_b1, g_a2, g_ao], meta, groups)
    pieces = swap_heads(pieces)
    grad_rel = attend_backward(pieces, qkv_true, out_t, logs, meta, slopes, ring, rows)
    grad_rel, mlp_total = lax.optimization_barrier((grad_rel, mlp_total))
    mlp_total = shift_one((mlp_total.astype(F32) + part_mlp[2].astype(F32)).astype(BF), "tensor")
    early.step(grad_rel)
    pieces = swap_heads([grad_rel[e * count : (e + 1) * count] for e in range(SEQ_DEVS)])
    pieces, mlp_total = lax.optimization_barrier((pieces, mlp_total))
    early.step(pieces[3])
    mlp_total = ring_scatter([part_mlp[0], mlp_total] + part_mlp[3:], "tensor", first=True)
    g_bq, g_aq, gu1, gqkv = joined_gradients(pieces, n1, b_q, u1, meta)
    late = pack([g_aq], [g_bq], meta, groups)
    part_in1 = gn1_product(gqkv, gu1, a_q, w_qkv, w_starts, ring)
    part_in1, mlp_total = lax.optimization_barrier((part_in1, mlp_total))
    layer_output = (mid + (mlp_total + second_feed_bias)).astype(BF)
    early.step(part_in1[0])
    grad_n1 = ring_scatter(part_in1, "tensor", (late,))
    hidden_grad = grad_mid + norm_backward(grad_n1, unit1, inverse1, ln1_gain)

    g_a1, g_b2, g_bo = place(*early.result[0], seq_adapter)
    g_b1, g_a2, g_ao = place(*early.result[1], seq_adapter)
    (g_aq,) = place(*late.result[0], seq_adapter)
    (g_bq,) = place(*late.result[1], seq_adapter)
    return (layer_output, hidden_grad, g_aq, g_bq, g_ao, g_bo, g_a1, g_b1, g_a2, g_b2)


def solution(mesh):
    rows, cols = P(("dp", "tensor"), None), P(None, None, ("dp", "tensor"))
    placed = (
        rows,
        P(),
        P(),
        P("dp", "tensor"),
        P("tensor"),
        P("tensor", "dp"),
        P(),
        P(),
        P(),
        P("dp", "tensor"),
        P("tensor"),
        P("tensor", "dp"),
    ) + (P(),) * 11 + (rows,)
    return jax.shard_map(
        local,
        mesh=mesh,
        in_specs=placed,
        out_specs=(rows, rows) + (cols,) * 8,
        check_vma=False,
    )
```

```python
import functools

import jax
import jax.numpy as jnp
from jax import lax
from jax.experimental import pallas as pl
from jax.experimental.pallas import tpu as pltpu
from jax.sharding import PartitionSpec as P

H = 32
HD = 64
ADAPTERS = 8
SEQ_DEVS = 4
PIC = 256
EPS = 1e-05
FACTOR = 0.5
BF = jnp.bfloat16
F32 = jnp.float32
BLOCK = 256
VMEM_BYTES = 56 * 1024 * 1024
SMALL_VMEM_BYTES = 28 * 1024 * 1024
US = 10**9


def dot(a, b):
    return jnp.dot(a, b, preferred_element_type=F32)


def dot_nt(a, b):
    return lax.dot_general(a, b, (((1,), (1,)), ((), ())), preferred_element_type=F32)


def dot_tn(a, b):
    return lax.dot_general(a, b, (((0,), (0,)), ((), ())), preferred_element_type=F32)


def hold(value, *until):
    return lax.optimization_barrier((value,) + until)[0]


def gelu_and_slope(f):
    phi = 0.5 * (1.0 + lax.erf(f * (0.5**0.5)))
    density = jnp.exp(-0.5 * f * f) * (0.5 / jnp.pi) ** 0.5
    return f * phi, phi + f * density


def norm_forward(values, gain, shift):
    centred = values - jnp.mean(values, axis=-1, keepdims=True)
    inverse = lax.rsqrt(jnp.mean(centred * centred, axis=-1, keepdims=True) + EPS)
    unit = centred * inverse
    return unit * gain + shift, unit, inverse


def norm_backward(upstream, unit, inverse, gain):
    scaled = upstream * gain
    return inverse * (
        scaled
        - jnp.mean(scaled, axis=-1, keepdims=True)
        - unit * jnp.mean(scaled * unit, axis=-1, keepdims=True)
    )


def shift_one(array, axis):
    n = lax.axis_size(axis)
    return lax.ppermute(array, axis, [(i, (i + 1) % n) for i in range(n)])


def ring_gather(array, axis, hops=None):
    pieces = [array]
    for _ in range(lax.axis_size(axis) - 1 if hops is None else hops):
        pieces.append(shift_one(pieces[-1], axis))
    return pieces


def halves(array):
    middle = array.shape[0] // 2
    return [array[:middle], array[middle:]]


def shift_all(arrays, axis):
    return [shift_one(a, axis) for a in arrays]


class Side:
    def __init__(self, operands, stages):
        self.operands, self.make, self.stages = operands, stages, None
        self.flying, self.result = (), None

    def step(self, beside):
        if self.result is not None:
            return beside
        if self.stages is None:
            beside, self.operands = lax.optimization_barrier((beside, self.operands))
            self.stages = self.make(*self.operands)
            self.flying = next(self.stages)
            return beside
        beside, landed = lax.optimization_barrier((beside, self.flying))
        try:
            self.flying = self.stages.send(landed)
        except StopIteration as stop:
            self.result = stop.value
        return beside


def add_terms(moved, terms, dtype):
    return [(m.astype(F32) + t.astype(F32)).astype(dtype) for m, t in zip(moved, terms)]


def ring_scatter(pieces, axis, beside=None, moved=None):
    following = pieces[2:] + pieces[:1]
    total = None if moved is not None else pieces[1]
    for i, terms in enumerate(following):
        if total is not None:
            moved = shift_all(total, axis)
        if beside is not None:
            moved = beside(i, moved)
        total = add_terms(moved, terms, F32 if i == len(following) - 1 else BF)
    return total


def exchange(array, distance):
    n = lax.axis_size("dp")
    return lax.ppermute(array, "dp", [(i, i ^ distance) for i in range(n)])


def span_of(positions, meta_ref, spans, outside):
    label = jnp.full(positions.shape, outside, jnp.int32)
    for j in range(spans):
        start = meta_ref[2 + j]
        label = jnp.where((positions >= start) & (positions < start + PIC), j, label)
    return label


def allowed_block(i, j, meta_ref, spans):
    key_pos = j * BLOCK + lax.broadcasted_iota(jnp.int32, (BLOCK, BLOCK), 0)
    row_pos = i * BLOCK + lax.broadcasted_iota(jnp.int32, (BLOCK, BLOCK), 1)
    key_label = span_of(key_pos, meta_ref, spans, -1)
    row_label = span_of(row_pos, meta_ref, spans, -2)
    return (key_pos <= row_pos) | (key_label == row_label)


def crosses(i, meta_ref, spans):
    edge = (i + 1) * BLOCK
    found = jnp.bool_(False)
    for j in range(spans):
        start = meta_ref[2 + j]
        found = found | ((start < edge) & (edge < start + PIC))
    return found


def block_rows(i):
    return pl.ds(pl.multiple_of(i * BLOCK, BLOCK), BLOCK)


def reorder_starts(meta_ref, parts, ring, rows):
    part, spot = meta_ref[0], meta_ref[1]
    for e in range(parts):
        for k in range(ring):
            back = spot - k
            back = jnp.where(back < 0, back + ring, back)
            true_start = ((part ^ e) * ring + back) * rows
            yield e, k, pl.ds(pl.multiple_of(true_start, rows), rows)


def prepare_block(b, heads, qkv_ref, slope_ref, kaug_ref, qaug_ref):
    rows = block_rows(b)
    lane = lax.broadcasted_iota(jnp.int32, (BLOCK, HD), 1)
    pos = b * BLOCK + lax.broadcasted_iota(jnp.int32, (BLOCK, HD), 0)
    ones = jnp.where(lane < 3, 1.0, 0.0).astype(BF)
    for h in range(heads):
        at = h * 3 * HD
        query = qkv_ref[rows, at : at + HD] * jnp.asarray(0.125, BF)
        key = qkv_ref[rows, at + HD : at + 2 * HD]
        offset = pos.astype(F32) * (slope_ref[h] * 0.125)
        high = offset.astype(BF).astype(F32)
        middle = (offset - high).astype(BF).astype(F32)
        low = offset - high - middle
        extra = jnp.where(
            lane == 0, high, jnp.where(lane == 1, middle, jnp.where(lane == 2, low, 0.0))
        ).astype(BF)
        qaug_ref[h, rows, :] = jnp.concatenate([query, ones], axis=1)
        kaug_ref[h, rows, :] = jnp.concatenate([key, extra], axis=1)


def forward_kernel(heads, parts, ring, rows, spans, meta_ref, slope_ref, *refs):
    piece_refs = refs[:parts]
    ctx_refs = refs[parts : 2 * parts]
    qkv_ref, out_t_ref, log_ref, kaug_ref, qaug_ref, vt_ref, top_ref, total_ref = refs[2 * parts :]
    length = qkv_ref.shape[0]
    blocks = length // BLOCK
    for e, k, dst in reorder_starts(meta_ref, parts, ring, rows):
        qkv_ref[dst, :] = piece_refs[e][k * rows : (k + 1) * rows, :]
    eye = (
        lax.broadcasted_iota(jnp.int32, (HD, HD), 0) == lax.broadcasted_iota(jnp.int32, (HD, HD), 1)
    ).astype(BF)

    def prepare(b, unused):
        prepare_block(b, heads, qkv_ref, slope_ref, kaug_ref, qaug_ref)
        cols = block_rows(b)
        for h in range(heads):
            at = h * 3 * HD + 2 * HD
            value = qkv_ref[cols, at : at + HD]
            vt_ref[h, :HD, cols] = dot_nt(eye, value).astype(BF)
            row = lax.broadcasted_iota(jnp.int32, (16, BLOCK), 0)
            vt_ref[h, HD:, cols] = jnp.where(row == 0, 1.0, 0.0).astype(BF)
        return unused

    lax.fori_loop(0, blocks, prepare, 0)

    for i in range(blocks):
        rows_i = slice(i * BLOCK, (i + 1) * BLOCK)
        allowed = allowed_block(i, i, meta_ref, spans)
        outs = []
        for h in range(heads):
            query = qaug_ref[h, rows_i, :]
            scores = dot_nt(kaug_ref[h, : (i + 1) * BLOCK, :], query)
            own = jnp.where(allowed, scores[i * BLOCK :], -1e30)
            top = jnp.max(own, axis=0, keepdims=True)
            if i:
                scores = scores[: i * BLOCK]
                top = jnp.maximum(top, jnp.max(scores, axis=0, keepdims=True))
            total = dot(vt_ref[h, :, rows_i], jnp.exp(own - top).astype(BF))
            if i:
                total = total + dot(
                    vt_ref[h, :, : i * BLOCK], jnp.exp(scores - top).astype(BF)
                )
            top_ref[h : h + 1, :] = top
            total_ref[h] = total

        if i < blocks - 1:

            @pl.when(crosses(i, meta_ref, spans))
            def _(i=i, rows_i=rows_i):
                allowed = allowed_block(i, i + 1, meta_ref, spans)
                for h in range(heads):
                    scores = dot_nt(
                        kaug_ref[h, (i + 1) * BLOCK : (i + 2) * BLOCK, :], qaug_ref[h, rows_i, :]
                    )
                    scores = jnp.where(allowed, scores, -1e30)
                    old_top = top_ref[h : h + 1, :]
                    top = jnp.maximum(old_top, jnp.max(scores, axis=0, keepdims=True))
                    weight = jnp.exp(scores - top).astype(BF)
                    total_ref[h] = total_ref[h] * jnp.exp(old_top - top) + dot(
                        vt_ref[h, :, (i + 1) * BLOCK : (i + 2) * BLOCK], weight
                    )
                    top_ref[h : h + 1, :] = top

        for h in range(heads):
            total = total_ref[h]
            amount = total[HD : HD + 1]
            outs.append(total[:HD] / amount)
            log_ref[h : h + 1, rows_i] = top_ref[h : h + 1, :] + jnp.log(amount)
        if heads * HD < 128:
            outs.append(jnp.zeros((128 - heads * HD, BLOCK), F32))
        out_t_ref[:, rows_i] = jnp.concatenate(outs, axis=0)

    for e, k, true_rows in reorder_starts(meta_ref, parts, ring, rows):
        turned = out_t_ref[:, true_rows].T.astype(BF)
        ctx_refs[e][k * rows : (k + 1) * rows, :] = turned[:, : heads * HD]


def backward_kernel(heads, parts, ring, rows, spans, meta_ref, slope_ref, *refs):
    piece_refs = refs[:parts]
    qkv_ref, out_t_ref, log_ref = refs[parts : parts + 3]
    grad_refs = refs[parts + 3 : 2 * parts + 3]
    (
        g_ref,
        kaug_ref,
        qaug_ref,
        kt_ref,
        gq_ref,
        gg_ref,
        delta_ref,
        dqt_ref,
        dkv_ref,
    ) = refs[2 * parts + 3 :]
    length = qkv_ref.shape[0]
    blocks = length // BLOCK
    for e, k, dst in reorder_starts(meta_ref, parts, ring, rows):
        g_ref[dst, :] = piece_refs[e][k * rows : (k + 1) * rows, :]
    eye = (
        lax.broadcasted_iota(jnp.int32, (HD, HD), 0) == lax.broadcasted_iota(jnp.int32, (HD, HD), 1)
    ).astype(BF)

    def prepare(b, unused):
        prepare_block(b, heads, qkv_ref, slope_ref, kaug_ref, qaug_ref)
        cols = block_rows(b)
        blank = jnp.zeros((BLOCK, HD), BF)
        grad_t = g_ref[cols, :].astype(F32)
        if heads * HD < 128:
            grad_t = jnp.concatenate([grad_t, jnp.zeros((BLOCK, 128 - heads * HD), F32)], axis=1)
        product = grad_t.T * out_t_ref[:, cols]
        for h in range(heads):
            at = h * 3 * HD
            kt_ref[h, :, cols] = dot_nt(eye, qkv_ref[cols, at + HD : at + 2 * HD]).astype(BF)
            query = qkv_ref[cols, at : at + HD] * jnp.asarray(0.125, BF)
            gq_ref[h, cols, :] = jnp.concatenate([blank, query], axis=1)
            gg_ref[h, cols, :] = jnp.concatenate([g_ref[cols, h * HD : (h + 1) * HD], blank], axis=1)
            delta_ref[h : h + 1, cols] = jnp.sum(
                product[h * HD : (h + 1) * HD], axis=0, keepdims=True
            )
        return unused

    lax.fori_loop(0, blocks, prepare, 0)

    def part_of(h, keys, queries, allowed):
        at = h * 3 * HD + 2 * HD
        scores = dot_nt(kaug_ref[h, keys, :], qaug_ref[h, queries, :])
        first = jnp.where(allowed, scores[:, :BLOCK], -1e30)
        if scores.shape[1] > BLOCK:
            scores = jnp.concatenate([first, scores[:, BLOCK:]], axis=1)
        else:
            scores = first
        weight = jnp.exp(scores - log_ref[h : h + 1, queries])
        grad_weight = dot_nt(qkv_ref[keys, at : at + HD], g_ref[queries, h * HD : (h + 1) * HD])
        grad_score = (weight * (grad_weight - delta_ref[h : h + 1, queries])).astype(BF)
        dkv = dot(weight.astype(BF), gg_ref[h, queries, :]) + dot(grad_score, gq_ref[h, queries, :])
        return dkv, dot(kt_ref[h, :, keys], grad_score)

    for j in range(blocks):
        keys = slice(j * BLOCK, (j + 1) * BLOCK)
        queries = slice(j * BLOCK, length)
        allowed = allowed_block(j, j, meta_ref, spans)
        for h in range(heads):
            dkv, dq = part_of(h, keys, queries, allowed)
            dkv_ref[h, keys, :] = dkv
            rows_h = slice(h * HD, (h + 1) * HD)
            if j:
                dq = dq + dqt_ref[rows_h, queries]
            dqt_ref[rows_h, queries] = dq

        if j:

            @pl.when(crosses(j - 1, meta_ref, spans))
            def _(j=j, keys=keys):
                queries = slice((j - 1) * BLOCK, j * BLOCK)
                allowed = allowed_block(j - 1, j, meta_ref, spans)
                for h in range(heads):
                    dkv, dq = part_of(h, keys, queries, allowed)
                    dkv_ref[h, keys, :] += dkv
                    dqt_ref[h * HD : (h + 1) * HD, queries] += dq

    for e, k, true_rows in reorder_starts(meta_ref, parts, ring, rows):
        columns = []
        grad_q = (dqt_ref[:, true_rows] * 0.125).T
        for h in range(heads):
            dkv = dkv_ref[h, true_rows, :]
            columns += [grad_q[:, h * HD : (h + 1) * HD], dkv[:, HD:], dkv[:, :HD]]
        grad_refs[e][k * rows : (k + 1) * rows, :] = jnp.concatenate(columns, axis=1).astype(BF)


def specs(count_smem, count_vmem):
    return [pl.BlockSpec(memory_space=pltpu.SMEM)] * count_smem + [
        pl.BlockSpec(memory_space=pltpu.VMEM)
    ] * count_vmem


def attend_forward(pieces, meta, slopes, ring, rows):
    heads = slopes.shape[0]
    parts = len(pieces)
    length = parts * pieces[0].shape[0]
    wide = max(128, heads * HD)
    outs = pl.pallas_call(
        functools.partial(forward_kernel, heads, parts, ring, rows, meta.shape[0] - 2),
        out_shape=tuple(
            [jax.ShapeDtypeStruct((length // parts, heads * HD), BF)] * parts
            + [
                jax.ShapeDtypeStruct((length, heads * 3 * HD), BF),
                jax.ShapeDtypeStruct((wide, length), F32),
                jax.ShapeDtypeStruct((8, length), F32),
            ]
        ),
        in_specs=specs(2, parts),
        out_specs=tuple(specs(0, parts + 3)),
        scratch_shapes=[
            pltpu.VMEM((heads, length, 128), BF),
            pltpu.VMEM((heads, length, 128), BF),
            pltpu.VMEM((heads, HD + 16, length), BF),
            pltpu.VMEM((8, BLOCK), F32),
            pltpu.VMEM((heads, HD + 16, BLOCK), F32),
        ],
        compiler_params=pltpu.CompilerParams(vmem_limit_bytes=VMEM_BYTES),
        cost_estimate=pl.CostEstimate(
            flops=2 * US, bytes_accessed=length * heads * HD * 20, transcendentals=0
        ),
    )(meta, slopes, *pieces)
    return list(outs[:parts]), *outs[parts:]


def attend_backward(pieces, qkv, out_t, logs, meta, slopes, ring, rows):
    heads = slopes.shape[0]
    parts = len(pieces)
    length = qkv.shape[0]
    wide = max(128, heads * HD)
    outs = pl.pallas_call(
        functools.partial(backward_kernel, heads, parts, ring, rows, meta.shape[0] - 2),
        out_shape=tuple([jax.ShapeDtypeStruct((length // parts, heads * 3 * HD), BF)] * parts),
        in_specs=specs(2, parts + 3),
        out_specs=tuple(specs(0, parts)),
        scratch_shapes=[
            pltpu.VMEM((length, heads * HD), BF),
            pltpu.VMEM((heads, length, 128), BF),
            pltpu.VMEM((heads, length, 128), BF),
            pltpu.VMEM((heads, HD, length), BF),
            pltpu.VMEM((heads, length, 128), BF),
            pltpu.VMEM((heads, length, 128), BF),
            pltpu.VMEM((8, length), F32),
            pltpu.VMEM((wide, length), F32),
            pltpu.VMEM((heads, length, 128), F32),
        ],
        compiler_params=pltpu.CompilerParams(vmem_limit_bytes=VMEM_BYTES),
        cost_estimate=pl.CostEstimate(
            flops=2 * US, bytes_accessed=length * heads * HD * 20, transcendentals=0
        ),
    )(meta, slopes, *pieces, qkv, out_t, logs)
    return list(outs)


def take_columns(ref, part, e, width):
    def each(use):
        if width % 128 == 0:
            start = pl.multiple_of((part ^ e) * width, width)
            use(ref.at[:, pl.ds(start, width)])
        else:
            for p in range(SEQ_DEVS):

                @pl.when(part == p)
                def _():
                    use(ref.at[:, pl.ds((p ^ e) * width, width)])

    return each


def column_loop(total, body):
    step = min(256, total)

    def one(i, unused):
        body(pl.ds(pl.multiple_of(i * step, step), step))
        return unused

    lax.fori_loop(0, total // step, one, 0)


def load_weights(w_pieces, w_ref, sems, starts_ref):
    copies = []
    for i, piece in enumerate(w_pieces):
        count = piece.shape[0]
        start = pl.multiple_of(starts_ref[i], min(128, count))
        copy = pltpu.make_async_copy(piece, w_ref.at[pl.ds(start, count), :], sems.at[i])
        copy.start()
        copies.append(copy)
    return copies


def load_shards(w_pieces, w_ref, sems, places_ref):
    copies = []
    for i, piece in enumerate(w_pieces):
        if len(piece.shape) == 3:
            copy = pltpu.make_async_copy(piece, w_ref, sems.at[i])
        else:
            count = piece.shape[0]
            start = pl.multiple_of(places_ref[2 * i + 1], count)
            target = w_ref.at[places_ref[2 * i], pl.ds(start, count), :]
            copy = pltpu.make_async_copy(piece, target, sems.at[i])
        copy.start()
        copies.append(copy)
    return copies


def normed_rows(rows_ref, gain_ref, shift_ref):
    return norm_forward(rows_ref[...].astype(F32), gain_ref[...], shift_ref[...])[0].astype(BF)


def prepare_qkv_kernel(count, starts_ref, *refs):
    h_pieces, refs = refs[:count], refs[count:]
    gain_ref, shift_ref, w_pieces, (w_ref, x_ref, sems) = refs[0], refs[1], refs[2:-3], refs[-3:]
    copies = load_weights(w_pieces, w_ref, sems, starts_ref)
    rows = h_pieces[0].shape[0]
    for k in range(count):
        x_ref[k * rows : (k + 1) * rows, :] = normed_rows(h_pieces[k], gain_ref, shift_ref)
    for copy in copies:
        copy.wait()


def prepare_qkv(h_pieces, gain, shift, w_pieces, starts):
    count, n_w = len(h_pieces), len(w_pieces)
    rows, depth = h_pieces[0].shape
    cols = w_pieces[0].shape[1]
    return pl.pallas_call(
        functools.partial(prepare_qkv_kernel, count),
        out_shape=[pltpu.VMEM((depth, cols), BF), pltpu.VMEM((count * rows, depth), BF)],
        in_specs=specs(1, count + 2) + [pl.BlockSpec(memory_space=pl.ANY)] * n_w,
        out_specs=specs(0, 2),
        scratch_shapes=[pltpu.SemaphoreType.DMA((n_w,))],
        compiler_params=pltpu.CompilerParams(vmem_limit_bytes=SMALL_VMEM_BYTES),
        cost_estimate=pl.CostEstimate(flops=3 * US, bytes_accessed=2**20, transcendentals=0),
    )(starts, *h_pieces, gain, shift, *w_pieces)


def qkv_kernel(meta_ref, first_ref, last_ref, gain_ref, shift_ref, a_ref, b_ref, bias_ref, *refs):
    w_ref, q_refs, (u_ref, x_ref, o_ref) = refs[0], refs[1 : 1 + SEQ_DEVS], refs[1 + SEQ_DEVS :]
    before = first_ref.shape[0]
    x_ref[:before, :] = first_ref[...]
    x_ref[before:, :] = normed_rows(last_ref, gain_ref, shift_ref)
    u_ref[...] = dot_nt(x_ref[...], a_ref[...]).astype(BF)

    def body(cols):
        total = dot(x_ref[...], w_ref[:, cols])
        total = total + FACTOR * dot(u_ref[...], b_ref[:, cols]) + bias_ref[:, cols]
        o_ref[:, cols] = total.astype(BF)

    column_loop(o_ref.shape[1], body)
    for e in range(SEQ_DEVS):

        def store(src, e=e):
            q_refs[e][...] = src[...]

        take_columns(o_ref, meta_ref[0], e, q_refs[e].shape[1])(store)


def qkv_product(first, last, gain, shift, a, b, bias, w, meta):
    count, depth = first.shape[0] + last.shape[0], first.shape[1]
    cols = b.shape[1]
    outs = pl.pallas_call(
        qkv_kernel,
        out_shape=tuple(
            [jax.ShapeDtypeStruct((count, cols // SEQ_DEVS), BF)] * SEQ_DEVS
            + [
                jax.ShapeDtypeStruct((count, a.shape[0]), BF),
                jax.ShapeDtypeStruct((count, depth), BF),
            ]
        ),
        in_specs=specs(1, 8),
        out_specs=tuple(specs(0, SEQ_DEVS + 2)),
        scratch_shapes=[pltpu.VMEM((count, cols), BF)],
        compiler_params=pltpu.CompilerParams(vmem_limit_bytes=SMALL_VMEM_BYTES),
        cost_estimate=pl.CostEstimate(flops=2 * US, bytes_accessed=2**20, transcendentals=0),
    )(meta, first, last, gain, shift, a, b, bias, w)
    return list(outs[:SEQ_DEVS]), outs[SEQ_DEVS], outs[SEQ_DEVS + 1]


def load_kernel(first_ref, second_ref, first_out, second_out, sems):
    shards, half = first_ref.shape[0], first_ref.shape[1]
    depth = second_ref.shape[2]
    chunks = first_out.shape[1] // depth
    copies = []

    def copy(src, dst):
        copies.append(pltpu.make_async_copy(src, dst, sems.at[len(copies)]))

    for i in range(shards):
        copy(first_ref.at[i], first_out.at[pl.ds(2 * i * half, half), :])
        for h in range(chunks):
            copy(
                second_ref.at[i, pl.ds(h * half, half)],
                first_out.at[pl.ds((2 * i + 1) * half, half), pl.ds(h * depth, depth)],
            )
        copy(second_ref.at[i, pl.ds(chunks * half, chunks * depth)], second_out.at[i])
    for each in copies:
        each.start()
    for each in copies:
        each.wait()


def load_to_vmem(first, second):
    shards, half, hidden = first.shape
    chunks = hidden // second.shape[2]
    return pl.pallas_call(
        load_kernel,
        out_shape=[
            pltpu.VMEM((shards * half * 2, hidden), BF),
            pltpu.VMEM((shards, hidden, second.shape[2]), BF),
        ],
        in_specs=[pl.BlockSpec(memory_space=pl.ANY)] * 2,
        out_specs=[pl.BlockSpec(memory_space=pltpu.VMEM)] * 2,
        scratch_shapes=[pltpu.SemaphoreType.DMA((shards * (chunks + 2),))],
        compiler_params=pltpu.CompilerParams(vmem_limit_bytes=2 * 1024 * 1024),
        cost_estimate=pl.CostEstimate(flops=5 * US, bytes_accessed=2**20, transcendentals=0),
    )(*[pltpu.with_memory_space_constraint(w, pltpu.HBM) for w in (first, second)])


def store_rows(refs, cols, total):
    at = 0
    for ref in refs:
        ref[:, cols] = total[at : at + ref.shape[0]]
        at += ref.shape[0]


def out_kernel(ring, n_w, meta_ref, places_ref, *refs):
    c_pieces = refs[:SEQ_DEVS]
    a_ref, b_ref = refs[SEQ_DEVS : SEQ_DEVS + 2]
    w_pieces, refs = refs[SEQ_DEVS + 2 : SEQ_DEVS + 2 + n_w], refs[SEQ_DEVS + 2 + n_w :]
    p_refs = refs[:ring]
    ctx_ref, u_ref, w_ref, sems = refs[ring:]
    copies = load_shards(w_pieces, w_ref, sems, places_ref)
    width = c_pieces[0].shape[1]
    for e in range(SEQ_DEVS):

        def store(dst, e=e):
            dst[...] = c_pieces[e][...]

        take_columns(ctx_ref, meta_ref[0], e, width)(store)
    u_ref[...] = dot_nt(ctx_ref[...], a_ref[...]).astype(BF)
    for copy in copies:
        copy.wait()
    shards, unused, wide = w_ref.shape
    for j in range(shards):
        cols = slice(j * wide, (j + 1) * wide)
        total = dot(ctx_ref[...], w_ref[j]) + FACTOR * dot(u_ref[...], b_ref[:, cols])
        store_rows(p_refs, cols, total.astype(BF))


def paired(pieces):
    return [list(pieces[i : i + 2]) for i in range(0, len(pieces), 2)]


def out_product(c_pieces, a, b, w_pieces, places, meta, ring, shards):
    count, width = c_pieces[0].shape
    rank, depth = b.shape
    n_w = len(w_pieces)
    outs = pl.pallas_call(
        functools.partial(out_kernel, 2 * ring, n_w),
        out_shape=tuple(
            [jax.ShapeDtypeStruct((count // ring // 2, depth), BF)] * (2 * ring)
            + [
                jax.ShapeDtypeStruct((count, width * SEQ_DEVS), BF),
                jax.ShapeDtypeStruct((count, rank), BF),
            ]
        ),
        in_specs=specs(2, SEQ_DEVS + 2) + [pl.BlockSpec(memory_space=pl.ANY)] * n_w,
        out_specs=tuple(specs(0, 2 * ring + 2)),
        scratch_shapes=[
            pltpu.VMEM((shards, width * SEQ_DEVS, depth // shards), BF),
            pltpu.SemaphoreType.DMA((n_w,)),
        ],
        compiler_params=pltpu.CompilerParams(vmem_limit_bytes=VMEM_BYTES),
        cost_estimate=pl.CostEstimate(flops=3 * US, bytes_accessed=2**20, transcendentals=0),
    )(meta, places, *c_pieces, a, b, *w_pieces)
    return paired(outs[: 2 * ring]), outs[2 * ring], outs[2 * ring + 1]


def mlp_kernel(count, add, *refs):
    n2_refs, (gy_ref, a1_ref, b2_ref, b1_ref, a2_ref, bias_ref), refs = (
        refs[:count],
        refs[count : count + 6],
        refs[count + 6 :],
    )
    w1_ref, w2_ref, before, refs = refs[0], refs[1], refs[2 : 2 + add], refs[2 + add :]
    p_refs, m_ref, grads = refs[:count], refs[count], refs[count + 1 : count + 5]
    x_ref, act_ref, slope_ref, gf_ref = refs[count + 5 :]
    shards, hidden, wide = w2_ref.shape
    at = 0
    for ref in n2_refs:
        x_ref[at : at + ref.shape[0], :] = ref[...]
        at += ref.shape[0]
    u3 = dot_nt(x_ref[...], a1_ref[...]).astype(BF)
    gu4 = (FACTOR * dot_nt(gy_ref[...], b2_ref[...])).astype(BF)
    for h in range(0, hidden, wide):
        cols = slice(h, h + wide)
        f = dot(x_ref[...], w1_ref[:, cols])
        f = f + FACTOR * dot(u3, b1_ref[:, cols]) + bias_ref[:, cols]
        act, slope = gelu_and_slope(f)
        act_ref[:, cols] = act.astype(BF)
        slope_ref[:, cols] = slope
    for h in range(0, hidden, wide):
        cols = slice(h, h + wide)
        gact = dot(gu4, a2_ref[:, cols])
        for j in range(shards):
            gact = gact + dot_nt(gy_ref[:, j * wide : (j + 1) * wide], w2_ref[j, cols, :])
        gf_ref[:, cols] = (gact * slope_ref[:, cols]).astype(BF)
    gu3 = (FACTOR * dot_nt(gf_ref[...], b1_ref[...])).astype(BF)
    for j in range(shards):
        cols = slice(j * wide, (j + 1) * wide)
        total = dot_nt(gf_ref[...], w1_ref[cols, :]) + dot(gu3, a1_ref[:, cols])
        store_rows(p_refs, cols, total.astype(BF))
    u4 = dot_nt(act_ref[...], a2_ref[...]).astype(BF)
    for j in range(shards):
        cols = slice(j * wide, (j + 1) * wide)
        total = dot(act_ref[...], w2_ref[j]) + FACTOR * dot(u4, b2_ref[:, cols])
        m_ref[:, cols] = total.astype(BF)
    products = [
        FACTOR * dot_tn(u3, gf_ref[...]),
        dot_tn(gu4, act_ref[...]),
        dot_tn(gu3, x_ref[...]),
        FACTOR * dot_tn(u4, gy_ref[...]),
    ]
    for i, product in enumerate(products):
        grads[i][...] = product + before[i][...] if add else product


def mlp_both_ways(n2_pieces, gy, a1, b1, a2, b2, bias, weights, before):
    count = len(n2_pieces)
    total, depth = gy.shape
    rank, hidden = b1.shape
    outs = pl.pallas_call(
        functools.partial(mlp_kernel, count, len(before)),
        out_shape=(
            [jax.ShapeDtypeStruct(piece.shape, BF) for piece in n2_pieces]
            + [jax.ShapeDtypeStruct((total, depth), BF)]
            + [jax.ShapeDtypeStruct((rank, hidden), F32)] * 2
            + [jax.ShapeDtypeStruct((rank, depth), F32)] * 2
        ),
        in_specs=specs(0, count + 8 + len(before)),
        out_specs=specs(0, count + 5),
        scratch_shapes=[
            pltpu.VMEM((total, depth), BF),
            pltpu.VMEM((total, hidden), BF),
            pltpu.VMEM((total, hidden), F32),
            pltpu.VMEM((total, hidden), BF),
        ],
        compiler_params=pltpu.CompilerParams(vmem_limit_bytes=SMALL_VMEM_BYTES),
        cost_estimate=pl.CostEstimate(
            flops=10 * US, bytes_accessed=4 * depth * hidden, transcendentals=0
        ),
    )(*n2_pieces, gy, a1, b2, b1, a2, bias, *weights, *before)
    return list(outs[:count]), outs[count], list(outs[count + 1 :])


def pack_into(full, own, ring, groups, meta_ref, full_ref, cols_ref):
    part, spot = meta_ref[0], meta_ref[1]
    at = 0
    for ref in full:
        width = ref.shape[1] // (ring * SEQ_DEVS * groups)
        for g in range(groups):
            for p in range(SEQ_DEVS):
                for z in range(ring):
                    k = z - spot
                    k = jnp.where(k < 0, k + ring, k)
                    column = ((g * SEQ_DEVS + p) * ring + z) * width
                    full_ref[k, part ^ p, g, :, at : at + width] = ref[
                        :, column : column + width
                    ].astype(BF)
        at += width
    at = 0
    for ref in own:
        width = ref.shape[1] // (SEQ_DEVS * groups)
        for p in range(SEQ_DEVS):
            for r in range(groups):
                column = (p * groups + r) * width
                cols_ref[part ^ p, r, :, at : at + width] = ref[:, column : column + width].astype(
                    BF
                )
        at += width


def pack_shapes(full_cols, own_cols, rank, ring, groups):
    full_widths = [c // (ring * SEQ_DEVS * groups) for c in full_cols]
    own_widths = [c // (SEQ_DEVS * groups) for c in own_cols]
    shapes = [
        jax.ShapeDtypeStruct((ring, SEQ_DEVS, groups, rank, sum(full_widths)), BF),
        jax.ShapeDtypeStruct((SEQ_DEVS, groups, rank, sum(own_widths)), BF),
    ]
    return shapes, full_widths, own_widths


def gctx_kernel(n_g, n_w, meta_ref, places_ref, *refs):
    g_pieces, refs = refs[:n_g], refs[n_g:]
    a_ref, b_ref, ctx_ref, u2_ref = refs[:4]
    w_pieces, refs = refs[4 : 4 + n_w], refs[4 + n_w :]
    c_refs = refs[:SEQ_DEVS]
    gbo_ref, gao_ref, g_ref, o_ref, w_ref, sems = refs[SEQ_DEVS:]
    copies = load_shards(w_pieces, w_ref, sems, places_ref)
    rows = g_pieces[0].shape[0]
    for k in range(n_g):
        g_ref[k * rows : (k + 1) * rows, :] = g_pieces[k][...]
    gu2 = (FACTOR * dot_nt(g_ref[...], b_ref[...])).astype(BF)
    shards, unused, wide = w_ref.shape
    total = dot(gu2, a_ref[...])
    gbo_ref[...] = FACTOR * dot_tn(u2_ref[...], g_ref[...])
    gao_ref[...] = dot_tn(gu2, ctx_ref[...])
    for copy in copies:
        copy.wait()
    for j in range(shards):
        total = total + dot_nt(g_ref[:, j * wide : (j + 1) * wide], w_ref[j])
    o_ref[...] = total.astype(BF)
    for e in range(SEQ_DEVS):

        def store(src, e=e):
            c_refs[e][...] = src[...]

        take_columns(o_ref, meta_ref[0], e, c_refs[e].shape[1])(store)


def gctx_product(g_pieces, a, b, w_pieces, places, ctx, u2, meta, shards):
    n_g, n_w = len(g_pieces), len(w_pieces)
    depth = g_pieces[0].shape[1]
    count, cols = ctx.shape
    rank = a.shape[0]
    outs = pl.pallas_call(
        functools.partial(gctx_kernel, n_g, n_w),
        out_shape=tuple(
            [jax.ShapeDtypeStruct((count, cols // SEQ_DEVS), BF)] * SEQ_DEVS
            + [jax.ShapeDtypeStruct((rank, depth), F32), jax.ShapeDtypeStruct((rank, cols), F32)]
        ),
        in_specs=specs(2, n_g + 4) + [pl.BlockSpec(memory_space=pl.ANY)] * n_w,
        out_specs=tuple(specs(0, SEQ_DEVS + 2)),
        scratch_shapes=[
            pltpu.VMEM((count, depth), BF),
            pltpu.VMEM((count, cols), BF),
            pltpu.VMEM((shards, cols, depth // shards), BF),
            pltpu.SemaphoreType.DMA((n_w,)),
        ],
        compiler_params=pltpu.CompilerParams(vmem_limit_bytes=VMEM_BYTES),
        cost_estimate=pl.CostEstimate(flops=3 * US, bytes_accessed=2**20, transcendentals=0),
    )(meta, places, *g_pieces, a, b, ctx, u2, *w_pieces)
    return list(outs[:SEQ_DEVS]), outs[SEQ_DEVS], outs[SEQ_DEVS + 1]


def joined_kernel(ring, groups, n_w, meta_ref, starts_ref, *refs):
    q_pieces, refs = refs[:SEQ_DEVS], refs[SEQ_DEVS:]
    x_ref, b_ref, u1_ref, full, own = *refs[:3], refs[3:6], refs[6:9]
    w_pieces, refs = refs[9 : 9 + n_w], refs[9 + n_w :]
    q_ref, gu_ref, w_ref, full_ref, cols_ref, gb_ref, ga_ref, sems = refs
    copies = load_weights(w_pieces, w_ref, sems, starts_ref)
    for e in range(SEQ_DEVS):

        def store(dst, e=e):
            dst[...] = q_pieces[e][...]

        take_columns(q_ref, meta_ref[0], e, q_pieces[e].shape[1])(store)
    gu1 = (FACTOR * dot_nt(q_ref[...], b_ref[...])).astype(BF)
    gu_ref[...] = gu1
    gb_ref[...] = FACTOR * dot_tn(u1_ref[...], q_ref[...])
    ga_ref[...] = dot_tn(gu1, x_ref[...])
    pack_into(
        [ga_ref, *full], [gb_ref, *own], ring, groups, meta_ref, full_ref, cols_ref
    )
    for copy in copies:
        copy.wait()


def joined_gradients(q_pieces, n1, b, u1, full, own, w_pieces, starts, meta, ring, groups):
    n_w = len(w_pieces)
    count, depth = n1.shape
    rank, cols = b.shape
    shapes, full_widths, own_widths = pack_shapes(
        [depth] + [g.shape[1] for g in full],
        [cols] + [g.shape[1] for g in own],
        rank,
        ring,
        groups,
    )
    near = [pltpu.VMEM((count, cols), BF), pltpu.VMEM((count, rank), BF)]
    near.append(pltpu.VMEM((depth, cols), BF))
    outs = pl.pallas_call(
        functools.partial(joined_kernel, ring, groups, n_w),
        out_shape=near + shapes,
        in_specs=specs(2, SEQ_DEVS + 9) + [pl.BlockSpec(memory_space=pl.ANY)] * n_w,
        out_specs=specs(0, 5),
        scratch_shapes=[
            pltpu.VMEM((rank, cols), F32),
            pltpu.VMEM((rank, depth), F32),
            pltpu.SemaphoreType.DMA((n_w,)),
        ],
        compiler_params=pltpu.CompilerParams(vmem_limit_bytes=SMALL_VMEM_BYTES),
        cost_estimate=pl.CostEstimate(flops=5 * US, bytes_accessed=2**20, transcendentals=0),
    )(meta, starts, *q_pieces, n1, b, u1, *full, *own, *w_pieces)
    stages = functools.partial(
        reduce_stages, full_widths=full_widths, own_widths=own_widths, groups=groups
    )
    return outs[:3], Side(list(outs[3:]), stages)


def gn1_kernel(q_ref, gu_ref, w_ref, a_ref, *p_refs):
    def body(cols):
        total = dot_nt(q_ref[...], w_ref[cols, :]) + dot(gu_ref[...], a_ref[:, cols])
        store_rows(p_refs, cols, total.astype(BF))

    column_loop(w_ref.shape[0], body)


def gn1_product(gqkv, gu1, w, a, ring):
    count, depth = gqkv.shape[0], a.shape[1]
    return paired(
        pl.pallas_call(
            gn1_kernel,
            out_shape=[jax.ShapeDtypeStruct((count // ring // 2, depth), BF)] * (2 * ring),
            in_specs=specs(0, 4),
            out_specs=specs(0, 2 * ring),
            compiler_params=pltpu.CompilerParams(vmem_limit_bytes=SMALL_VMEM_BYTES),
            cost_estimate=pl.CostEstimate(flops=5 * US, bytes_accessed=2**20, transcendentals=0),
        )(gqkv, gu1, w, a)
    )


def reduce_stages(packed, packed_own, full_widths, own_widths, groups):
    ring, n = lax.axis_size("tensor"), lax.axis_size("dp")
    spot, data = lax.axis_index("tensor"), lax.axis_index("dp")
    group = data // SEQ_DEVS
    wide = sum(full_widths)
    landed = yield [
        lax.ppermute(packed[k], "tensor", [(i, (i + k) % ring) for i in range(ring)])
        for k in range(1, ring)
    ]
    total = sum([x.astype(F32) for x in landed], packed[0].astype(F32)).astype(BF)
    total = jnp.concatenate([total, packed_own], axis=3)
    landed = yield [exchange(total[e], e) for e in range(1, SEQ_DEVS)]
    own = sum([x.astype(F32) for x in landed], total[0].astype(F32)).astype(BF)

    def block(k):
        return lax.dynamic_index_in_dim(own, (group + k) % groups, 0, keepdims=False)

    flying = []
    for k in range(1, groups):
        pairs = [(i, (i + k * SEQ_DEVS) % n) for i in range(n)]
        flying.append(lax.ppermute(block(k)[:, :wide], "dp", pairs))
    for k in range(groups):
        pairs = []
        for i in range(n):
            for z in range(ring):
                r = (i // SEQ_DEVS + k) % groups
                pairs.append((i * ring + z, z * n + (i % SEQ_DEVS) * groups + r))
        flying.append(lax.ppermute(block(k)[:, wide:], ("dp", "tensor"), pairs))
    landed = yield flying
    full = [block(0)[:, :wide]] + list(landed[: groups - 1])
    full = [(piece, (group - k) % groups) for k, piece in enumerate(full)]
    mine = (data * ring + spot) % groups
    cols = [(piece, (mine - k) % groups) for k, piece in enumerate(landed[groups - 1 :])]
    return (full, full_widths), (cols, own_widths)


def place(pieces, widths, seq_adapter):
    slots = jnp.arange(ADAPTERS, dtype=jnp.int32)
    whole = 0.0
    for piece, sequence in pieces:
        slot = lax.dynamic_index_in_dim(seq_adapter, sequence, 0, keepdims=False)
        whole = whole + jnp.where((slots == slot)[:, None, None], piece[None].astype(F32), 0.0)
    outs, at = [], 0
    for width in widths:
        outs.append(whole[:, :, at : at + width])
        at += width
    return outs


def gather_first(shard, rows_in, data, small):
    n, count = lax.axis_size("dp"), shard.shape[0]
    if n != 8 or lax.axis_size("tensor") != 4:
        whole = lax.all_gather(shard, "dp", axis=0, tiled=True)
        return [whole], [0 * data], ring_gather(rows_in, "tensor"), small
    half = count // 2
    by_x, by_y, by_c = exchange(shard, 2), exchange(shard, 4), exchange(shard, 1)
    ring = [rows_in, shift_one(rows_in, "tensor")]
    by_x, by_y, by_c, ring[1], *small = lax.optimization_barrier(
        (by_x, by_y, by_c, ring[1]) + small
    )
    corner_a, corner_b = exchange(by_x[:half], 4), exchange(by_y[half:], 2)
    by_xc, by_yc = exchange(by_x, 1), exchange(by_y, 1)
    ring.append(shift_one(ring[1], "tensor"))
    corner_a, corner_b, by_xc, by_yc, ring[2], small[0] = lax.optimization_barrier(
        (corner_a, corner_b, by_xc, by_yc, ring[2], small[0])
    )
    far_a, far_b = exchange(corner_a, 1), exchange(corner_b, 1)
    ring.append(shift_one(ring[2], "tensor"))
    pieces = [shard, by_c, by_x, by_xc, by_y, by_yc, corner_a, far_a, corner_b, far_b]
    starts = [(data ^ e) * count for e in range(8)]
    starts += [(data ^ e) * count + half for e in (6, 7)]
    return pieces, starts, ring, small


def gather_shards(shard, data):
    stages = shard_stages(data)
    next(stages)
    return stages


def shard_stages(data):
    n = lax.axis_size("dp")
    shard = yield None
    if n != 8:
        landed = yield [lax.all_gather(shard, "dp", axis=0, tiled=False)]
        landed = yield landed
        landed = yield landed
        yield landed, jnp.zeros((2,), jnp.int32)
        return
    half = shard.shape[0] // 2
    by_x, by_y, by_c = yield [exchange(shard, 2), exchange(shard, 4), exchange(shard, 1)]
    sent = [exchange(by_x[:half], 4), exchange(by_y[half:], 2), exchange(by_x, 1), exchange(by_y, 1)]
    corner_a, corner_b, by_xc, by_yc = yield sent
    far_a, far_b = yield [exchange(corner_a, 1), exchange(corner_b, 1)]
    pieces = [shard, by_c, by_x, by_xc, by_y, by_yc, corner_a, far_a, corner_b, far_b]
    places = [(data ^ e, 0 * data) for e in range(8)] + [(data ^ e, 0 * data + half) for e in (6, 7)]
    yield pieces, jnp.stack([p for place in places for p in place]).astype(jnp.int32)


def swap_heads(pieces, beside=()):
    across, far, near = exchange(pieces[2], 2), exchange(pieces[3], 2), exchange(pieces[1], 1)
    across, far, near, beside = lax.optimization_barrier((across, far, near, beside))
    return [pieces[0], near, across, exchange(far, 1)], beside


def local(
    hidden_in,
    ln1_gain,
    ln1_bias,
    qkv_weight,
    joined_bias,
    out_weight,
    output_bias,
    ln2_gain,
    ln2_bias,
    fc1_weight,
    first_feed_bias,
    fc2_weight,
    second_feed_bias,
    qkv_down,
    qkv_up,
    out_down,
    out_up,
    fc1_down,
    fc1_up,
    fc2_down,
    fc2_up,
    seq_adapter,
    span_starts,
    cotangent,
):
    spot = lax.axis_index("tensor")
    data = lax.axis_index("dp")
    ring = lax.axis_size("tensor")
    groups = lax.axis_size("dp") // SEQ_DEVS
    group, part = data // SEQ_DEVS, data % SEQ_DEVS
    rows = hidden_in.shape[0]
    slot = lax.dynamic_index_in_dim(seq_adapter, group, 0, keepdims=False)
    starts = lax.dynamic_index_in_dim(span_starts, group, 0, keepdims=False)
    qkv_cols, ctx_cols, hidden_cols = qkv_weight.shape[1], out_weight.shape[0], fc1_weight.shape[1]
    heads = qkv_cols // (3 * HD) // SEQ_DEVS
    meta = jnp.concatenate([jnp.stack([part, spot]), starts]).astype(jnp.int32)
    first_head = (spot * SEQ_DEVS + part) * heads
    slopes = jnp.exp2(
        -8.0 * ((first_head + jnp.arange(heads, dtype=jnp.int32)).astype(F32) + 1.0) / H
    )

    def pick(stack):
        return lax.dynamic_index_in_dim(stack, slot, 0, keepdims=False)

    def own_cols(matrix, count):
        return lax.dynamic_slice_in_dim(matrix, spot * count, count, 1)

    a_q, b_q = pick(qkv_down), own_cols(pick(qkv_up), qkv_cols)
    a_o, b_o = own_cols(pick(out_down), ctx_cols), pick(out_up)
    a_1, b_1 = pick(fc1_down), own_cols(pick(fc1_up), hidden_cols)
    a_2, b_2 = own_cols(pick(fc2_down), hidden_cols), pick(fc2_up)

    n = lax.axis_size("dp")
    shard = fc1_weight.shape[0]
    chunks = hidden_cols // shard
    upper, lower = halves(fc1_weight)
    lower = jnp.transpose(lower.reshape(shard // 2, chunks, shard), (1, 0, 2)).reshape(-1, shard)
    fc_rest = jnp.concatenate([lower, fc2_weight], axis=0)
    w_qkv, w_starts, h_pieces, (upper, *small) = gather_first(
        qkv_weight, hidden_in, data, (upper, fc_rest, a_q, b_q, a_o, b_o, a_1, b_1, a_2, b_2, slopes)
    )
    fc_rest, a_q, b_q, a_o, b_o, a_1, b_1, a_2, b_2, slopes = small
    w_fc_first = lax.all_gather(upper, "dp", axis=0, tiled=False)
    w_starts = jnp.stack(w_starts).astype(jnp.int32)
    out_stages = gather_shards(out_weight, data)

    x = halves(hidden_in.astype(F32))
    w_qkv_near, n1_first = prepare_qkv(
        h_pieces[:-1], ln1_gain[None], ln1_bias[None], w_qkv, w_starts
    )
    h_pieces[-1], cotangent_held, held_out, w_qkv_near = lax.optimization_barrier(
        (h_pieces[-1], cotangent, out_weight, w_qkv_near)
    )
    gy = [cotangent, shift_one(cotangent_held, "tensor")]
    flying = out_stages.send(held_out)
    pieces, u1, n1 = qkv_product(
        n1_first,
        h_pieces[-1],
        ln1_gain[None],
        ln1_bias[None],
        a_q,
        b_q,
        joined_bias[None],
        w_qkv_near,
        meta,
    )
    pieces, flying = lax.optimization_barrier((pieces, flying))
    pieces, (gy[1], fc_rest) = swap_heads(pieces, (gy[1], fc_rest))
    w_fc_second = lax.all_gather(fc_rest, "dp", axis=0, tiled=False)
    gy += ring_gather(gy[-1], "tensor", ring - 3)[1:]
    pieces, flying = lax.optimization_barrier((pieces, flying))
    flying = out_stages.send(flying)
    pieces, qkv_true, out_t, logs = attend_forward(pieces, meta, slopes, ring, rows)
    pieces, gy, flying = lax.optimization_barrier((pieces, gy, flying))
    pieces, (flying, following) = swap_heads(
        pieces, (out_stages.send(flying), shift_one(gy[-1], "tensor"))
    )
    gy.append(following)
    w_out, places = out_stages.send(flying)
    part_out, ctx, u2 = out_product(pieces, a_o, b_o, w_out, places, meta, ring, n)
    weights = [w_fc_first, w_fc_second]

    def load_beside(hop, moved):
        if hop == ring - 3:
            moved, weights[:] = lax.optimization_barrier((moved, weights))
        if hop == ring - 2:
            moved, weights[:] = lax.optimization_barrier((moved, load_to_vmem(*weights)))
        return moved

    summed = ring_scatter(part_out, "tensor", load_beside)
    mid = [rows_in + (term + output_bias) for rows_in, term in zip(x, summed)]

    normed2 = [norm_forward(m, ln2_gain, ln2_bias) for m in mid]
    block = [normed.astype(BF) for normed, unused, unused in normed2]
    part_in2, part_mlp, fc_grads = [], [], []
    for k in range(ring):
        following = shift_all(block if k < ring - 1 else part_in2[1], "tensor")
        grad_pieces, out_piece, fc_grads = mlp_both_ways(
            block, gy[k], a_1, b_1, a_2, b_2, first_feed_bias[None], weights, fc_grads
        )
        part_in2.append(grad_pieces)
        part_mlp.append(out_piece)
        block, part_in2[1:], fc_grads = lax.optimization_barrier(
            (following, part_in2[1:], fc_grads)
        )
    g_b1, g_a2, g_a1, g_b2 = fc_grads
    grad_n2 = ring_scatter(part_in2, "tensor", moved=block)
    grad_mid = [
        top.astype(F32) + norm_backward(grad, unit, inverse, ln2_gain)
        for top, grad, (unused, unit, inverse) in zip(halves(cotangent), grad_n2, normed2)
    ]
    gm = [[g.astype(BF) for g in grad_mid]]
    for k in range(ring):
        if k < ring - 1:
            gm.append(shift_all(gm[-1], "tensor"))
    gm = [half for pair in gm for half in pair]

    mlp_total, gm = lax.optimization_barrier((part_mlp[1], gm))
    mlp_total = shift_one(mlp_total, "tensor")
    pieces, g_bo, g_ao = gctx_product(gm, a_o, b_o, w_out, places, ctx, u2, meta, n)
    pieces, mlp_total = swap_heads(pieces, mlp_total)
    (mlp_total,) = add_terms([mlp_total], part_mlp[2:3], BF)
    mlp_total = shift_one(mlp_total, "tensor")
    pieces = attend_backward(pieces, qkv_true, out_t, logs, meta, slopes, ring, rows)
    pieces, mlp_total = lax.optimization_barrier((pieces, mlp_total))
    (mlp_total,) = add_terms([mlp_total], (part_mlp[3:] + part_mlp[:1])[:1], BF)
    pieces, mlp_total = swap_heads(pieces, shift_one(mlp_total, "tensor"))
    for terms in (part_mlp[3:] + part_mlp[:1])[1:]:
        (mlp_total,) = add_terms([mlp_total], [terms], F32)
        if terms is not part_mlp[0]:
            mlp_total = shift_one(mlp_total.astype(BF), "tensor")
    (gqkv, gu1, w_qkv_near), late = joined_gradients(
        pieces,
        n1,
        b_q,
        u1,
        [g_bo, g_a1, g_b2],
        [g_ao, g_b1, g_a2],
        w_qkv,
        w_starts,
        meta,
        ring,
        groups,
    )
    late.step(())
    part_in1 = gn1_product(gqkv, gu1, w_qkv_near, a_q, ring)
    part_in1 = late.step(part_in1)

    def reduce_beside(hop, moved):
        late.step(moved[0])
        return moved

    grad_n1 = ring_scatter(part_in1, "tensor", reduce_beside)
    while late.result is None:
        late.step(())
    layer_output = jnp.concatenate(
        [(m + (t + second_feed_bias)).astype(BF) for m, t in zip(mid, halves(mlp_total))], axis=0
    )
    normed1 = [norm_forward(rows_in, ln1_gain, ln1_bias) for rows_in in x]
    hidden_grad = jnp.concatenate(
        [
            g + norm_backward(grad, unit, inverse, ln1_gain)
            for g, grad, (unused, unit, inverse) in zip(grad_mid, grad_n1, normed1)
        ],
        axis=0,
    )

    g_aq, g_bo, g_a1, g_b2 = place(*late.result[0], seq_adapter)
    g_bq, g_ao, g_b1, g_a2 = place(*late.result[1], seq_adapter)
    return (layer_output, hidden_grad, g_aq, g_bq, g_ao, g_bo, g_a1, g_b1, g_a2, g_b2)


def solution(mesh):
    rows, cols = P(("dp", "tensor"), None), P(None, None, ("dp", "tensor"))
    placed = (
        rows,
        P(),
        P(),
        P("dp", "tensor"),
        P("tensor"),
        P("tensor", "dp"),
        P(),
        P(),
        P(),
        P("dp", "tensor"),
        P("tensor"),
        P("tensor", "dp"),
    ) + (P(),) * 11 + (rows,)
    return jax.shard_map(
        local,
        mesh=mesh,
        in_specs=placed,
        out_specs=(rows, rows) + (cols,) * 8,
        check_vma=False,
    )
```

```python
import functools

import jax
import jax.numpy as jnp
from jax import lax
from jax.experimental import pallas as pl
from jax.experimental.pallas import tpu as pltpu
from jax.sharding import PartitionSpec as P

H = 32
HD = 64
ADAPTERS = 8
SEQ_DEVS = 4
PIC = 256
EPS = 1e-05
FACTOR = 0.5
BF = jnp.bfloat16
F32 = jnp.float32
BLOCK = 256
VMEM_BYTES = 56 * 1024 * 1024
SMALL_VMEM_BYTES = 28 * 1024 * 1024
US = 10**9


def dot(a, b):
    return jnp.dot(a, b, preferred_element_type=F32)


def dot_nt(a, b):
    return lax.dot_general(a, b, (((1,), (1,)), ((), ())), preferred_element_type=F32)


def dot_tn(a, b):
    return lax.dot_general(a, b, (((0,), (0,)), ((), ())), preferred_element_type=F32)


def hold(value, *until):
    return lax.optimization_barrier((value,) + until)[0]


def gelu_and_slope(f):
    phi = 0.5 * (1.0 + lax.erf(f * (0.5**0.5)))
    density = jnp.exp(-0.5 * f * f) * (0.5 / jnp.pi) ** 0.5
    return f * phi, phi + f * density


def norm_forward(values, gain, shift):
    centred = values - jnp.mean(values, axis=-1, keepdims=True)
    inverse = lax.rsqrt(jnp.mean(centred * centred, axis=-1, keepdims=True) + EPS)
    unit = centred * inverse
    return unit * gain + shift, unit, inverse


def norm_backward(upstream, unit, inverse, gain):
    scaled = upstream * gain
    return inverse * (
        scaled
        - jnp.mean(scaled, axis=-1, keepdims=True)
        - unit * jnp.mean(scaled * unit, axis=-1, keepdims=True)
    )


def shift_one(array, axis):
    n = lax.axis_size(axis)
    return lax.ppermute(array, axis, [(i, (i + 1) % n) for i in range(n)])


def ring_gather(array, axis, hops=None):
    pieces = [array]
    for _ in range(lax.axis_size(axis) - 1 if hops is None else hops):
        pieces.append(shift_one(pieces[-1], axis))
    return pieces


def halves(array):
    middle = array.shape[0] // 2
    return [array[:middle], array[middle:]]


def shift_all(arrays, axis):
    return [shift_one(a, axis) for a in arrays]


class Side:
    def __init__(self, operands, stages):
        self.operands, self.make, self.stages = operands, stages, None
        self.flying, self.result = (), None

    def step(self, beside):
        if self.result is not None:
            return beside
        if self.stages is None:
            beside, self.operands = lax.optimization_barrier((beside, self.operands))
            self.stages = self.make(*self.operands)
            self.flying = next(self.stages)
            return beside
        beside, landed = lax.optimization_barrier((beside, self.flying))
        try:
            self.flying = self.stages.send(landed)
        except StopIteration as stop:
            self.result = stop.value
        return beside


def add_terms(moved, terms, dtype):
    return [(m.astype(F32) + t.astype(F32)).astype(dtype) for m, t in zip(moved, terms)]


def ring_scatter(pieces, axis, beside=None, moved=None):
    following = pieces[2:] + pieces[:1]
    total = None if moved is not None else pieces[1]
    for i, terms in enumerate(following):
        if total is not None:
            moved = shift_all(total, axis)
        if beside is not None and total is not None:
            moved = beside(i, moved)
        total = add_terms(moved, terms, F32 if i == len(following) - 1 else BF)
    return total


def exchange(array, distance):
    n = lax.axis_size("dp")
    return lax.ppermute(array, "dp", [(i, i ^ distance) for i in range(n)])


def span_of(positions, meta_ref, spans, outside):
    label = jnp.full(positions.shape, outside, jnp.int32)
    for j in range(spans):
        start = meta_ref[2 + j]
        label = jnp.where((positions >= start) & (positions < start + PIC), j, label)
    return label


def allowed_block(i, j, meta_ref, spans):
    key_pos = j * BLOCK + lax.broadcasted_iota(jnp.int32, (BLOCK, BLOCK), 0)
    row_pos = i * BLOCK + lax.broadcasted_iota(jnp.int32, (BLOCK, BLOCK), 1)
    key_label = span_of(key_pos, meta_ref, spans, -1)
    row_label = span_of(row_pos, meta_ref, spans, -2)
    return (key_pos <= row_pos) | (key_label == row_label)


def crosses(i, meta_ref, spans):
    edge = (i + 1) * BLOCK
    found = jnp.bool_(False)
    for j in range(spans):
        start = meta_ref[2 + j]
        found = found | ((start < edge) & (edge < start + PIC))
    return found


def block_rows(i):
    return pl.ds(pl.multiple_of(i * BLOCK, BLOCK), BLOCK)


def together(ring):
    return [list(range(ring))]


def leaving(ring):
    return [[1], list(range(2, ring)) + [0]]


def true_blocks(meta_ref, parts, ring, rows, groups):
    part, spot = meta_ref[0], meta_ref[1]
    for g, group in enumerate(groups):
        for at, k in enumerate(group):
            for e in range(parts):
                back = spot - k
                back = jnp.where(back < 0, back + ring, back)
                start = pl.multiple_of(((part ^ e) * ring + back) * rows, rows)
                yield g * parts + e, slice(at * rows, (at + 1) * rows), pl.ds(start, rows)


def prepare_block(b, heads, qkv_ref, slope_ref, kaug_ref, qaug_ref):
    rows = block_rows(b)
    lane = lax.broadcasted_iota(jnp.int32, (BLOCK, HD), 1)
    pos = b * BLOCK + lax.broadcasted_iota(jnp.int32, (BLOCK, HD), 0)
    ones = jnp.where(lane < 3, 1.0, 0.0).astype(BF)
    for h in range(heads):
        at = h * 3 * HD
        query = qkv_ref[rows, at : at + HD] * jnp.asarray(0.125, BF)
        key = qkv_ref[rows, at + HD : at + 2 * HD]
        offset = pos.astype(F32) * (slope_ref[h] * 0.125)
        high = offset.astype(BF).astype(F32)
        middle = (offset - high).astype(BF).astype(F32)
        low = offset - high - middle
        extra = jnp.where(
            lane == 0, high, jnp.where(lane == 1, middle, jnp.where(lane == 2, low, 0.0))
        ).astype(BF)
        qaug_ref[h, rows, :] = jnp.concatenate([query, ones], axis=1)
        kaug_ref[h, rows, :] = jnp.concatenate([key, extra], axis=1)


def forward_kernel(heads, parts, ring, rows, spans, meta_ref, slope_ref, *refs):
    piece_refs = refs[:parts]
    ctx_refs = refs[parts : 2 * parts]
    qkv_ref, out_t_ref, log_ref, kaug_ref, qaug_ref, vt_ref, top_ref, total_ref = refs[2 * parts :]
    length = qkv_ref.shape[0]
    blocks = length // BLOCK
    for i, block, dst in true_blocks(meta_ref, parts, ring, rows, together(ring)):
        qkv_ref[dst, :] = piece_refs[i][block, :]
    eye = (
        lax.broadcasted_iota(jnp.int32, (HD, HD), 0) == lax.broadcasted_iota(jnp.int32, (HD, HD), 1)
    ).astype(BF)

    def prepare(b, unused):
        prepare_block(b, heads, qkv_ref, slope_ref, kaug_ref, qaug_ref)
        cols = block_rows(b)
        for h in range(heads):
            at = h * 3 * HD + 2 * HD
            value = qkv_ref[cols, at : at + HD]
            vt_ref[h, :HD, cols] = dot_nt(eye, value).astype(BF)
            row = lax.broadcasted_iota(jnp.int32, (16, BLOCK), 0)
            vt_ref[h, HD:, cols] = jnp.where(row == 0, 1.0, 0.0).astype(BF)
        return unused

    lax.fori_loop(0, blocks, prepare, 0)

    for i in range(blocks):
        rows_i = slice(i * BLOCK, (i + 1) * BLOCK)
        allowed = allowed_block(i, i, meta_ref, spans)
        outs = []
        for h in range(heads):
            query = qaug_ref[h, rows_i, :]
            scores = dot_nt(kaug_ref[h, : (i + 1) * BLOCK, :], query)
            own = jnp.where(allowed, scores[i * BLOCK :], -1e30)
            top = jnp.max(own, axis=0, keepdims=True)
            if i:
                scores = scores[: i * BLOCK]
                top = jnp.maximum(top, jnp.max(scores, axis=0, keepdims=True))
            total = dot(vt_ref[h, :, rows_i], jnp.exp(own - top).astype(BF))
            if i:
                total = total + dot(
                    vt_ref[h, :, : i * BLOCK], jnp.exp(scores - top).astype(BF)
                )
            top_ref[h : h + 1, :] = top
            total_ref[h] = total

        if i < blocks - 1:

            @pl.when(crosses(i, meta_ref, spans))
            def _(i=i, rows_i=rows_i):
                allowed = allowed_block(i, i + 1, meta_ref, spans)
                for h in range(heads):
                    scores = dot_nt(
                        kaug_ref[h, (i + 1) * BLOCK : (i + 2) * BLOCK, :], qaug_ref[h, rows_i, :]
                    )
                    scores = jnp.where(allowed, scores, -1e30)
                    old_top = top_ref[h : h + 1, :]
                    top = jnp.maximum(old_top, jnp.max(scores, axis=0, keepdims=True))
                    weight = jnp.exp(scores - top).astype(BF)
                    total_ref[h] = total_ref[h] * jnp.exp(old_top - top) + dot(
                        vt_ref[h, :, (i + 1) * BLOCK : (i + 2) * BLOCK], weight
                    )
                    top_ref[h : h + 1, :] = top

        for h in range(heads):
            total = total_ref[h]
            amount = total[HD : HD + 1]
            outs.append(total[:HD] / amount)
            log_ref[h : h + 1, rows_i] = top_ref[h : h + 1, :] + jnp.log(amount)
        if heads * HD < 128:
            outs.append(jnp.zeros((128 - heads * HD, BLOCK), F32))
        out_t_ref[:, rows_i] = jnp.concatenate(outs, axis=0)

    for i, block, true_rows in true_blocks(meta_ref, parts, ring, rows, together(ring)):
        turned = out_t_ref[:, true_rows].T.astype(BF)
        ctx_refs[i][block, :] = turned[:, : heads * HD]


def backward_kernel(heads, parts, ring, rows, spans, meta_ref, slope_ref, *refs):
    piece_refs = refs[:parts]
    qkv_ref, out_t_ref, log_ref = refs[parts : parts + 3]
    grad_refs = refs[parts + 3 : 3 * parts + 3]
    (
        g_ref,
        kaug_ref,
        qaug_ref,
        kt_ref,
        gq_ref,
        gg_ref,
        delta_ref,
        dqt_ref,
        dkv_ref,
    ) = refs[3 * parts + 3 :]
    length = qkv_ref.shape[0]
    blocks = length // BLOCK
    for i, block, dst in true_blocks(meta_ref, parts, ring, rows, together(ring)):
        g_ref[dst, :] = piece_refs[i][block, :]
    eye = (
        lax.broadcasted_iota(jnp.int32, (HD, HD), 0) == lax.broadcasted_iota(jnp.int32, (HD, HD), 1)
    ).astype(BF)

    def prepare(b, unused):
        prepare_block(b, heads, qkv_ref, slope_ref, kaug_ref, qaug_ref)
        cols = block_rows(b)
        blank = jnp.zeros((BLOCK, HD), BF)
        grad_t = g_ref[cols, :].astype(F32)
        if heads * HD < 128:
            grad_t = jnp.concatenate([grad_t, jnp.zeros((BLOCK, 128 - heads * HD), F32)], axis=1)
        product = grad_t.T * out_t_ref[:, cols]
        for h in range(heads):
            at = h * 3 * HD
            kt_ref[h, :, cols] = dot_nt(eye, qkv_ref[cols, at + HD : at + 2 * HD]).astype(BF)
            query = qkv_ref[cols, at : at + HD] * jnp.asarray(0.125, BF)
            gq_ref[h, cols, :] = jnp.concatenate([blank, query], axis=1)
            gg_ref[h, cols, :] = jnp.concatenate([g_ref[cols, h * HD : (h + 1) * HD], blank], axis=1)
            delta_ref[h : h + 1, cols] = jnp.sum(
                product[h * HD : (h + 1) * HD], axis=0, keepdims=True
            )
        return unused

    lax.fori_loop(0, blocks, prepare, 0)

    def part_of(h, keys, queries, allowed):
        at = h * 3 * HD + 2 * HD
        scores = dot_nt(kaug_ref[h, keys, :], qaug_ref[h, queries, :])
        first = jnp.where(allowed, scores[:, :BLOCK], -1e30)
        if scores.shape[1] > BLOCK:
            scores = jnp.concatenate([first, scores[:, BLOCK:]], axis=1)
        else:
            scores = first
        weight = jnp.exp(scores - log_ref[h : h + 1, queries])
        grad_weight = dot_nt(qkv_ref[keys, at : at + HD], g_ref[queries, h * HD : (h + 1) * HD])
        grad_score = (weight * (grad_weight - delta_ref[h : h + 1, queries])).astype(BF)
        dkv = dot(weight.astype(BF), gg_ref[h, queries, :]) + dot(grad_score, gq_ref[h, queries, :])
        return dkv, dot(kt_ref[h, :, keys], grad_score)

    for j in range(blocks):
        keys = slice(j * BLOCK, (j + 1) * BLOCK)
        queries = slice(j * BLOCK, length)
        allowed = allowed_block(j, j, meta_ref, spans)
        for h in range(heads):
            dkv, dq = part_of(h, keys, queries, allowed)
            dkv_ref[h, keys, :] = dkv
            rows_h = slice(h * HD, (h + 1) * HD)
            if j:
                dq = dq + dqt_ref[rows_h, queries]
            dqt_ref[rows_h, queries] = dq

        if j:

            @pl.when(crosses(j - 1, meta_ref, spans))
            def _(j=j, keys=keys):
                queries = slice((j - 1) * BLOCK, j * BLOCK)
                allowed = allowed_block(j - 1, j, meta_ref, spans)
                for h in range(heads):
                    dkv, dq = part_of(h, keys, queries, allowed)
                    dkv_ref[h, keys, :] += dkv
                    dqt_ref[h * HD : (h + 1) * HD, queries] += dq

    for i, block, true_rows in true_blocks(meta_ref, parts, ring, rows, leaving(ring)):
        columns = []
        grad_q = (dqt_ref[:, true_rows] * 0.125).T
        for h in range(heads):
            dkv = dkv_ref[h, true_rows, :]
            columns += [grad_q[:, h * HD : (h + 1) * HD], dkv[:, HD:], dkv[:, :HD]]
        grad_refs[i][block, :] = jnp.concatenate(columns, axis=1).astype(BF)


def specs(count_smem, count_vmem):
    return [pl.BlockSpec(memory_space=pltpu.SMEM)] * count_smem + [
        pl.BlockSpec(memory_space=pltpu.VMEM)
    ] * count_vmem


def attend_forward(pieces, meta, slopes, ring, rows):
    heads = slopes.shape[0]
    parts = len(pieces)
    length = parts * pieces[0].shape[0]
    wide = max(128, heads * HD)
    outs = pl.pallas_call(
        functools.partial(forward_kernel, heads, parts, ring, rows, meta.shape[0] - 2),
        out_shape=tuple(
            [jax.ShapeDtypeStruct((length // parts, heads * HD), BF)] * parts
            + [
                jax.ShapeDtypeStruct((length, heads * 3 * HD), BF),
                jax.ShapeDtypeStruct((wide, length), F32),
                jax.ShapeDtypeStruct((8, length), F32),
            ]
        ),
        in_specs=specs(2, parts),
        out_specs=tuple(specs(0, parts + 3)),
        scratch_shapes=[
            pltpu.VMEM((heads, length, 128), BF),
            pltpu.VMEM((heads, length, 128), BF),
            pltpu.VMEM((heads, HD + 16, length), BF),
            pltpu.VMEM((8, BLOCK), F32),
            pltpu.VMEM((heads, HD + 16, BLOCK), F32),
        ],
        compiler_params=pltpu.CompilerParams(vmem_limit_bytes=VMEM_BYTES),
        cost_estimate=pl.CostEstimate(
            flops=2 * US, bytes_accessed=length * heads * HD * 20, transcendentals=0
        ),
    )(meta, slopes, *pieces)
    return list(outs[:parts]), *outs[parts:]


def attend_backward(pieces, qkv, out_t, logs, meta, slopes, ring, rows):
    heads = slopes.shape[0]
    parts = len(pieces)
    length = qkv.shape[0]
    wide = max(128, heads * HD)
    outs = pl.pallas_call(
        functools.partial(backward_kernel, heads, parts, ring, rows, meta.shape[0] - 2),
        out_shape=tuple(
            jax.ShapeDtypeStruct((len(group) * rows, heads * 3 * HD), BF)
            for group in leaving(ring)
            for unused in range(parts)
        ),
        in_specs=specs(2, parts + 3),
        out_specs=tuple(specs(0, 2 * parts)),
        scratch_shapes=[
            pltpu.VMEM((length, heads * HD), BF),
            pltpu.VMEM((heads, length, 128), BF),
            pltpu.VMEM((heads, length, 128), BF),
            pltpu.VMEM((heads, HD, length), BF),
            pltpu.VMEM((heads, length, 128), BF),
            pltpu.VMEM((heads, length, 128), BF),
            pltpu.VMEM((8, length), F32),
            pltpu.VMEM((wide, length), F32),
            pltpu.VMEM((heads, length, 128), F32),
        ],
        compiler_params=pltpu.CompilerParams(vmem_limit_bytes=VMEM_BYTES),
        cost_estimate=pl.CostEstimate(
            flops=2 * US, bytes_accessed=length * heads * HD * 20, transcendentals=0
        ),
    )(meta, slopes, *pieces, qkv, out_t, logs)
    return list(outs[:parts]), list(outs[parts:])


def take_columns(ref, part, e, width):
    def each(use):
        if width % 128 == 0:
            start = pl.multiple_of((part ^ e) * width, width)
            use(ref.at[:, pl.ds(start, width)])
        else:
            for p in range(SEQ_DEVS):

                @pl.when(part == p)
                def _():
                    use(ref.at[:, pl.ds((p ^ e) * width, width)])

    return each


def column_loop(total, body):
    step = min(256, total)

    def one(i, unused):
        body(pl.ds(pl.multiple_of(i * step, step), step))
        return unused

    lax.fori_loop(0, total // step, one, 0)


def in_hbm(pieces):
    return [pltpu.with_memory_space_constraint(piece, pltpu.HBM) for piece in pieces]


def load_weights(w_pieces, w_ref, sems, starts_ref):
    copies = []
    for i, piece in enumerate(w_pieces):
        count = piece.shape[0]
        start = pl.multiple_of(starts_ref[i], min(128, count))
        copy = pltpu.make_async_copy(piece, w_ref.at[pl.ds(start, count), :], sems.at[i])
        copy.start()
        copies.append(copy)
    return copies


def load_shards(w_pieces, w_ref, sems, places_ref):
    copies = []
    for i, piece in enumerate(w_pieces):
        if len(piece.shape) == 3:
            copy = pltpu.make_async_copy(piece, w_ref, sems.at[i])
        else:
            count = piece.shape[0]
            start = pl.multiple_of(places_ref[2 * i + 1], count)
            target = w_ref.at[places_ref[2 * i], pl.ds(start, count), :]
            copy = pltpu.make_async_copy(piece, target, sems.at[i])
        copy.start()
        copies.append(copy)
    return copies


def normed_rows(rows_ref, gain_ref, shift_ref):
    return norm_forward(rows_ref[...].astype(F32), gain_ref[...], shift_ref[...])[0].astype(BF)


def prepare_qkv_kernel(count, starts_ref, *refs):
    h_pieces, refs = refs[:count], refs[count:]
    gain_ref, shift_ref, w_pieces, (w_ref, x_ref, sems) = refs[0], refs[1], refs[2:-3], refs[-3:]
    copies = load_weights(w_pieces, w_ref, sems, starts_ref)
    rows = h_pieces[0].shape[0]
    for k in range(count):
        x_ref[k * rows : (k + 1) * rows, :] = normed_rows(h_pieces[k], gain_ref, shift_ref)
    for copy in copies:
        copy.wait()


def prepare_qkv(h_pieces, gain, shift, w_pieces, starts):
    count, n_w = len(h_pieces), len(w_pieces)
    rows, depth = h_pieces[0].shape
    cols = w_pieces[0].shape[1]
    return pl.pallas_call(
        functools.partial(prepare_qkv_kernel, count),
        out_shape=[pltpu.VMEM((depth, cols), BF), pltpu.VMEM((count * rows, depth), BF)],
        in_specs=specs(1, count + 2) + [pl.BlockSpec(memory_space=pl.ANY)] * n_w,
        out_specs=specs(0, 2),
        scratch_shapes=[pltpu.SemaphoreType.DMA((n_w,))],
        compiler_params=pltpu.CompilerParams(vmem_limit_bytes=SMALL_VMEM_BYTES),
        cost_estimate=pl.CostEstimate(flops=3 * US, bytes_accessed=2**20, transcendentals=0),
    )(starts, *h_pieces, gain, shift, *in_hbm(w_pieces))


def qkv_kernel(meta_ref, first_ref, last_ref, gain_ref, shift_ref, a_ref, b_ref, bias_ref, *refs):
    w_ref, q_refs, (u_ref, x_ref, o_ref) = refs[0], refs[1 : 1 + SEQ_DEVS], refs[1 + SEQ_DEVS :]
    before = first_ref.shape[0]
    x_ref[:before, :] = first_ref[...]
    x_ref[before:, :] = normed_rows(last_ref, gain_ref, shift_ref)
    u_ref[...] = dot_nt(x_ref[...], a_ref[...]).astype(BF)

    def body(cols):
        total = dot(x_ref[...], w_ref[:, cols])
        total = total + FACTOR * dot(u_ref[...], b_ref[:, cols]) + bias_ref[:, cols]
        o_ref[:, cols] = total.astype(BF)

    column_loop(o_ref.shape[1], body)
    for e in range(SEQ_DEVS):

        def store(src, e=e):
            q_refs[e][...] = src[...]

        take_columns(o_ref, meta_ref[0], e, q_refs[e].shape[1])(store)


def qkv_product(first, last, gain, shift, a, b, bias, w, meta):
    count, depth = first.shape[0] + last.shape[0], first.shape[1]
    cols = b.shape[1]
    outs = pl.pallas_call(
        qkv_kernel,
        out_shape=tuple(
            [jax.ShapeDtypeStruct((count, cols // SEQ_DEVS), BF)] * SEQ_DEVS
            + [
                jax.ShapeDtypeStruct((count, a.shape[0]), BF),
                jax.ShapeDtypeStruct((count, depth), BF),
            ]
        ),
        in_specs=specs(1, 8),
        out_specs=tuple(specs(0, SEQ_DEVS + 2)),
        scratch_shapes=[pltpu.VMEM((count, cols), BF)],
        compiler_params=pltpu.CompilerParams(vmem_limit_bytes=SMALL_VMEM_BYTES),
        cost_estimate=pl.CostEstimate(flops=2 * US, bytes_accessed=2**20, transcendentals=0),
    )(meta, first, last, gain, shift, a, b, bias, w)
    return list(outs[:SEQ_DEVS]), outs[SEQ_DEVS], outs[SEQ_DEVS + 1]


def load_kernel(first_ref, second_ref, first_out, second_out, sems):
    shards, half = first_ref.shape[0], first_ref.shape[1]
    depth = second_ref.shape[2]
    chunks = first_out.shape[1] // depth
    copies = []

    def copy(src, dst):
        copies.append(pltpu.make_async_copy(src, dst, sems.at[len(copies)]))

    for i in range(shards):
        copy(first_ref.at[i], first_out.at[pl.ds(2 * i * half, half), :])
        for h in range(chunks):
            copy(
                second_ref.at[i, pl.ds(h * half, half)],
                first_out.at[pl.ds((2 * i + 1) * half, half), pl.ds(h * depth, depth)],
            )
        copy(second_ref.at[i, pl.ds(chunks * half, chunks * depth)], second_out.at[i])
    for each in copies:
        each.start()
    for each in copies:
        each.wait()


def load_to_vmem(first, second):
    shards, half, hidden = first.shape
    chunks = hidden // second.shape[2]
    return pl.pallas_call(
        load_kernel,
        out_shape=[
            pltpu.VMEM((shards * half * 2, hidden), BF),
            pltpu.VMEM((shards, hidden, second.shape[2]), BF),
        ],
        in_specs=[pl.BlockSpec(memory_space=pl.ANY)] * 2,
        out_specs=[pl.BlockSpec(memory_space=pltpu.VMEM)] * 2,
        scratch_shapes=[pltpu.SemaphoreType.DMA((shards * (chunks + 2),))],
        compiler_params=pltpu.CompilerParams(vmem_limit_bytes=2 * 1024 * 1024),
        cost_estimate=pl.CostEstimate(flops=5 * US, bytes_accessed=2**20, transcendentals=0),
    )(*[pltpu.with_memory_space_constraint(w, pltpu.HBM) for w in (first, second)])


def store_rows(refs, cols, total):
    at = 0
    for ref in refs:
        ref[:, cols] = total[at : at + ref.shape[0]]
        at += ref.shape[0]


def out_kernel(ring, n_w, meta_ref, places_ref, *refs):
    c_pieces = refs[:SEQ_DEVS]
    a_ref, b_ref = refs[SEQ_DEVS : SEQ_DEVS + 2]
    w_pieces, refs = refs[SEQ_DEVS + 2 : SEQ_DEVS + 2 + n_w], refs[SEQ_DEVS + 2 + n_w :]
    p_refs = refs[:ring]
    ctx_ref, u_ref, w_ref, sems = refs[ring:]
    copies = load_shards(w_pieces, w_ref, sems, places_ref)
    width = c_pieces[0].shape[1]
    for e in range(SEQ_DEVS):

        def store(dst, e=e):
            dst[...] = c_pieces[e][...]

        take_columns(ctx_ref, meta_ref[0], e, width)(store)
    u_ref[...] = dot_nt(ctx_ref[...], a_ref[...]).astype(BF)
    for copy in copies:
        copy.wait()
    shards, unused, wide = w_ref.shape
    for j in range(shards):
        cols = slice(j * wide, (j + 1) * wide)
        total = dot(ctx_ref[...], w_ref[j]) + FACTOR * dot(u_ref[...], b_ref[:, cols])
        store_rows(p_refs, cols, total.astype(BF))


def paired(pieces):
    return [list(pieces[i : i + 2]) for i in range(0, len(pieces), 2)]


def out_product(c_pieces, a, b, w_pieces, places, meta, ring, shards):
    count, width = c_pieces[0].shape
    rank, depth = b.shape
    n_w = len(w_pieces)
    outs = pl.pallas_call(
        functools.partial(out_kernel, 2 * ring, n_w),
        out_shape=tuple(
            [jax.ShapeDtypeStruct((count // ring // 2, depth), BF)] * (2 * ring)
            + [
                jax.ShapeDtypeStruct((count, width * SEQ_DEVS), BF),
                jax.ShapeDtypeStruct((count, rank), BF),
            ]
        ),
        in_specs=specs(2, SEQ_DEVS + 2) + [pl.BlockSpec(memory_space=pl.ANY)] * n_w,
        out_specs=tuple(specs(0, 2 * ring + 2)),
        scratch_shapes=[
            pltpu.VMEM((shards, width * SEQ_DEVS, depth // shards), BF),
            pltpu.SemaphoreType.DMA((n_w,)),
        ],
        compiler_params=pltpu.CompilerParams(vmem_limit_bytes=VMEM_BYTES),
        cost_estimate=pl.CostEstimate(flops=3 * US, bytes_accessed=2**20, transcendentals=0),
    )(meta, places, *c_pieces, a, b, *w_pieces)
    return paired(outs[: 2 * ring]), outs[2 * ring], outs[2 * ring + 1]


def mlp_kernel(count, add, *refs):
    n2_refs, (gy_ref, a1_ref, b2_ref, b1_ref, a2_ref, bias_ref), refs = (
        refs[:count],
        refs[count : count + 6],
        refs[count + 6 :],
    )
    w1_ref, w2_ref, before, refs = refs[0], refs[1], refs[2 : 2 + add], refs[2 + add :]
    p_refs, m_ref, grads = refs[:count], refs[count], refs[count + 1 : count + 5]
    x_ref, act_ref, slope_ref, gf_ref = refs[count + 5 :]
    shards, hidden, wide = w2_ref.shape
    at = 0
    for ref in n2_refs:
        x_ref[at : at + ref.shape[0], :] = ref[...]
        at += ref.shape[0]
    u3 = dot_nt(x_ref[...], a1_ref[...]).astype(BF)
    gu4 = (FACTOR * dot_nt(gy_ref[...], b2_ref[...])).astype(BF)
    for h in range(0, hidden, wide):
        cols = slice(h, h + wide)
        f = dot(x_ref[...], w1_ref[:, cols])
        f = f + FACTOR * dot(u3, b1_ref[:, cols]) + bias_ref[:, cols]
        act, slope = gelu_and_slope(f)
        act_ref[:, cols] = act.astype(BF)
        slope_ref[:, cols] = slope
    for h in range(0, hidden, wide):
        cols = slice(h, h + wide)
        gact = dot(gu4, a2_ref[:, cols])
        for j in range(shards):
            gact = gact + dot_nt(gy_ref[:, j * wide : (j + 1) * wide], w2_ref[j, cols, :])
        gf_ref[:, cols] = (gact * slope_ref[:, cols]).astype(BF)
    gu3 = (FACTOR * dot_nt(gf_ref[...], b1_ref[...])).astype(BF)
    for j in range(shards):
        cols = slice(j * wide, (j + 1) * wide)
        total = dot_nt(gf_ref[...], w1_ref[cols, :]) + dot(gu3, a1_ref[:, cols])
        store_rows(p_refs, cols, total.astype(BF))
    u4 = dot_nt(act_ref[...], a2_ref[...]).astype(BF)
    for j in range(shards):
        cols = slice(j * wide, (j + 1) * wide)
        total = dot(act_ref[...], w2_ref[j]) + FACTOR * dot(u4, b2_ref[:, cols])
        m_ref[:, cols] = total.astype(BF)
    products = [
        FACTOR * dot_tn(u3, gf_ref[...]),
        dot_tn(gu4, act_ref[...]),
        dot_tn(gu3, x_ref[...]),
        FACTOR * dot_tn(u4, gy_ref[...]),
    ]
    for i, product in enumerate(products):
        grads[i][...] = product + before[i][...] if add else product


def mlp_both_ways(n2_pieces, gy, a1, b1, a2, b2, bias, weights, before):
    count = len(n2_pieces)
    total, depth = gy.shape
    rank, hidden = b1.shape
    outs = pl.pallas_call(
        functools.partial(mlp_kernel, count, len(before)),
        out_shape=(
            [jax.ShapeDtypeStruct(piece.shape, BF) for piece in n2_pieces]
            + [jax.ShapeDtypeStruct((total, depth), BF)]
            + [jax.ShapeDtypeStruct((rank, hidden), F32)] * 2
            + [jax.ShapeDtypeStruct((rank, depth), F32)] * 2
        ),
        in_specs=specs(0, count + 8 + len(before)),
        out_specs=specs(0, count + 5),
        scratch_shapes=[
            pltpu.VMEM((total, depth), BF),
            pltpu.VMEM((total, hidden), BF),
            pltpu.VMEM((total, hidden), F32),
            pltpu.VMEM((total, hidden), BF),
        ],
        compiler_params=pltpu.CompilerParams(vmem_limit_bytes=SMALL_VMEM_BYTES),
        cost_estimate=pl.CostEstimate(
            flops=10 * US, bytes_accessed=4 * depth * hidden, transcendentals=0
        ),
    )(*n2_pieces, gy, a1, b2, b1, a2, bias, *weights, *before)
    return list(outs[:count]), outs[count], list(outs[count + 1 :])


def pack_into(full, own, ring, groups, meta_ref, out_ref):
    part, spot = meta_ref[0], meta_ref[1]
    wide = out_ref.shape[4]
    at = 0
    for ref in full:
        width = ref.shape[1] // (ring * SEQ_DEVS * groups)
        for g in range(groups):
            for p in range(SEQ_DEVS):
                for z in range(ring):
                    k = z - spot
                    k = jnp.where(k < 0, k + ring, k)
                    column = ((g * SEQ_DEVS + p) * ring + z) * width
                    out_ref[part ^ p, k, g, :, at : at + width] = ref[
                        :, column : column + width
                    ].astype(BF)
        at += width
    at = 0
    for ref in own:
        width = ref.shape[1] // (SEQ_DEVS * groups)
        for p in range(SEQ_DEVS):
            for r in range(groups):
                column = (p * groups + r) * width
                out_ref[part ^ p, ring + at // wide, r, :, at % wide : at % wide + width] = ref[
                    :, column : column + width
                ].astype(BF)
        at += width


def pack_shapes(full_cols, own_cols, rank, ring, groups):
    full_widths = [c // (ring * SEQ_DEVS * groups) for c in full_cols]
    own_widths = [c // (SEQ_DEVS * groups) for c in own_cols]
    wide = sum(full_widths)
    rows = ring + sum(own_widths) // wide
    shapes = [jax.ShapeDtypeStruct((SEQ_DEVS, rows, groups, rank, wide), BF)]
    return shapes, full_widths, own_widths


def gctx_kernel(n_g, n_w, meta_ref, places_ref, *refs):
    g_pieces, refs = refs[:n_g], refs[n_g:]
    a_ref, b_ref, ctx_ref, u2_ref = refs[:4]
    w_pieces, refs = refs[4 : 4 + n_w], refs[4 + n_w :]
    c_refs = refs[:SEQ_DEVS]
    gbo_ref, gao_ref, g_ref, o_ref, w_ref, sems = refs[SEQ_DEVS:]
    copies = load_shards(w_pieces, w_ref, sems, places_ref)
    rows = g_pieces[0].shape[0]
    for k in range(n_g):
        g_ref[k * rows : (k + 1) * rows, :] = g_pieces[k][...]
    gu2 = (FACTOR * dot_nt(g_ref[...], b_ref[...])).astype(BF)
    shards, unused, wide = w_ref.shape
    total = dot(gu2, a_ref[...])
    gbo_ref[...] = FACTOR * dot_tn(u2_ref[...], g_ref[...])
    gao_ref[...] = dot_tn(gu2, ctx_ref[...])
    for copy in copies:
        copy.wait()
    for j in range(shards):
        total = total + dot_nt(g_ref[:, j * wide : (j + 1) * wide], w_ref[j])
    o_ref[...] = total.astype(BF)
    for e in range(SEQ_DEVS):

        def store(src, e=e):
            c_refs[e][...] = src[...]

        take_columns(o_ref, meta_ref[0], e, c_refs[e].shape[1])(store)


def gctx_product(g_pieces, a, b, w_pieces, places, ctx, u2, meta, shards):
    n_g, n_w = len(g_pieces), len(w_pieces)
    depth = g_pieces[0].shape[1]
    count, cols = ctx.shape
    rank = a.shape[0]
    outs = pl.pallas_call(
        functools.partial(gctx_kernel, n_g, n_w),
        out_shape=tuple(
            [jax.ShapeDtypeStruct((count, cols // SEQ_DEVS), BF)] * SEQ_DEVS
            + [jax.ShapeDtypeStruct((rank, depth), F32), jax.ShapeDtypeStruct((rank, cols), F32)]
        ),
        in_specs=specs(2, n_g + 4) + [pl.BlockSpec(memory_space=pl.ANY)] * n_w,
        out_specs=tuple(specs(0, SEQ_DEVS + 2)),
        scratch_shapes=[
            pltpu.VMEM((count, depth), BF),
            pltpu.VMEM((count, cols), BF),
            pltpu.VMEM((shards, cols, depth // shards), BF),
            pltpu.SemaphoreType.DMA((n_w,)),
        ],
        compiler_params=pltpu.CompilerParams(vmem_limit_bytes=VMEM_BYTES),
        cost_estimate=pl.CostEstimate(flops=3 * US, bytes_accessed=2**20, transcendentals=0),
    )(meta, places, *g_pieces, a, b, ctx, u2, *w_pieces)
    return list(outs[:SEQ_DEVS]), outs[SEQ_DEVS], outs[SEQ_DEVS + 1]


def near_kernel(starts_ref, *refs):
    w_pieces, w_ref, sems = refs[:-2], refs[-2], refs[-1]
    for copy in load_weights(w_pieces, w_ref, sems, starts_ref):
        copy.wait()


def load_rows_to_vmem(w_pieces, starts, shape):
    n_w = len(w_pieces)
    return pl.pallas_call(
        near_kernel,
        out_shape=pltpu.VMEM(shape, BF),
        in_specs=specs(1, 0) + [pl.BlockSpec(memory_space=pl.ANY)] * n_w,
        out_specs=specs(0, 1)[0],
        scratch_shapes=[pltpu.SemaphoreType.DMA((n_w,))],
        compiler_params=pltpu.CompilerParams(vmem_limit_bytes=2 * 1024 * 1024),
        cost_estimate=pl.CostEstimate(flops=2 * US, bytes_accessed=2**20, transcendentals=0),
    )(starts, *in_hbm(w_pieces))


def gather_columns(q_pieces, q_ref, meta_ref):
    for e in range(SEQ_DEVS):

        def store(dst, e=e):
            dst[...] = q_pieces[e][...]

        take_columns(q_ref, meta_ref[0], e, q_pieces[e].shape[1])(store)


def gn1_rows(q_ref, gu1, a_ref, w_ref, p_refs):
    def body(cols):
        total = dot_nt(q_ref[...], w_ref[cols, :]) + dot(gu1, a_ref[:, cols])
        store_rows(p_refs, cols, total.astype(BF))

    column_loop(w_ref.shape[0], body)


def gn1_first_kernel(meta_ref, *refs):
    q_pieces, (a_ref, b_ref, w_ref), refs = refs[:SEQ_DEVS], refs[SEQ_DEVS : SEQ_DEVS + 3], refs[SEQ_DEVS + 3 :]
    *p_refs, q_ref, gu_ref = refs
    gather_columns(q_pieces, q_ref, meta_ref)
    gu_ref[...] = (FACTOR * dot_nt(q_ref[...], b_ref[...])).astype(BF)
    gn1_rows(q_ref, gu_ref[...], a_ref, w_ref, p_refs)


def gn1_first(q_pieces, a, b, w, meta):
    rows = q_pieces[0].shape[0]
    rank, depth = a.shape
    outs = pl.pallas_call(
        gn1_first_kernel,
        out_shape=[jax.ShapeDtypeStruct((rows // 2, depth), BF)] * 2
        + [jax.ShapeDtypeStruct((rows, b.shape[1]), BF), jax.ShapeDtypeStruct((rows, rank), BF)],
        in_specs=specs(1, SEQ_DEVS + 3),
        out_specs=specs(0, 4),
        compiler_params=pltpu.CompilerParams(vmem_limit_bytes=SMALL_VMEM_BYTES),
        cost_estimate=pl.CostEstimate(flops=3 * US, bytes_accessed=2**20, transcendentals=0),
    )(meta, *q_pieces, a, b, w)
    return list(outs[:2]), outs[2], outs[3]


def gn1_rest_kernel(ring, groups, blocks, meta_ref, *refs):
    q_pieces, refs = refs[:SEQ_DEVS], refs[SEQ_DEVS:]
    q1_ref, gu1_ref, x_ref, u_ref, a_ref, b_ref, w_ref = refs[:7]
    full, own, p_refs, refs = refs[7:10], refs[10:13], refs[13 : 13 + blocks], refs[13 + blocks :]
    out_ref, q_ref, gb_ref, ga_ref = refs
    rows = q1_ref.shape[0]
    gather_columns(q_pieces, q_ref, meta_ref)
    gu1 = (FACTOR * dot_nt(q_ref[...], b_ref[...])).astype(BF)
    gn1_rows(q_ref, gu1, a_ref, w_ref, p_refs)
    here = slice(rows, 2 * rows)
    x = jnp.concatenate([x_ref[2 * rows :, :], x_ref[:rows, :]], axis=0)
    u = jnp.concatenate([u_ref[2 * rows :, :], u_ref[:rows, :]], axis=0)
    gb_ref[...] = FACTOR * (dot_tn(u, q_ref[...]) + dot_tn(u_ref[here, :], q1_ref[...]))
    ga_ref[...] = dot_tn(gu1, x) + dot_tn(gu1_ref[...], x_ref[here, :])
    pack_into([ga_ref, *full], [gb_ref, *own], ring, groups, meta_ref, out_ref)


def gn1_rest(q_pieces, q1, gu1, n1, u1, a, b, w, full, own, meta, ring, groups):
    count = q_pieces[0].shape[0]
    rank, depth = a.shape
    cols = b.shape[1]
    rows = q1.shape[0]
    blocks = 2 * count // rows
    shapes, full_widths, own_widths = pack_shapes(
        [depth] + [g.shape[1] for g in full],
        [cols] + [g.shape[1] for g in own],
        rank,
        ring,
        groups,
    )
    outs = pl.pallas_call(
        functools.partial(gn1_rest_kernel, ring, groups, blocks),
        out_shape=[jax.ShapeDtypeStruct((rows // 2, depth), BF)] * blocks + shapes,
        in_specs=specs(1, SEQ_DEVS + 13),
        out_specs=specs(0, blocks + 1),
        scratch_shapes=[
            pltpu.VMEM((count, cols), BF),
            pltpu.VMEM((rank, cols), F32),
            pltpu.VMEM((rank, depth), F32),
        ],
        compiler_params=pltpu.CompilerParams(vmem_limit_bytes=SMALL_VMEM_BYTES),
        cost_estimate=pl.CostEstimate(flops=6 * US, bytes_accessed=2**20, transcendentals=0),
    )(meta, *q_pieces, q1, gu1, n1, u1, a, b, w, *full, *own)
    stages = functools.partial(
        reduce_stages, full_widths=full_widths, own_widths=own_widths, groups=groups
    )
    return paired(outs[:blocks]), Side(list(outs[blocks:]), stages)


def reduce_stages(packed, full_widths, own_widths, groups):
    ring, n = lax.axis_size("tensor"), lax.axis_size("dp")
    group = lax.axis_index("dp") // SEQ_DEVS
    landed = yield [exchange(packed[e], e) for e in range(1, SEQ_DEVS)]
    total = sum([x.astype(F32) for x in landed], packed[0].astype(F32)).astype(BF)

    def block(array, k):
        return lax.dynamic_index_in_dim(array, (group + k) % groups, -3, keepdims=False)

    flying = [
        lax.ppermute(total[k], "tensor", [(i, (i + k) % ring) for i in range(ring)])
        for k in range(1, ring)
    ]
    for k in range(groups):
        pairs = []
        for i in range(n):
            for z in range(ring):
                r = (i // SEQ_DEVS + k) % groups
                pairs.append((i * ring + z, z * n + (i % SEQ_DEVS) * groups + r))
        flying.append(lax.ppermute(block(total[ring:], k), ("dp", "tensor"), pairs))
    landed = yield flying
    own = list(landed[ring - 1 :])
    total = sum([x.astype(F32) for x in landed[: ring - 1]], total[0].astype(F32)).astype(BF)
    flying = []
    for k in range(1, groups):
        pairs = [(i, (i + k * SEQ_DEVS) % n) for i in range(n)]
        flying.append(lax.ppermute(block(total, k), "dp", pairs))
    landed = yield flying
    return ([block(total, 0)] + list(landed), full_widths), (own, own_widths)


def place_kernel(n_full, n_own, full_widths, own_widths, home_ref, adapter_ref, *refs):
    outs = refs[n_full + n_own :]
    for out in outs:
        out[...] = jnp.zeros(out.shape, F32)
    for i, ref in enumerate(refs[: n_full + n_own]):
        k = i if i < n_full else i - n_full
        sequence = home_ref[int(i >= n_full)] - k
        sequence = jnp.where(sequence < 0, sequence + n_full, sequence)
        slot, at = adapter_ref[sequence], 0
        targets = outs[: len(full_widths)] if i < n_full else outs[len(full_widths) :]
        for out, width in zip(targets, full_widths if i < n_full else own_widths):
            if i < n_full:
                columns = ref[:, at : at + width]
            else:
                wide = ref.shape[2]
                columns = ref[at // wide, :, at % wide : at % wide + width]
            out[slot] = out[slot] + columns.astype(F32)
            at += width


def place(full, full_widths, own, own_widths, home, seq_adapter):
    rank = full[0].shape[0]
    widths = full_widths + own_widths
    return pl.pallas_call(
        functools.partial(place_kernel, len(full), len(own), full_widths, own_widths),
        out_shape=[jax.ShapeDtypeStruct((ADAPTERS, rank, w), F32) for w in widths],
        in_specs=specs(2, len(full) + len(own)),
        out_specs=specs(0, len(widths)),
        compiler_params=pltpu.CompilerParams(vmem_limit_bytes=VMEM_BYTES),
        cost_estimate=pl.CostEstimate(flops=US, bytes_accessed=2**20, transcendentals=0),
    )(home, seq_adapter, *full, *own)


def gather_first(shard, rows_in, data, small):
    n, count = lax.axis_size("dp"), shard.shape[0]
    if n != 8 or lax.axis_size("tensor") != 4:
        whole = lax.all_gather(shard, "dp", axis=0, tiled=True)
        return [whole], [0 * data], ring_gather(rows_in, "tensor"), small
    half = count // 2
    by_x, by_y, by_c = exchange(shard, 2), exchange(shard, 4), exchange(shard, 1)
    ring = [rows_in, shift_one(rows_in, "tensor")]
    by_x, by_y, by_c, ring[1], *small = lax.optimization_barrier(
        (by_x, by_y, by_c, ring[1]) + small
    )
    corner_a, corner_b = exchange(by_x[:half], 4), exchange(by_y[half:], 2)
    by_xc, by_yc = exchange(by_x, 1), exchange(by_y, 1)
    ring.append(shift_one(ring[1], "tensor"))
    corner_a, corner_b, by_xc, by_yc, ring[2], small[:2] = lax.optimization_barrier(
        (corner_a, corner_b, by_xc, by_yc, ring[2], small[:2])
    )
    far_a, far_b = exchange(corner_a, 1), exchange(corner_b, 1)
    ring.append(shift_one(ring[2], "tensor"))
    pieces = [shard, by_c, by_x, by_xc, by_y, by_yc, corner_a, far_a, corner_b, far_b]
    starts = [(data ^ e) * count for e in range(8)]
    starts += [(data ^ e) * count + half for e in (6, 7)]
    return pieces, starts, ring, small


def gather_shards(shard, data):
    stages = shard_stages(data)
    next(stages)
    return stages


def shard_stages(data):
    n = lax.axis_size("dp")
    shard = yield None
    if n != 8:
        landed = yield [lax.all_gather(shard, "dp", axis=0, tiled=False)]
        landed = yield landed
        landed = yield landed
        yield landed
        return
    half = shard.shape[0] // 2
    by_x, by_y, by_c = yield [exchange(shard, 2), exchange(shard, 4), exchange(shard, 1)]
    sent = [exchange(by_x[:half], 4), exchange(by_y[half:], 2), exchange(by_x, 1), exchange(by_y, 1)]
    corner_a, corner_b, by_xc, by_yc = yield sent
    far_a, far_b = yield [exchange(corner_a, 1), exchange(corner_b, 1)]
    pieces = [shard, by_c, by_x, by_xc, by_y, by_yc, corner_a, far_a, corner_b, far_b]
    yield pieces


def shard_places(shard, data):
    if lax.axis_size("dp") != 8:
        return jnp.zeros((2,), jnp.int32)
    half = shard.shape[0] // 2
    places = [(data ^ e, 0 * data) for e in range(8)] + [(data ^ e, 0 * data + half) for e in (6, 7)]
    return jnp.stack([p for place in places for p in place]).astype(jnp.int32)


def swap_start(pieces):
    return [exchange(pieces[2], 2), exchange(pieces[3], 2), exchange(pieces[1], 1)]


def swap_end(pieces, landed):
    across, far, near = landed
    return [pieces[0], near, across, exchange(far, 1)]


def swap_heads(pieces, beside=()):
    across, far, near = exchange(pieces[2], 2), exchange(pieces[3], 2), exchange(pieces[1], 1)
    across, far, near, beside = lax.optimization_barrier((across, far, near, beside))
    return [pieces[0], near, across, exchange(far, 1)], beside


def local(
    hidden_in,
    ln1_gain,
    ln1_bias,
    qkv_weight,
    joined_bias,
    out_weight,
    output_bias,
    ln2_gain,
    ln2_bias,
    fc1_weight,
    first_feed_bias,
    fc2_weight,
    second_feed_bias,
    qkv_down,
    qkv_up,
    out_down,
    out_up,
    fc1_down,
    fc1_up,
    fc2_down,
    fc2_up,
    seq_adapter,
    span_starts,
    cotangent,
):
    spot = lax.axis_index("tensor")
    data = lax.axis_index("dp")
    ring = lax.axis_size("tensor")
    groups = lax.axis_size("dp") // SEQ_DEVS
    group, part = data // SEQ_DEVS, data % SEQ_DEVS
    rows = hidden_in.shape[0]
    slot = lax.dynamic_index_in_dim(seq_adapter, group, 0, keepdims=False)
    starts = lax.dynamic_index_in_dim(span_starts, group, 0, keepdims=False)
    qkv_cols, ctx_cols, hidden_cols = qkv_weight.shape[1], out_weight.shape[0], fc1_weight.shape[1]
    heads = qkv_cols // (3 * HD) // SEQ_DEVS
    meta = jnp.concatenate([jnp.stack([part, spot]), starts]).astype(jnp.int32)
    first_head = (spot * SEQ_DEVS + part) * heads
    slopes = jnp.exp2(
        -8.0 * ((first_head + jnp.arange(heads, dtype=jnp.int32)).astype(F32) + 1.0) / H
    )

    def pick(stack):
        return lax.dynamic_index_in_dim(stack, slot, 0, keepdims=False)

    def own_cols(matrix, count):
        return lax.dynamic_slice_in_dim(matrix, spot * count, count, 1)

    a_q, b_q = pick(qkv_down), own_cols(pick(qkv_up), qkv_cols)
    a_o, b_o = own_cols(pick(out_down), ctx_cols), pick(out_up)
    a_1, b_1 = pick(fc1_down), own_cols(pick(fc1_up), hidden_cols)
    a_2, b_2 = own_cols(pick(fc2_down), hidden_cols), pick(fc2_up)

    n = lax.axis_size("dp")
    shard = fc1_weight.shape[0]
    chunks = hidden_cols // shard
    upper, lower = halves(fc1_weight)
    lower = jnp.transpose(lower.reshape(shard // 2, chunks, shard), (1, 0, 2)).reshape(-1, shard)
    fc_rest = jnp.concatenate([lower, fc2_weight], axis=0)
    places = shard_places(out_weight, data)
    home = jnp.stack([group, (data * ring + spot) % groups]).astype(jnp.int32)
    w_qkv, w_starts, h_pieces, (upper, *small) = gather_first(
        qkv_weight,
        hidden_in,
        data,
        (upper, out_weight, fc_rest, places, home)
        + (a_q, b_q, a_o, b_o, a_1, b_1, a_2, b_2, slopes),
    )
    held_out, fc_rest, places, home, a_q, b_q, a_o, b_o, a_1, b_1, a_2, b_2, slopes = small
    w_fc_first = lax.all_gather(upper, "dp", axis=0, tiled=False)
    w_starts = jnp.stack(w_starts).astype(jnp.int32)
    out_stages = gather_shards(out_weight, data)
    flying = out_stages.send(held_out)

    x = halves(hidden_in.astype(F32))
    w_qkv_near, n1_first = prepare_qkv(
        h_pieces[:-1], ln1_gain[None], ln1_bias[None], w_qkv, w_starts
    )
    h_pieces[-1], cotangent_held, flying, w_qkv_near = lax.optimization_barrier(
        (h_pieces[-1], cotangent, flying, w_qkv_near)
    )
    gy = [cotangent, shift_one(cotangent_held, "tensor")]
    flying = out_stages.send(flying)
    pieces, u1, n1 = qkv_product(
        n1_first,
        h_pieces[-1],
        ln1_gain[None],
        ln1_bias[None],
        a_q,
        b_q,
        joined_bias[None],
        w_qkv_near,
        meta,
    )
    pieces, flying, fc_rest = lax.optimization_barrier((pieces, flying, fc_rest))
    flying = out_stages.send(flying)
    w_fc_second = lax.all_gather(fc_rest, "dp", axis=0, tiled=False)
    pieces, (gy, flying) = swap_heads(pieces, (gy, flying))
    gy.append(shift_one(gy[1], "tensor"))
    pieces, qkv_true, out_t, logs = attend_forward(pieces, meta, slopes, ring, rows)
    pieces, gy = lax.optimization_barrier((pieces, gy))
    gy += ring_gather(gy[-1], "tensor", ring - 3)[1:]
    pieces, unused = swap_heads(pieces)
    pieces, gy = lax.optimization_barrier((pieces, gy))
    w_out = out_stages.send(flying)
    part_out, ctx, u2 = out_product(pieces, a_o, b_o, w_out, places, meta, ring, n)
    weights = [w_fc_first, w_fc_second]

    def load_beside(hop, moved):
        if hop == ring - 3:
            moved, weights[:] = lax.optimization_barrier((moved, weights))
        if hop == ring - 2:
            moved, weights[:] = lax.optimization_barrier((moved, load_to_vmem(*weights)))
        return moved

    summed = ring_scatter(part_out, "tensor", load_beside)
    mid = [rows_in + (term + output_bias) for rows_in, term in zip(x, summed)]

    normed2 = [norm_forward(m, ln2_gain, ln2_bias) for m in mid]
    block = [normed.astype(BF) for normed, unused, unused in normed2]
    part_in2, part_mlp, fc_grads = [], [], []
    for k in range(ring):
        following = shift_all(block if k < ring - 1 else part_in2[1], "tensor")
        grad_pieces, out_piece, fc_grads = mlp_both_ways(
            block, gy[k], a_1, b_1, a_2, b_2, first_feed_bias[None], weights, fc_grads
        )
        part_in2.append(grad_pieces)
        part_mlp.append(out_piece)
        block, part_in2[1:], fc_grads = lax.optimization_barrier(
            (following, part_in2[1:], fc_grads)
        )
    g_b1, g_a2, g_a1, g_b2 = fc_grads
    grad_n2 = ring_scatter(part_in2, "tensor", moved=block)
    grad_mid = [
        top.astype(F32) + norm_backward(grad, unit, inverse, ln2_gain)
        for top, grad, (unused, unit, inverse) in zip(halves(cotangent), grad_n2, normed2)
    ]
    gm = [[g.astype(BF) for g in grad_mid]]
    for k in range(ring):
        if k < ring - 1:
            gm.append(shift_all(gm[-1], "tensor"))
    gm = [half for pair in gm for half in pair]

    mlp_total, gm = lax.optimization_barrier((part_mlp[1], gm))
    mlp_total = shift_one(mlp_total, "tensor")
    pieces, g_bo, g_ao = gctx_product(gm, a_o, b_o, w_out, places, ctx, u2, meta, n)
    pieces, mlp_total = swap_heads(pieces, mlp_total)
    (mlp_total,) = add_terms([mlp_total], part_mlp[2:3], BF)
    mlp_total = shift_one(mlp_total, "tensor")
    first, second = attend_backward(pieces, qkv_true, out_t, logs, meta, slopes, ring, rows)
    first, second, mlp_total = lax.optimization_barrier((first, second, mlp_total))
    (mlp_total,) = add_terms([mlp_total], (part_mlp[3:] + part_mlp[:1])[:1], BF)
    mlp_total = shift_one(mlp_total, "tensor")
    landed = swap_start(first)
    w_near = load_rows_to_vmem(w_qkv, w_starts, (qkv_down.shape[2], qkv_cols))
    landed, w_near, second = lax.optimization_barrier((landed, w_near, second))
    first = swap_end(first, landed)
    landed = swap_start(second)
    part_first, q1, gu1 = gn1_first(first, a_q, b_q, w_near, meta)
    part_first, mlp_total = lax.optimization_barrier((part_first, mlp_total))
    for terms in (part_mlp[3:] + part_mlp[:1])[1:]:
        (mlp_total,) = add_terms([mlp_total], [terms], F32)
        if terms is not part_mlp[0]:
            mlp_total = shift_one(mlp_total.astype(BF), "tensor")
    moved = shift_all(part_first, "tensor")
    second = swap_end(second, landed)
    part_rest, late = gn1_rest(
        second,
        q1,
        gu1,
        n1,
        u1,
        a_q,
        b_q,
        w_near,
        [g_bo, g_a1, g_b2],
        [g_ao, g_b1, g_a2],
        meta,
        ring,
        groups,
    )
    moved, part_rest = lax.optimization_barrier((moved, part_rest))
    late.step(())
    part_in1 = part_rest[-1:] + [part_first] + part_rest[:-1]

    def reduce_beside(hop, moved):
        late.step(moved[0])
        return moved

    grad_n1 = ring_scatter(part_in1, "tensor", reduce_beside, moved)
    while late.result is None:
        late.step(())
    layer_output = jnp.concatenate(
        [(m + (t + second_feed_bias)).astype(BF) for m, t in zip(mid, halves(mlp_total))], axis=0
    )
    normed1 = [norm_forward(rows_in, ln1_gain, ln1_bias) for rows_in in x]
    hidden_grad = jnp.concatenate(
        [
            g + norm_backward(grad, unit, inverse, ln1_gain)
            for g, grad, (unused, unit, inverse) in zip(grad_mid, grad_n1, normed1)
        ],
        axis=0,
    )

    (full, full_widths), (own, own_widths) = late.result
    g_aq, g_bo, g_a1, g_b2, g_bq, g_ao, g_b1, g_a2 = place(
        full, full_widths, own, own_widths, home, seq_adapter
    )
    return (layer_output, hidden_grad, g_aq, g_bq, g_ao, g_bo, g_a1, g_b1, g_a2, g_b2)


def solution(mesh):
    rows, cols = P(("dp", "tensor"), None), P(None, None, ("dp", "tensor"))
    placed = (
        rows,
        P(),
        P(),
        P("dp", "tensor"),
        P("tensor"),
        P("tensor", "dp"),
        P(),
        P(),
        P(),
        P("dp", "tensor"),
        P("tensor"),
        P("tensor", "dp"),
    ) + (P(),) * 11 + (rows,)
    return jax.shard_map(
        local,
        mesh=mesh,
        in_specs=placed,
        out_specs=(rows, rows) + (cols,) * 8,
        check_vma=False,
    )
```

```python
import functools

import jax
import jax.numpy as jnp
from jax import lax
from jax.experimental import pallas as pl
from jax.experimental.pallas import tpu as pltpu
from jax.sharding import PartitionSpec as P

H = 32
HD = 64
ADAPTERS = 8
SEQ_DEVS = 4
PIC = 256
EPS = 1e-05
FACTOR = 0.5
BF = jnp.bfloat16
F32 = jnp.float32
FORWARD_BLOCK, BACKWARD_BLOCK = 512, 256
VMEM_BYTES = 56 * 1024 * 1024
SMALL_VMEM_BYTES = 28 * 1024 * 1024
US = 10**9


def dot(a, b):
    return jnp.dot(a, b, preferred_element_type=F32)


def dot_nt(a, b):
    return lax.dot_general(a, b, (((1,), (1,)), ((), ())), preferred_element_type=F32)


def dot_tn(a, b):
    return lax.dot_general(a, b, (((0,), (0,)), ((), ())), preferred_element_type=F32)


def hold(value, *until):
    return lax.optimization_barrier((value,) + until)[0]


def gelu_and_slope(f):
    phi = 0.5 * (1.0 + lax.erf(f * (0.5**0.5)))
    density = jnp.exp(-0.5 * f * f) * (0.5 / jnp.pi) ** 0.5
    return f * phi, phi + f * density


def norm_forward(values, gain, shift):
    centred = values - jnp.mean(values, axis=-1, keepdims=True)
    inverse = lax.rsqrt(jnp.mean(centred * centred, axis=-1, keepdims=True) + EPS)
    unit = centred * inverse
    return unit * gain + shift, unit, inverse


def norm_backward(upstream, unit, inverse, gain):
    scaled = upstream * gain
    return inverse * (
        scaled
        - jnp.mean(scaled, axis=-1, keepdims=True)
        - unit * jnp.mean(scaled * unit, axis=-1, keepdims=True)
    )


def shift_one(array, axis):
    n = lax.axis_size(axis)
    return lax.ppermute(array, axis, [(i, (i + 1) % n) for i in range(n)])


def ring_gather(array, axis, hops=None):
    pieces = [array]
    for _ in range(lax.axis_size(axis) - 1 if hops is None else hops):
        pieces.append(shift_one(pieces[-1], axis))
    return pieces


def halves(array):
    middle = array.shape[0] // 2
    return [array[:middle], array[middle:]]


def shift_all(arrays, axis):
    return [shift_one(a, axis) for a in arrays]


class Side:
    def __init__(self, operands, stages):
        self.operands, self.make, self.stages = operands, stages, None
        self.flying, self.result = (), None

    def step(self, beside):
        if self.result is not None:
            return beside
        if self.stages is None:
            beside, self.operands = lax.optimization_barrier((beside, self.operands))
            self.stages = self.make(*self.operands)
            self.flying = next(self.stages)
            return beside
        beside, landed = lax.optimization_barrier((beside, self.flying))
        try:
            self.flying = self.stages.send(landed)
        except StopIteration as stop:
            self.result = stop.value
        return beside


def add_terms(moved, terms, dtype):
    return [(m.astype(F32) + t.astype(F32)).astype(dtype) for m, t in zip(moved, terms)]


def ring_scatter(pieces, axis, beside=None, moved=None):
    following = pieces[2:] + pieces[:1]
    total = None if moved is not None else pieces[1]
    for i, terms in enumerate(following):
        if total is not None:
            moved = shift_all(total, axis)
        if beside is not None and total is not None:
            moved = beside(i, moved)
        total = add_terms(moved, terms, F32 if i == len(following) - 1 else BF)
    return total


def exchange(array, distance):
    n = lax.axis_size("dp")
    return lax.ppermute(array, "dp", [(i, i ^ distance) for i in range(n)])


def span_of(positions, meta_ref, spans, outside):
    label = jnp.full(positions.shape, outside, jnp.int32)
    for j in range(spans):
        start = meta_ref[2 + j]
        label = jnp.where((positions >= start) & (positions < start + PIC), j, label)
    return label


def allowed_block(i, j, size, meta_ref, spans):
    key_pos = j * size + lax.broadcasted_iota(jnp.int32, (size, size), 0)
    row_pos = i * size + lax.broadcasted_iota(jnp.int32, (size, size), 1)
    key_label = span_of(key_pos, meta_ref, spans, -1)
    row_label = span_of(row_pos, meta_ref, spans, -2)
    return (key_pos <= row_pos) | (key_label == row_label)


def crosses(i, size, meta_ref, spans):
    edge = (i + 1) * size
    found = jnp.bool_(False)
    for j in range(spans):
        start = meta_ref[2 + j]
        found = found | ((start < edge) & (edge < start + PIC))
    return found


def block_rows(i, size):
    return pl.ds(pl.multiple_of(i * size, size), size)


def together(ring):
    return [list(range(ring))]


def leaving(ring):
    return [[1], list(range(2, ring)) + [0]]


def true_blocks(meta_ref, parts, ring, rows, groups):
    part, spot = meta_ref[0], meta_ref[1]
    for g, group in enumerate(groups):
        for at, k in enumerate(group):
            for e in range(parts):
                back = spot - k
                back = jnp.where(back < 0, back + ring, back)
                start = pl.multiple_of(((part ^ e) * ring + back) * rows, rows)
                yield g * parts + e, slice(at * rows, (at + 1) * rows), pl.ds(start, rows)


def prepare_block(b, size, heads, qkv_ref, slope_ref, kaug_ref, qaug_ref):
    rows = block_rows(b, size)
    lane = lax.broadcasted_iota(jnp.int32, (size, HD), 1)
    pos = b * size + lax.broadcasted_iota(jnp.int32, (size, HD), 0)
    ones = jnp.where(lane < 3, 1.0, 0.0).astype(BF)
    for h in range(heads):
        at = h * 3 * HD
        query = qkv_ref[rows, at : at + HD] * jnp.asarray(0.125, BF)
        key = qkv_ref[rows, at + HD : at + 2 * HD]
        offset = pos.astype(F32) * (slope_ref[h] * 0.125)
        high = offset.astype(BF).astype(F32)
        middle = (offset - high).astype(BF).astype(F32)
        low = offset - high - middle
        extra = jnp.where(
            lane == 0, high, jnp.where(lane == 1, middle, jnp.where(lane == 2, low, 0.0))
        ).astype(BF)
        qaug_ref[h, rows, :] = jnp.concatenate([query, ones], axis=1)
        kaug_ref[h, rows, :] = jnp.concatenate([key, extra], axis=1)


def forward_kernel(size, heads, parts, ring, rows, spans, meta_ref, slope_ref, *refs):
    piece_refs = refs[:parts]
    ctx_refs = refs[parts : 2 * parts]
    qkv_ref, out_t_ref, log_ref, kaug_ref, qaug_ref, vt_ref, top_ref, total_ref = refs[2 * parts :]
    length = qkv_ref.shape[0]
    blocks = length // size
    for i, block, dst in true_blocks(meta_ref, parts, ring, rows, together(ring)):
        qkv_ref[dst, :] = piece_refs[i][block, :]
    eye = (
        lax.broadcasted_iota(jnp.int32, (HD, HD), 0) == lax.broadcasted_iota(jnp.int32, (HD, HD), 1)
    ).astype(BF)

    def prepare(b, unused):
        prepare_block(b, size, heads, qkv_ref, slope_ref, kaug_ref, qaug_ref)
        cols = block_rows(b, size)
        for h in range(heads):
            at = h * 3 * HD + 2 * HD
            value = qkv_ref[cols, at : at + HD]
            vt_ref[h, :HD, cols] = dot_nt(eye, value).astype(BF)
            row = lax.broadcasted_iota(jnp.int32, (16, size), 0)
            vt_ref[h, HD:, cols] = jnp.where(row == 0, 1.0, 0.0).astype(BF)
        return unused

    lax.fori_loop(0, blocks, prepare, 0)

    for i in range(blocks):
        rows_i = slice(i * size, (i + 1) * size)
        allowed = allowed_block(i, i, size, meta_ref, spans)
        outs = []
        for h in range(heads):
            query = qaug_ref[h, rows_i, :]
            scores = dot_nt(kaug_ref[h, : (i + 1) * size, :], query)
            own = jnp.where(allowed, scores[i * size :], -1e30)
            top = jnp.max(own, axis=0, keepdims=True)
            if i:
                scores = scores[: i * size]
                top = jnp.maximum(top, jnp.max(scores, axis=0, keepdims=True))
            total = dot(vt_ref[h, :, rows_i], jnp.exp(own - top).astype(BF))
            if i:
                total = total + dot(
                    vt_ref[h, :, : i * size], jnp.exp(scores - top).astype(BF)
                )
            top_ref[h : h + 1, :] = top
            total_ref[h] = total

        if i < blocks - 1:

            @pl.when(crosses(i, size, meta_ref, spans))
            def _(i=i, rows_i=rows_i):
                allowed = allowed_block(i, i + 1, size, meta_ref, spans)
                for h in range(heads):
                    scores = dot_nt(
                        kaug_ref[h, (i + 1) * size : (i + 2) * size, :], qaug_ref[h, rows_i, :]
                    )
                    scores = jnp.where(allowed, scores, -1e30)
                    old_top = top_ref[h : h + 1, :]
                    top = jnp.maximum(old_top, jnp.max(scores, axis=0, keepdims=True))
                    weight = jnp.exp(scores - top).astype(BF)
                    total_ref[h] = total_ref[h] * jnp.exp(old_top - top) + dot(
                        vt_ref[h, :, (i + 1) * size : (i + 2) * size], weight
                    )
                    top_ref[h : h + 1, :] = top

        for h in range(heads):
            total = total_ref[h]
            amount = total[HD : HD + 1]
            outs.append(total[:HD] / amount)
            log_ref[h : h + 1, rows_i] = top_ref[h : h + 1, :] + jnp.log(amount)
        if heads * HD < 128:
            outs.append(jnp.zeros((128 - heads * HD, size), F32))
        out_t_ref[:, rows_i] = jnp.concatenate(outs, axis=0)

    for i, block, true_rows in true_blocks(meta_ref, parts, ring, rows, together(ring)):
        turned = out_t_ref[:, true_rows].T.astype(BF)
        ctx_refs[i][block, :] = turned[:, : heads * HD]


def backward_kernel(size, heads, parts, ring, rows, spans, meta_ref, slope_ref, *refs):
    piece_refs = refs[:parts]
    qkv_ref, out_t_ref, log_ref = refs[parts : parts + 3]
    grad_refs = refs[parts + 3 : 3 * parts + 3]
    (
        g_ref,
        kaug_ref,
        qaug_ref,
        kt_ref,
        gq_ref,
        gg_ref,
        delta_ref,
        dqt_ref,
        dkv_ref,
    ) = refs[3 * parts + 3 :]
    length = qkv_ref.shape[0]
    blocks = length // size
    for i, block, dst in true_blocks(meta_ref, parts, ring, rows, together(ring)):
        g_ref[dst, :] = piece_refs[i][block, :]
    eye = (
        lax.broadcasted_iota(jnp.int32, (HD, HD), 0) == lax.broadcasted_iota(jnp.int32, (HD, HD), 1)
    ).astype(BF)

    def prepare(b, unused):
        prepare_block(b, size, heads, qkv_ref, slope_ref, kaug_ref, qaug_ref)
        cols = block_rows(b, size)
        blank = jnp.zeros((size, HD), BF)
        grad_t = g_ref[cols, :].astype(F32)
        if heads * HD < 128:
            grad_t = jnp.concatenate([grad_t, jnp.zeros((size, 128 - heads * HD), F32)], axis=1)
        product = grad_t.T * out_t_ref[:, cols]
        for h in range(heads):
            at = h * 3 * HD
            kt_ref[h, :, cols] = dot_nt(eye, qkv_ref[cols, at + HD : at + 2 * HD]).astype(BF)
            query = qkv_ref[cols, at : at + HD] * jnp.asarray(0.125, BF)
            gq_ref[h, cols, :] = jnp.concatenate([blank, query], axis=1)
            gg_ref[h, cols, :] = jnp.concatenate([g_ref[cols, h * HD : (h + 1) * HD], blank], axis=1)
            delta_ref[h : h + 1, cols] = jnp.sum(
                product[h * HD : (h + 1) * HD], axis=0, keepdims=True
            )
        return unused

    lax.fori_loop(0, blocks, prepare, 0)

    def part_of(h, keys, queries, allowed):
        at = h * 3 * HD + 2 * HD
        scores = dot_nt(kaug_ref[h, keys, :], qaug_ref[h, queries, :])
        first = jnp.where(allowed, scores[:, :size], -1e30)
        if scores.shape[1] > size:
            scores = jnp.concatenate([first, scores[:, size:]], axis=1)
        else:
            scores = first
        weight = jnp.exp(scores - log_ref[h : h + 1, queries])
        grad_weight = dot_nt(qkv_ref[keys, at : at + HD], g_ref[queries, h * HD : (h + 1) * HD])
        grad_score = (weight * (grad_weight - delta_ref[h : h + 1, queries])).astype(BF)
        dkv = dot(weight.astype(BF), gg_ref[h, queries, :]) + dot(grad_score, gq_ref[h, queries, :])
        return dkv, dot(kt_ref[h, :, keys], grad_score)

    for j in range(blocks):
        keys = slice(j * size, (j + 1) * size)
        queries = slice(j * size, length)
        allowed = allowed_block(j, j, size, meta_ref, spans)
        for h in range(heads):
            dkv, dq = part_of(h, keys, queries, allowed)
            dkv_ref[h, keys, :] = dkv
            rows_h = slice(h * HD, (h + 1) * HD)
            if j:
                dq = dq + dqt_ref[rows_h, queries]
            dqt_ref[rows_h, queries] = dq

        if j:

            @pl.when(crosses(j - 1, size, meta_ref, spans))
            def _(j=j, keys=keys):
                queries = slice((j - 1) * size, j * size)
                allowed = allowed_block(j - 1, j, size, meta_ref, spans)
                for h in range(heads):
                    dkv, dq = part_of(h, keys, queries, allowed)
                    dkv_ref[h, keys, :] += dkv
                    dqt_ref[h * HD : (h + 1) * HD, queries] += dq

    for i, block, true_rows in true_blocks(meta_ref, parts, ring, rows, leaving(ring)):
        columns = []
        grad_q = (dqt_ref[:, true_rows] * 0.125).T
        for h in range(heads):
            dkv = dkv_ref[h, true_rows, :]
            columns += [grad_q[:, h * HD : (h + 1) * HD], dkv[:, HD:], dkv[:, :HD]]
        grad_refs[i][block, :] = jnp.concatenate(columns, axis=1).astype(BF)


def specs(count_smem, count_vmem):
    return [pl.BlockSpec(memory_space=pltpu.SMEM)] * count_smem + [
        pl.BlockSpec(memory_space=pltpu.VMEM)
    ] * count_vmem


def attend_forward(pieces, meta, slopes, ring, rows):
    heads = slopes.shape[0]
    parts = len(pieces)
    length = parts * pieces[0].shape[0]
    wide = max(128, heads * HD)
    outs = pl.pallas_call(
        functools.partial(forward_kernel, FORWARD_BLOCK, heads, parts, ring, rows, meta.shape[0] - 2),
        out_shape=tuple(
            [jax.ShapeDtypeStruct((length // parts, heads * HD), BF)] * parts
            + [
                jax.ShapeDtypeStruct((length, heads * 3 * HD), BF),
                jax.ShapeDtypeStruct((wide, length), F32),
                jax.ShapeDtypeStruct((8, length), F32),
            ]
        ),
        in_specs=specs(2, parts),
        out_specs=tuple(specs(0, parts + 3)),
        scratch_shapes=[
            pltpu.VMEM((heads, length, 128), BF),
            pltpu.VMEM((heads, length, 128), BF),
            pltpu.VMEM((heads, HD + 16, length), BF),
            pltpu.VMEM((8, FORWARD_BLOCK), F32),
            pltpu.VMEM((heads, HD + 16, FORWARD_BLOCK), F32),
        ],
        compiler_params=pltpu.CompilerParams(vmem_limit_bytes=VMEM_BYTES),
        cost_estimate=pl.CostEstimate(
            flops=2 * US, bytes_accessed=length * heads * HD * 20, transcendentals=0
        ),
    )(meta, slopes, *pieces)
    return list(outs[:parts]), *outs[parts:]


def attend_backward(pieces, qkv, out_t, logs, meta, slopes, ring, rows):
    heads = slopes.shape[0]
    parts = len(pieces)
    length = qkv.shape[0]
    wide = max(128, heads * HD)
    outs = pl.pallas_call(
        functools.partial(backward_kernel, BACKWARD_BLOCK, heads, parts, ring, rows, meta.shape[0] - 2),
        out_shape=tuple(
            jax.ShapeDtypeStruct((len(group) * rows, heads * 3 * HD), BF)
            for group in leaving(ring)
            for unused in range(parts)
        ),
        in_specs=specs(2, parts + 3),
        out_specs=tuple(specs(0, 2 * parts)),
        scratch_shapes=[
            pltpu.VMEM((length, heads * HD), BF),
            pltpu.VMEM((heads, length, 128), BF),
            pltpu.VMEM((heads, length, 128), BF),
            pltpu.VMEM((heads, HD, length), BF),
            pltpu.VMEM((heads, length, 128), BF),
            pltpu.VMEM((heads, length, 128), BF),
            pltpu.VMEM((8, length), F32),
            pltpu.VMEM((wide, length), F32),
            pltpu.VMEM((heads, length, 128), F32),
        ],
        compiler_params=pltpu.CompilerParams(vmem_limit_bytes=VMEM_BYTES),
        cost_estimate=pl.CostEstimate(
            flops=2 * US, bytes_accessed=length * heads * HD * 20, transcendentals=0
        ),
    )(meta, slopes, *pieces, qkv, out_t, logs)
    return list(outs[:parts]), list(outs[parts:])


def take_columns(ref, part, e, width):
    def each(use):
        if width % 128 == 0:
            start = pl.multiple_of((part ^ e) * width, width)
            use(ref.at[:, pl.ds(start, width)])
        else:
            for p in range(SEQ_DEVS):

                @pl.when(part == p)
                def _():
                    use(ref.at[:, pl.ds((p ^ e) * width, width)])

    return each


def column_loop(total, body):
    step = min(256, total)

    def one(i, unused):
        body(pl.ds(pl.multiple_of(i * step, step), step))
        return unused

    lax.fori_loop(0, total // step, one, 0)


def in_hbm(pieces):
    return [pltpu.with_memory_space_constraint(piece, pltpu.HBM) for piece in pieces]


def load_weights(w_pieces, w_ref, sems, starts_ref):
    copies = []
    for i, piece in enumerate(w_pieces):
        count = piece.shape[0]
        start = pl.multiple_of(starts_ref[i], min(128, count))
        copy = pltpu.make_async_copy(piece, w_ref.at[pl.ds(start, count), :], sems.at[i])
        copy.start()
        copies.append(copy)
    return copies


def load_shards(w_pieces, w_ref, sems, places_ref):
    copies = []
    for i, piece in enumerate(w_pieces):
        if len(piece.shape) == 3:
            copy = pltpu.make_async_copy(piece, w_ref, sems.at[i])
        else:
            count = piece.shape[0]
            start = pl.multiple_of(places_ref[2 * i + 1], count)
            target = w_ref.at[places_ref[2 * i], pl.ds(start, count), :]
            copy = pltpu.make_async_copy(piece, target, sems.at[i])
        copy.start()
        copies.append(copy)
    return copies


def normed_rows(rows_ref, gain_ref, shift_ref):
    return norm_forward(rows_ref[...].astype(F32), gain_ref[...], shift_ref[...])[0].astype(BF)


def prepare_qkv_kernel(count, starts_ref, *refs):
    h_pieces, refs = refs[:count], refs[count:]
    gain_ref, shift_ref, w_pieces, (w_ref, x_ref, sems) = refs[0], refs[1], refs[2:-3], refs[-3:]
    copies = load_weights(w_pieces, w_ref, sems, starts_ref)
    rows = h_pieces[0].shape[0]
    for k in range(count):
        x_ref[k * rows : (k + 1) * rows, :] = normed_rows(h_pieces[k], gain_ref, shift_ref)
    for copy in copies:
        copy.wait()


def prepare_qkv(h_pieces, gain, shift, w_pieces, starts):
    count, n_w = len(h_pieces), len(w_pieces)
    rows, depth = h_pieces[0].shape
    cols = w_pieces[0].shape[1]
    return pl.pallas_call(
        functools.partial(prepare_qkv_kernel, count),
        out_shape=[pltpu.VMEM((depth, cols), BF), pltpu.VMEM((count * rows, depth), BF)],
        in_specs=specs(1, count + 2) + [pl.BlockSpec(memory_space=pl.ANY)] * n_w,
        out_specs=specs(0, 2),
        scratch_shapes=[pltpu.SemaphoreType.DMA((n_w,))],
        compiler_params=pltpu.CompilerParams(vmem_limit_bytes=SMALL_VMEM_BYTES),
        cost_estimate=pl.CostEstimate(flops=3 * US, bytes_accessed=2**20, transcendentals=0),
    )(starts, *h_pieces, gain, shift, *in_hbm(w_pieces))


def qkv_kernel(meta_ref, first_ref, last_ref, gain_ref, shift_ref, a_ref, b_ref, bias_ref, *refs):
    w_ref, q_refs, (u_ref, x_ref, o_ref) = refs[0], refs[1 : 1 + SEQ_DEVS], refs[1 + SEQ_DEVS :]
    before = first_ref.shape[0]
    x_ref[:before, :] = first_ref[...]
    x_ref[before:, :] = normed_rows(last_ref, gain_ref, shift_ref)
    u_ref[...] = dot_nt(x_ref[...], a_ref[...]).astype(BF)

    def body(cols):
        total = dot(x_ref[...], w_ref[:, cols])
        total = total + FACTOR * dot(u_ref[...], b_ref[:, cols]) + bias_ref[:, cols]
        o_ref[:, cols] = total.astype(BF)

    column_loop(o_ref.shape[1], body)
    for e in range(SEQ_DEVS):

        def store(src, e=e):
            q_refs[e][...] = src[...]

        take_columns(o_ref, meta_ref[0], e, q_refs[e].shape[1])(store)


def qkv_product(first, last, gain, shift, a, b, bias, w, meta):
    count, depth = first.shape[0] + last.shape[0], first.shape[1]
    cols = b.shape[1]
    outs = pl.pallas_call(
        qkv_kernel,
        out_shape=tuple(
            [jax.ShapeDtypeStruct((count, cols // SEQ_DEVS), BF)] * SEQ_DEVS
            + [
                jax.ShapeDtypeStruct((count, a.shape[0]), BF),
                jax.ShapeDtypeStruct((count, depth), BF),
            ]
        ),
        in_specs=specs(1, 8),
        out_specs=tuple(specs(0, SEQ_DEVS + 2)),
        scratch_shapes=[pltpu.VMEM((count, cols), BF)],
        compiler_params=pltpu.CompilerParams(vmem_limit_bytes=SMALL_VMEM_BYTES),
        cost_estimate=pl.CostEstimate(flops=2 * US, bytes_accessed=2**20, transcendentals=0),
    )(meta, first, last, gain, shift, a, b, bias, w)
    return list(outs[:SEQ_DEVS]), outs[SEQ_DEVS], outs[SEQ_DEVS + 1]


def load_kernel(first_ref, second_ref, first_out, second_out, sems):
    shards, half = first_ref.shape[0], first_ref.shape[1]
    depth = second_ref.shape[2]
    chunks = first_out.shape[1] // depth
    copies = []

    def copy(src, dst):
        copies.append(pltpu.make_async_copy(src, dst, sems.at[len(copies)]))

    for i in range(shards):
        copy(first_ref.at[i], first_out.at[pl.ds(2 * i * half, half), :])
        for h in range(chunks):
            copy(
                second_ref.at[i, pl.ds(h * half, half)],
                first_out.at[pl.ds((2 * i + 1) * half, half), pl.ds(h * depth, depth)],
            )
        copy(second_ref.at[i, pl.ds(chunks * half, chunks * depth)], second_out.at[i])
    for each in copies:
        each.start()
    for each in copies:
        each.wait()


def load_to_vmem(first, second):
    shards, half, hidden = first.shape
    chunks = hidden // second.shape[2]
    return pl.pallas_call(
        load_kernel,
        out_shape=[
            pltpu.VMEM((shards * half * 2, hidden), BF),
            pltpu.VMEM((shards, hidden, second.shape[2]), BF),
        ],
        in_specs=[pl.BlockSpec(memory_space=pl.ANY)] * 2,
        out_specs=[pl.BlockSpec(memory_space=pltpu.VMEM)] * 2,
        scratch_shapes=[pltpu.SemaphoreType.DMA((shards * (chunks + 2),))],
        compiler_params=pltpu.CompilerParams(vmem_limit_bytes=2 * 1024 * 1024),
        cost_estimate=pl.CostEstimate(flops=5 * US, bytes_accessed=2**20, transcendentals=0),
    )(*[pltpu.with_memory_space_constraint(w, pltpu.HBM) for w in (first, second)])


def store_rows(refs, cols, total):
    at = 0
    for ref in refs:
        ref[:, cols] = total[at : at + ref.shape[0]]
        at += ref.shape[0]


def out_kernel(ring, n_w, meta_ref, places_ref, *refs):
    c_pieces = refs[:SEQ_DEVS]
    a_ref, b_ref = refs[SEQ_DEVS : SEQ_DEVS + 2]
    w_pieces, refs = refs[SEQ_DEVS + 2 : SEQ_DEVS + 2 + n_w], refs[SEQ_DEVS + 2 + n_w :]
    p_refs = refs[:ring]
    ctx_ref, u_ref, w_ref, sems = refs[ring:]
    copies = load_shards(w_pieces, w_ref, sems, places_ref)
    width = c_pieces[0].shape[1]
    for e in range(SEQ_DEVS):

        def store(dst, e=e):
            dst[...] = c_pieces[e][...]

        take_columns(ctx_ref, meta_ref[0], e, width)(store)
    u_ref[...] = dot_nt(ctx_ref[...], a_ref[...]).astype(BF)
    for copy in copies:
        copy.wait()
    shards, unused, wide = w_ref.shape
    for j in range(shards):
        cols = slice(j * wide, (j + 1) * wide)
        total = dot(ctx_ref[...], w_ref[j]) + FACTOR * dot(u_ref[...], b_ref[:, cols])
        store_rows(p_refs, cols, total.astype(BF))


def paired(pieces):
    return [list(pieces[i : i + 2]) for i in range(0, len(pieces), 2)]


def out_product(c_pieces, a, b, w_pieces, places, meta, ring, shards):
    count, width = c_pieces[0].shape
    rank, depth = b.shape
    n_w = len(w_pieces)
    outs = pl.pallas_call(
        functools.partial(out_kernel, 2 * ring, n_w),
        out_shape=tuple(
            [jax.ShapeDtypeStruct((count // ring // 2, depth), BF)] * (2 * ring)
            + [
                jax.ShapeDtypeStruct((count, width * SEQ_DEVS), BF),
                jax.ShapeDtypeStruct((count, rank), BF),
            ]
        ),
        in_specs=specs(2, SEQ_DEVS + 2) + [pl.BlockSpec(memory_space=pl.ANY)] * n_w,
        out_specs=tuple(specs(0, 2 * ring + 2)),
        scratch_shapes=[
            pltpu.VMEM((shards, width * SEQ_DEVS, depth // shards), BF),
            pltpu.SemaphoreType.DMA((n_w,)),
        ],
        compiler_params=pltpu.CompilerParams(vmem_limit_bytes=VMEM_BYTES),
        cost_estimate=pl.CostEstimate(flops=3 * US, bytes_accessed=2**20, transcendentals=0),
    )(meta, places, *c_pieces, a, b, *w_pieces)
    return paired(outs[: 2 * ring]), outs[2 * ring], outs[2 * ring + 1]


def mlp_kernel(count, add, *refs):
    n2_refs, (gy_ref, a1_ref, b2_ref, b1_ref, a2_ref, bias_ref), refs = (
        refs[:count],
        refs[count : count + 6],
        refs[count + 6 :],
    )
    w1_ref, w2_ref, before, refs = refs[0], refs[1], refs[2 : 2 + add], refs[2 + add :]
    p_refs, m_ref, grads = refs[:count], refs[count], refs[count + 1 : count + 5]
    x_ref, act_ref, slope_ref, gf_ref = refs[count + 5 :]
    shards, hidden, wide = w2_ref.shape
    at = 0
    for ref in n2_refs:
        x_ref[at : at + ref.shape[0], :] = ref[...]
        at += ref.shape[0]
    u3 = dot_nt(x_ref[...], a1_ref[...]).astype(BF)
    gu4 = (FACTOR * dot_nt(gy_ref[...], b2_ref[...])).astype(BF)
    for h in range(0, hidden, wide):
        cols = slice(h, h + wide)
        f = dot(x_ref[...], w1_ref[:, cols])
        f = f + FACTOR * dot(u3, b1_ref[:, cols]) + bias_ref[:, cols]
        act, slope = gelu_and_slope(f)
        act_ref[:, cols] = act.astype(BF)
        slope_ref[:, cols] = slope
    for h in range(0, hidden, wide):
        cols = slice(h, h + wide)
        gact = dot(gu4, a2_ref[:, cols])
        for j in range(shards):
            gact = gact + dot_nt(gy_ref[:, j * wide : (j + 1) * wide], w2_ref[j, cols, :])
        gf_ref[:, cols] = (gact * slope_ref[:, cols]).astype(BF)
    gu3 = (FACTOR * dot_nt(gf_ref[...], b1_ref[...])).astype(BF)
    for j in range(shards):
        cols = slice(j * wide, (j + 1) * wide)
        total = dot_nt(gf_ref[...], w1_ref[cols, :]) + dot(gu3, a1_ref[:, cols])
        store_rows(p_refs, cols, total.astype(BF))
    u4 = dot_nt(act_ref[...], a2_ref[...]).astype(BF)
    for j in range(shards):
        cols = slice(j * wide, (j + 1) * wide)
        total = dot(act_ref[...], w2_ref[j]) + FACTOR * dot(u4, b2_ref[:, cols])
        m_ref[:, cols] = total.astype(BF)
    products = [
        FACTOR * dot_tn(u3, gf_ref[...]),
        dot_tn(gu4, act_ref[...]),
        dot_tn(gu3, x_ref[...]),
        FACTOR * dot_tn(u4, gy_ref[...]),
    ]
    for i, product in enumerate(products):
        grads[i][...] = product + before[i][...] if add else product


def mlp_both_ways(n2_pieces, gy, a1, b1, a2, b2, bias, weights, before):
    count = len(n2_pieces)
    total, depth = gy.shape
    rank, hidden = b1.shape
    outs = pl.pallas_call(
        functools.partial(mlp_kernel, count, len(before)),
        out_shape=(
            [jax.ShapeDtypeStruct(piece.shape, BF) for piece in n2_pieces]
            + [jax.ShapeDtypeStruct((total, depth), BF)]
            + [jax.ShapeDtypeStruct((rank, hidden), F32)] * 2
            + [jax.ShapeDtypeStruct((rank, depth), F32)] * 2
        ),
        in_specs=specs(0, count + 8 + len(before)),
        out_specs=specs(0, count + 5),
        scratch_shapes=[
            pltpu.VMEM((total, depth), BF),
            pltpu.VMEM((total, hidden), BF),
            pltpu.VMEM((total, hidden), F32),
            pltpu.VMEM((total, hidden), BF),
        ],
        compiler_params=pltpu.CompilerParams(vmem_limit_bytes=SMALL_VMEM_BYTES),
        cost_estimate=pl.CostEstimate(
            flops=10 * US, bytes_accessed=4 * depth * hidden, transcendentals=0
        ),
    )(*n2_pieces, gy, a1, b2, b1, a2, bias, *weights, *before)
    return list(outs[:count]), outs[count], list(outs[count + 1 :])


def pack_into(full, own, ring, groups, meta_ref, out_ref):
    part, spot = meta_ref[0], meta_ref[1]
    wide = out_ref.shape[4]
    at = 0
    for ref in full:
        width = ref.shape[1] // (ring * SEQ_DEVS * groups)
        for g in range(groups):
            for p in range(SEQ_DEVS):
                for z in range(ring):
                    k = z - spot
                    k = jnp.where(k < 0, k + ring, k)
                    column = ((g * SEQ_DEVS + p) * ring + z) * width
                    out_ref[part ^ p, k, g, :, at : at + width] = ref[
                        :, column : column + width
                    ].astype(BF)
        at += width
    at = 0
    for ref in own:
        width = ref.shape[1] // (SEQ_DEVS * groups)
        for p in range(SEQ_DEVS):
            for r in range(groups):
                column = (p * groups + r) * width
                out_ref[part ^ p, ring + at // wide, r, :, at % wide : at % wide + width] = ref[
                    :, column : column + width
                ].astype(BF)
        at += width


def pack_shapes(full_cols, own_cols, rank, ring, groups):
    full_widths = [c // (ring * SEQ_DEVS * groups) for c in full_cols]
    own_widths = [c // (SEQ_DEVS * groups) for c in own_cols]
    wide = sum(full_widths)
    rows = ring + sum(own_widths) // wide
    shapes = [jax.ShapeDtypeStruct((SEQ_DEVS, rows, groups, rank, wide), BF)]
    return shapes, full_widths, own_widths


def gctx_kernel(n_g, n_w, meta_ref, places_ref, *refs):
    g_pieces, refs = refs[:n_g], refs[n_g:]
    a_ref, b_ref, ctx_ref, u2_ref = refs[:4]
    w_pieces, refs = refs[4 : 4 + n_w], refs[4 + n_w :]
    c_refs = refs[:SEQ_DEVS]
    gbo_ref, gao_ref, g_ref, o_ref, w_ref, sems = refs[SEQ_DEVS:]
    copies = load_shards(w_pieces, w_ref, sems, places_ref)
    rows = g_pieces[0].shape[0]
    for k in range(n_g):
        g_ref[k * rows : (k + 1) * rows, :] = g_pieces[k][...]
    gu2 = (FACTOR * dot_nt(g_ref[...], b_ref[...])).astype(BF)
    shards, unused, wide = w_ref.shape
    total = dot(gu2, a_ref[...])
    gbo_ref[...] = FACTOR * dot_tn(u2_ref[...], g_ref[...])
    gao_ref[...] = dot_tn(gu2, ctx_ref[...])
    for copy in copies:
        copy.wait()
    for j in range(shards):
        total = total + dot_nt(g_ref[:, j * wide : (j + 1) * wide], w_ref[j])
    o_ref[...] = total.astype(BF)
    for e in range(SEQ_DEVS):

        def store(src, e=e):
            c_refs[e][...] = src[...]

        take_columns(o_ref, meta_ref[0], e, c_refs[e].shape[1])(store)


def gctx_product(g_pieces, a, b, w_pieces, places, ctx, u2, meta, shards):
    n_g, n_w = len(g_pieces), len(w_pieces)
    depth = g_pieces[0].shape[1]
    count, cols = ctx.shape
    rank = a.shape[0]
    outs = pl.pallas_call(
        functools.partial(gctx_kernel, n_g, n_w),
        out_shape=tuple(
            [jax.ShapeDtypeStruct((count, cols // SEQ_DEVS), BF)] * SEQ_DEVS
            + [jax.ShapeDtypeStruct((rank, depth), F32), jax.ShapeDtypeStruct((rank, cols), F32)]
        ),
        in_specs=specs(2, n_g + 4) + [pl.BlockSpec(memory_space=pl.ANY)] * n_w,
        out_specs=tuple(specs(0, SEQ_DEVS + 2)),
        scratch_shapes=[
            pltpu.VMEM((count, depth), BF),
            pltpu.VMEM((count, cols), BF),
            pltpu.VMEM((shards, cols, depth // shards), BF),
            pltpu.SemaphoreType.DMA((n_w,)),
        ],
        compiler_params=pltpu.CompilerParams(vmem_limit_bytes=VMEM_BYTES),
        cost_estimate=pl.CostEstimate(flops=3 * US, bytes_accessed=2**20, transcendentals=0),
    )(meta, places, *g_pieces, a, b, ctx, u2, *w_pieces)
    return list(outs[:SEQ_DEVS]), outs[SEQ_DEVS], outs[SEQ_DEVS + 1]


def near_kernel(starts_ref, *refs):
    w_pieces, w_ref, sems = refs[:-2], refs[-2], refs[-1]
    for copy in load_weights(w_pieces, w_ref, sems, starts_ref):
        copy.wait()


def load_rows_to_vmem(w_pieces, starts, shape):
    n_w = len(w_pieces)
    return pl.pallas_call(
        near_kernel,
        out_shape=pltpu.VMEM(shape, BF),
        in_specs=specs(1, 0) + [pl.BlockSpec(memory_space=pl.ANY)] * n_w,
        out_specs=specs(0, 1)[0],
        scratch_shapes=[pltpu.SemaphoreType.DMA((n_w,))],
        compiler_params=pltpu.CompilerParams(vmem_limit_bytes=2 * 1024 * 1024),
        cost_estimate=pl.CostEstimate(flops=2 * US, bytes_accessed=2**20, transcendentals=0),
    )(starts, *in_hbm(w_pieces))


def gather_columns(q_pieces, q_ref, meta_ref):
    for e in range(SEQ_DEVS):

        def store(dst, e=e):
            dst[...] = q_pieces[e][...]

        take_columns(q_ref, meta_ref[0], e, q_pieces[e].shape[1])(store)


def gn1_rows(q_ref, gu1, a_ref, w_ref, p_refs):
    def body(cols):
        total = dot_nt(q_ref[...], w_ref[cols, :]) + dot(gu1, a_ref[:, cols])
        store_rows(p_refs, cols, total.astype(BF))

    column_loop(w_ref.shape[0], body)


def gn1_first_kernel(meta_ref, *refs):
    q_pieces, (a_ref, b_ref, w_ref), refs = refs[:SEQ_DEVS], refs[SEQ_DEVS : SEQ_DEVS + 3], refs[SEQ_DEVS + 3 :]
    *p_refs, q_ref, gu_ref = refs
    gather_columns(q_pieces, q_ref, meta_ref)
    gu_ref[...] = (FACTOR * dot_nt(q_ref[...], b_ref[...])).astype(BF)
    gn1_rows(q_ref, gu_ref[...], a_ref, w_ref, p_refs)


def gn1_first(q_pieces, a, b, w, meta):
    rows = q_pieces[0].shape[0]
    rank, depth = a.shape
    outs = pl.pallas_call(
        gn1_first_kernel,
        out_shape=[jax.ShapeDtypeStruct((rows // 2, depth), BF)] * 2
        + [jax.ShapeDtypeStruct((rows, b.shape[1]), BF), jax.ShapeDtypeStruct((rows, rank), BF)],
        in_specs=specs(1, SEQ_DEVS + 3),
        out_specs=specs(0, 4),
        compiler_params=pltpu.CompilerParams(vmem_limit_bytes=SMALL_VMEM_BYTES),
        cost_estimate=pl.CostEstimate(flops=3 * US, bytes_accessed=2**20, transcendentals=0),
    )(meta, *q_pieces, a, b, w)
    return list(outs[:2]), outs[2], outs[3]


def gn1_rest_kernel(ring, groups, blocks, meta_ref, *refs):
    q_pieces, refs = refs[:SEQ_DEVS], refs[SEQ_DEVS:]
    q1_ref, gu1_ref, x_ref, u_ref, a_ref, b_ref, w_ref = refs[:7]
    full, own, p_refs, refs = refs[7:10], refs[10:13], refs[13 : 13 + blocks], refs[13 + blocks :]
    out_ref, q_ref, gb_ref, ga_ref = refs
    rows = q1_ref.shape[0]
    gather_columns(q_pieces, q_ref, meta_ref)
    gu1 = (FACTOR * dot_nt(q_ref[...], b_ref[...])).astype(BF)
    gn1_rows(q_ref, gu1, a_ref, w_ref, p_refs)
    here = slice(rows, 2 * rows)
    x = jnp.concatenate([x_ref[2 * rows :, :], x_ref[:rows, :]], axis=0)
    u = jnp.concatenate([u_ref[2 * rows :, :], u_ref[:rows, :]], axis=0)
    gb_ref[...] = FACTOR * (dot_tn(u, q_ref[...]) + dot_tn(u_ref[here, :], q1_ref[...]))
    ga_ref[...] = dot_tn(gu1, x) + dot_tn(gu1_ref[...], x_ref[here, :])
    pack_into([ga_ref, *full], [gb_ref, *own], ring, groups, meta_ref, out_ref)


def gn1_rest(q_pieces, q1, gu1, n1, u1, a, b, w, full, own, meta, ring, groups):
    count = q_pieces[0].shape[0]
    rank, depth = a.shape
    cols = b.shape[1]
    rows = q1.shape[0]
    blocks = 2 * count // rows
    shapes, full_widths, own_widths = pack_shapes(
        [depth] + [g.shape[1] for g in full],
        [cols] + [g.shape[1] for g in own],
        rank,
        ring,
        groups,
    )
    outs = pl.pallas_call(
        functools.partial(gn1_rest_kernel, ring, groups, blocks),
        out_shape=[jax.ShapeDtypeStruct((rows // 2, depth), BF)] * blocks + shapes,
        in_specs=specs(1, SEQ_DEVS + 13),
        out_specs=specs(0, blocks + 1),
        scratch_shapes=[
            pltpu.VMEM((count, cols), BF),
            pltpu.VMEM((rank, cols), F32),
            pltpu.VMEM((rank, depth), F32),
        ],
        compiler_params=pltpu.CompilerParams(vmem_limit_bytes=SMALL_VMEM_BYTES),
        cost_estimate=pl.CostEstimate(flops=6 * US, bytes_accessed=2**20, transcendentals=0),
    )(meta, *q_pieces, q1, gu1, n1, u1, a, b, w, *full, *own)
    stages = functools.partial(
        reduce_stages, full_widths=full_widths, own_widths=own_widths, groups=groups
    )
    return paired(outs[:blocks]), Side(list(outs[blocks:]), stages)


def reduce_stages(packed, full_widths, own_widths, groups):
    ring, n = lax.axis_size("tensor"), lax.axis_size("dp")
    group = lax.axis_index("dp") // SEQ_DEVS
    landed = yield [exchange(packed[e], e) for e in range(1, SEQ_DEVS)]
    total = sum([x.astype(F32) for x in landed], packed[0].astype(F32)).astype(BF)

    def block(array, k):
        return lax.dynamic_index_in_dim(array, (group + k) % groups, -3, keepdims=False)

    flying = [
        lax.ppermute(total[k], "tensor", [(i, (i + k) % ring) for i in range(ring)])
        for k in range(1, ring)
    ]
    for k in range(groups):
        pairs = []
        for i in range(n):
            for z in range(ring):
                r = (i // SEQ_DEVS + k) % groups
                pairs.append((i * ring + z, z * n + (i % SEQ_DEVS) * groups + r))
        flying.append(lax.ppermute(block(total[ring:], k), ("dp", "tensor"), pairs))
    landed = yield flying
    own = list(landed[ring - 1 :])
    total = sum([x.astype(F32) for x in landed[: ring - 1]], total[0].astype(F32)).astype(BF)
    flying = []
    for k in range(1, groups):
        pairs = [(i, (i + k * SEQ_DEVS) % n) for i in range(n)]
        flying.append(lax.ppermute(block(total, k), "dp", pairs))
    landed = yield flying
    return ([block(total, 0)] + list(landed), full_widths), (own, own_widths)


def place_kernel(n_full, n_own, full_widths, own_widths, home_ref, adapter_ref, *refs):
    outs = refs[n_full + n_own :]
    for out in outs:
        out[...] = jnp.zeros(out.shape, F32)
    for i, ref in enumerate(refs[: n_full + n_own]):
        k = i if i < n_full else i - n_full
        sequence = home_ref[int(i >= n_full)] - k
        sequence = jnp.where(sequence < 0, sequence + n_full, sequence)
        slot, at = adapter_ref[sequence], 0
        targets = outs[: len(full_widths)] if i < n_full else outs[len(full_widths) :]
        for out, width in zip(targets, full_widths if i < n_full else own_widths):
            if i < n_full:
                columns = ref[:, at : at + width]
            else:
                wide = ref.shape[2]
                columns = ref[at // wide, :, at % wide : at % wide + width]
            out[slot] = out[slot] + columns.astype(F32)
            at += width


def place(full, full_widths, own, own_widths, home, seq_adapter):
    rank = full[0].shape[0]
    widths = full_widths + own_widths
    return pl.pallas_call(
        functools.partial(place_kernel, len(full), len(own), full_widths, own_widths),
        out_shape=[jax.ShapeDtypeStruct((ADAPTERS, rank, w), F32) for w in widths],
        in_specs=specs(2, len(full) + len(own)),
        out_specs=specs(0, len(widths)),
        compiler_params=pltpu.CompilerParams(vmem_limit_bytes=VMEM_BYTES),
        cost_estimate=pl.CostEstimate(flops=US, bytes_accessed=2**20, transcendentals=0),
    )(home, seq_adapter, *full, *own)


def gather_first(shard, rows_in, data, small):
    n, count = lax.axis_size("dp"), shard.shape[0]
    if n != 8 or lax.axis_size("tensor") != 4:
        whole = lax.all_gather(shard, "dp", axis=0, tiled=True)
        return [whole], [0 * data], ring_gather(rows_in, "tensor"), small
    half = count // 2
    by_x, by_y, by_c = exchange(shard, 2), exchange(shard, 4), exchange(shard, 1)
    ring = [rows_in, shift_one(rows_in, "tensor")]
    by_x, by_y, by_c, ring[1], *small = lax.optimization_barrier(
        (by_x, by_y, by_c, ring[1]) + small
    )
    corner_a, corner_b = exchange(by_x[:half], 4), exchange(by_y[half:], 2)
    by_xc, by_yc = exchange(by_x, 1), exchange(by_y, 1)
    ring.append(shift_one(ring[1], "tensor"))
    corner_a, corner_b, by_xc, by_yc, ring[2], small[:2] = lax.optimization_barrier(
        (corner_a, corner_b, by_xc, by_yc, ring[2], small[:2])
    )
    far_a, far_b = exchange(corner_a, 1), exchange(corner_b, 1)
    ring.append(shift_one(ring[2], "tensor"))
    pieces = [shard, by_c, by_x, by_xc, by_y, by_yc, corner_a, far_a, corner_b, far_b]
    starts = [(data ^ e) * count for e in range(8)]
    starts += [(data ^ e) * count + half for e in (6, 7)]
    return pieces, starts, ring, small


def gather_shards(shard, data):
    stages = shard_stages(data)
    next(stages)
    return stages


def shard_stages(data):
    n = lax.axis_size("dp")
    shard = yield None
    if n != 8:
        landed = yield [lax.all_gather(shard, "dp", axis=0, tiled=False)]
        landed = yield landed
        landed = yield landed
        yield landed
        return
    half = shard.shape[0] // 2
    by_x, by_y, by_c = yield [exchange(shard, 2), exchange(shard, 4), exchange(shard, 1)]
    sent = [exchange(by_x[:half], 4), exchange(by_y[half:], 2), exchange(by_x, 1), exchange(by_y, 1)]
    corner_a, corner_b, by_xc, by_yc = yield sent
    far_a, far_b = yield [exchange(corner_a, 1), exchange(corner_b, 1)]
    pieces = [shard, by_c, by_x, by_xc, by_y, by_yc, corner_a, far_a, corner_b, far_b]
    yield pieces


def shard_places(shard, data):
    if lax.axis_size("dp") != 8:
        return jnp.zeros((2,), jnp.int32)
    half = shard.shape[0] // 2
    places = [(data ^ e, 0 * data) for e in range(8)] + [(data ^ e, 0 * data + half) for e in (6, 7)]
    return jnp.stack([p for place in places for p in place]).astype(jnp.int32)


def swap_start(pieces):
    return [exchange(pieces[2], 2), exchange(pieces[3], 2), exchange(pieces[1], 1)]


def swap_end(pieces, landed):
    across, far, near = landed
    return [pieces[0], near, across, exchange(far, 1)]


def swap_heads(pieces, beside=()):
    across, far, near = exchange(pieces[2], 2), exchange(pieces[3], 2), exchange(pieces[1], 1)
    across, far, near, beside = lax.optimization_barrier((across, far, near, beside))
    return [pieces[0], near, across, exchange(far, 1)], beside


def local(
    hidden_in,
    ln1_gain,
    ln1_bias,
    qkv_weight,
    joined_bias,
    out_weight,
    output_bias,
    ln2_gain,
    ln2_bias,
    fc1_weight,
    first_feed_bias,
    fc2_weight,
    second_feed_bias,
    qkv_down,
    qkv_up,
    out_down,
    out_up,
    fc1_down,
    fc1_up,
    fc2_down,
    fc2_up,
    seq_adapter,
    span_starts,
    cotangent,
):
    spot = lax.axis_index("tensor")
    data = lax.axis_index("dp")
    ring = lax.axis_size("tensor")
    groups = lax.axis_size("dp") // SEQ_DEVS
    group, part = data // SEQ_DEVS, data % SEQ_DEVS
    rows = hidden_in.shape[0]
    slot = lax.dynamic_index_in_dim(seq_adapter, group, 0, keepdims=False)
    starts = lax.dynamic_index_in_dim(span_starts, group, 0, keepdims=False)
    qkv_cols, ctx_cols, hidden_cols = qkv_weight.shape[1], out_weight.shape[0], fc1_weight.shape[1]
    heads = qkv_cols // (3 * HD) // SEQ_DEVS
    meta = jnp.concatenate([jnp.stack([part, spot]), starts]).astype(jnp.int32)
    first_head = (spot * SEQ_DEVS + part) * heads
    slopes = jnp.exp2(
        -8.0 * ((first_head + jnp.arange(heads, dtype=jnp.int32)).astype(F32) + 1.0) / H
    )

    def pick(stack):
        return lax.dynamic_index_in_dim(stack, slot, 0, keepdims=False)

    def own_cols(matrix, count):
        return lax.dynamic_slice_in_dim(matrix, spot * count, count, 1)

    a_q, b_q = pick(qkv_down), own_cols(pick(qkv_up), qkv_cols)
    a_o, b_o = own_cols(pick(out_down), ctx_cols), pick(out_up)
    a_1, b_1 = pick(fc1_down), own_cols(pick(fc1_up), hidden_cols)
    a_2, b_2 = own_cols(pick(fc2_down), hidden_cols), pick(fc2_up)

    n = lax.axis_size("dp")
    shard = fc1_weight.shape[0]
    chunks = hidden_cols // shard
    upper, lower = halves(fc1_weight)
    lower = jnp.transpose(lower.reshape(shard // 2, chunks, shard), (1, 0, 2)).reshape(-1, shard)
    fc_rest = jnp.concatenate([lower, fc2_weight], axis=0)
    places = shard_places(out_weight, data)
    home = jnp.stack([group, (data * ring + spot) % groups]).astype(jnp.int32)
    w_qkv, w_starts, h_pieces, (upper, *small) = gather_first(
        qkv_weight,
        hidden_in,
        data,
        (upper, out_weight, fc_rest, places, home)
        + (a_q, b_q, a_o, b_o, a_1, b_1, a_2, b_2, slopes),
    )
    held_out, fc_rest, places, home, a_q, b_q, a_o, b_o, a_1, b_1, a_2, b_2, slopes = small
    w_fc_first = lax.all_gather(upper, "dp", axis=0, tiled=False)
    w_starts = jnp.stack(w_starts).astype(jnp.int32)
    out_stages = gather_shards(out_weight, data)
    flying = out_stages.send(held_out)

    x = halves(hidden_in.astype(F32))
    w_qkv_near, n1_first = prepare_qkv(
        h_pieces[:-1], ln1_gain[None], ln1_bias[None], w_qkv, w_starts
    )
    h_pieces[-1], cotangent_held, flying, w_qkv_near = lax.optimization_barrier(
        (h_pieces[-1], cotangent, flying, w_qkv_near)
    )
    gy = [cotangent, shift_one(cotangent_held, "tensor")]
    flying = out_stages.send(flying)
    pieces, u1, n1 = qkv_product(
        n1_first,
        h_pieces[-1],
        ln1_gain[None],
        ln1_bias[None],
        a_q,
        b_q,
        joined_bias[None],
        w_qkv_near,
        meta,
    )
    pieces, flying, fc_rest = lax.optimization_barrier((pieces, flying, fc_rest))
    flying = out_stages.send(flying)
    w_fc_second = lax.all_gather(fc_rest, "dp", axis=0, tiled=False)
    pieces, (gy, flying) = swap_heads(pieces, (gy, flying))
    gy.append(shift_one(gy[1], "tensor"))
    pieces, qkv_true, out_t, logs = attend_forward(pieces, meta, slopes, ring, rows)
    pieces, gy = lax.optimization_barrier((pieces, gy))
    gy += ring_gather(gy[-1], "tensor", ring - 3)[1:]
    pieces, unused = swap_heads(pieces)
    pieces, gy = lax.optimization_barrier((pieces, gy))
    w_out = out_stages.send(flying)
    part_out, ctx, u2 = out_product(pieces, a_o, b_o, w_out, places, meta, ring, n)
    weights = [w_fc_first, w_fc_second]

    def load_beside(hop, moved):
        if hop == ring - 3:
            moved, weights[:] = lax.optimization_barrier((moved, weights))
        if hop == ring - 2:
            moved, weights[:] = lax.optimization_barrier((moved, load_to_vmem(*weights)))
        return moved

    summed = ring_scatter(part_out, "tensor", load_beside)
    mid = [rows_in + (term + output_bias) for rows_in, term in zip(x, summed)]

    normed2 = [norm_forward(m, ln2_gain, ln2_bias) for m in mid]
    block = [normed.astype(BF) for normed, unused, unused in normed2]
    part_in2, part_mlp, fc_grads = [], [], []
    for k in range(ring):
        following = shift_all(block if k < ring - 1 else part_in2[1], "tensor")
        grad_pieces, out_piece, fc_grads = mlp_both_ways(
            block, gy[k], a_1, b_1, a_2, b_2, first_feed_bias[None], weights, fc_grads
        )
        part_in2.append(grad_pieces)
        part_mlp.append(out_piece)
        block, part_in2[1:], fc_grads = lax.optimization_barrier(
            (following, part_in2[1:], fc_grads)
        )
    g_b1, g_a2, g_a1, g_b2 = fc_grads
    grad_n2 = ring_scatter(part_in2, "tensor", moved=block)
    grad_mid = [
        top.astype(F32) + norm_backward(grad, unit, inverse, ln2_gain)
        for top, grad, (unused, unit, inverse) in zip(halves(cotangent), grad_n2, normed2)
    ]
    gm = [[g.astype(BF) for g in grad_mid]]
    for k in range(ring):
        if k < ring - 1:
            gm.append(shift_all(gm[-1], "tensor"))
    gm = [half for pair in gm for half in pair]

    mlp_total, gm = lax.optimization_barrier((part_mlp[1], gm))
    mlp_total = shift_one(mlp_total, "tensor")
    pieces, g_bo, g_ao = gctx_product(gm, a_o, b_o, w_out, places, ctx, u2, meta, n)
    pieces, mlp_total = swap_heads(pieces, mlp_total)
    (mlp_total,) = add_terms([mlp_total], part_mlp[2:3], BF)
    mlp_total = shift_one(mlp_total, "tensor")
    first, second = attend_backward(pieces, qkv_true, out_t, logs, meta, slopes, ring, rows)
    first, second, mlp_total = lax.optimization_barrier((first, second, mlp_total))
    (mlp_total,) = add_terms([mlp_total], (part_mlp[3:] + part_mlp[:1])[:1], BF)
    mlp_total = shift_one(mlp_total, "tensor")
    landed = swap_start(first)
    w_near = load_rows_to_vmem(w_qkv, w_starts, (qkv_down.shape[2], qkv_cols))
    landed, w_near, second = lax.optimization_barrier((landed, w_near, second))
    first = swap_end(first, landed)
    landed = swap_start(second)
    part_first, q1, gu1 = gn1_first(first, a_q, b_q, w_near, meta)
    part_first, mlp_total = lax.optimization_barrier((part_first, mlp_total))
    for terms in (part_mlp[3:] + part_mlp[:1])[1:]:
        (mlp_total,) = add_terms([mlp_total], [terms], F32)
        if terms is not part_mlp[0]:
            mlp_total = shift_one(mlp_total.astype(BF), "tensor")
    moved = shift_all(part_first, "tensor")
    second = swap_end(second, landed)
    part_rest, late = gn1_rest(
        second,
        q1,
        gu1,
        n1,
        u1,
        a_q,
        b_q,
        w_near,
        [g_bo, g_a1, g_b2],
        [g_ao, g_b1, g_a2],
        meta,
        ring,
        groups,
    )
    moved, part_rest = lax.optimization_barrier((moved, part_rest))
    late.step(())
    part_in1 = part_rest[-1:] + [part_first] + part_rest[:-1]

    def reduce_beside(hop, moved):
        late.step(moved[0])
        return moved

    grad_n1 = ring_scatter(part_in1, "tensor", reduce_beside, moved)
    while late.result is None:
        late.step(())
    layer_output = jnp.concatenate(
        [(m + (t + second_feed_bias)).astype(BF) for m, t in zip(mid, halves(mlp_total))], axis=0
    )
    normed1 = [norm_forward(rows_in, ln1_gain, ln1_bias) for rows_in in x]
    hidden_grad = jnp.concatenate(
        [
            g + norm_backward(grad, unit, inverse, ln1_gain)
            for g, grad, (unused, unit, inverse) in zip(grad_mid, grad_n1, normed1)
        ],
        axis=0,
    )

    (full, full_widths), (own, own_widths) = late.result
    g_aq, g_bo, g_a1, g_b2, g_bq, g_ao, g_b1, g_a2 = place(
        full, full_widths, own, own_widths, home, seq_adapter
    )
    return (layer_output, hidden_grad, g_aq, g_bq, g_ao, g_bo, g_a1, g_b1, g_a2, g_b2)


def solution(mesh):
    rows, cols = P(("dp", "tensor"), None), P(None, None, ("dp", "tensor"))
    placed = (
        rows,
        P(),
        P(),
        P("dp", "tensor"),
        P("tensor"),
        P("tensor", "dp"),
        P(),
        P(),
        P(),
        P("dp", "tensor"),
        P("tensor"),
        P("tensor", "dp"),
    ) + (P(),) * 11 + (rows,)
    return jax.shard_map(
        local,
        mesh=mesh,
        in_specs=placed,
        out_specs=(rows, rows) + (cols,) * 8,
        check_vma=False,
    )
```

```python
import functools

import jax
import jax.numpy as jnp
from jax import lax
from jax.experimental import pallas as pl
from jax.experimental.pallas import tpu as pltpu
from jax.sharding import PartitionSpec as P

H = 32
HD = 64
ADAPTERS = 8
SEQ_DEVS = 4
PIC = 256
EPS = 1e-05
FACTOR = 0.5
BF = jnp.bfloat16
F32 = jnp.float32
FORWARD_BLOCK, BACKWARD_BLOCK = 512, 256
VMEM_BYTES = 56 * 1024 * 1024
SMALL_VMEM_BYTES = 28 * 1024 * 1024
US = 10**9


def dot(a, b):
    return jnp.dot(a, b, preferred_element_type=F32)


def dot_nt(a, b):
    return lax.dot_general(a, b, (((1,), (1,)), ((), ())), preferred_element_type=F32)


def dot_tn(a, b):
    return lax.dot_general(a, b, (((0,), (0,)), ((), ())), preferred_element_type=F32)


def hold(value, *until):
    return lax.optimization_barrier((value,) + until)[0]


def gelu_and_slope(f):
    phi = 0.5 * (1.0 + lax.erf(f * (0.5**0.5)))
    density = jnp.exp(-0.5 * f * f) * (0.5 / jnp.pi) ** 0.5
    return f * phi, phi + f * density


def norm_forward(values, gain, shift):
    centred = values - jnp.mean(values, axis=-1, keepdims=True)
    inverse = lax.rsqrt(jnp.mean(centred * centred, axis=-1, keepdims=True) + EPS)
    unit = centred * inverse
    return unit * gain + shift, unit, inverse


def norm_backward(upstream, unit, inverse, gain):
    scaled = upstream * gain
    return inverse * (
        scaled
        - jnp.mean(scaled, axis=-1, keepdims=True)
        - unit * jnp.mean(scaled * unit, axis=-1, keepdims=True)
    )


def shift_one(array, axis):
    n = lax.axis_size(axis)
    return lax.ppermute(array, axis, [(i, (i + 1) % n) for i in range(n)])


def ring_gather(array, axis, hops=None):
    pieces = [array]
    for _ in range(lax.axis_size(axis) - 1 if hops is None else hops):
        pieces.append(shift_one(pieces[-1], axis))
    return pieces


def halves(array):
    middle = array.shape[0] // 2
    return [array[:middle], array[middle:]]


def shift_all(arrays, axis):
    return [shift_one(a, axis) for a in arrays]


class Side:
    def __init__(self, operands, stages):
        self.operands, self.make, self.stages = operands, stages, None
        self.flying, self.result = (), None

    def step(self, beside):
        if self.result is not None:
            return beside
        if self.stages is None:
            beside, self.operands = lax.optimization_barrier((beside, self.operands))
            self.stages = self.make(*self.operands)
            self.flying = next(self.stages)
            return beside
        beside, landed = lax.optimization_barrier((beside, self.flying))
        try:
            self.flying = self.stages.send(landed)
        except StopIteration as stop:
            self.result = stop.value
        return beside


def add_terms(moved, terms, dtype):
    return [(m.astype(F32) + t.astype(F32)).astype(dtype) for m, t in zip(moved, terms)]


def ring_scatter(pieces, axis, beside=None, moved=None):
    following = pieces[2:] + pieces[:1]
    total = None if moved is not None else pieces[1]
    for i, terms in enumerate(following):
        if total is not None:
            moved = shift_all(total, axis)
        if beside is not None and total is not None:
            moved = beside(i, moved)
        total = add_terms(moved, terms, F32 if i == len(following) - 1 else BF)
    return total


def exchange(array, distance):
    n = lax.axis_size("dp")
    return lax.ppermute(array, "dp", [(i, i ^ distance) for i in range(n)])


def span_of(positions, meta_ref, spans, outside):
    label = jnp.full(positions.shape, outside, jnp.int32)
    for j in range(spans):
        start = meta_ref[2 + j]
        label = jnp.where((positions >= start) & (positions < start + PIC), j, label)
    return label


def allowed_block(i, j, size, meta_ref, spans):
    key_pos = j * size + lax.broadcasted_iota(jnp.int32, (size, size), 0)
    row_pos = i * size + lax.broadcasted_iota(jnp.int32, (size, size), 1)
    key_label = span_of(key_pos, meta_ref, spans, -1)
    row_label = span_of(row_pos, meta_ref, spans, -2)
    return (key_pos <= row_pos) | (key_label == row_label)


def crosses(i, size, meta_ref, spans):
    edge = (i + 1) * size
    found = jnp.bool_(False)
    for j in range(spans):
        start = meta_ref[2 + j]
        found = found | ((start < edge) & (edge < start + PIC))
    return found


def block_rows(i, size):
    return pl.ds(pl.multiple_of(i * size, size), size)


def together(ring):
    return [list(range(ring))]


def leaving(ring):
    return [[1], list(range(2, ring)) + [0]]


def true_blocks(meta_ref, parts, ring, rows, groups):
    part, spot = meta_ref[0], meta_ref[1]
    for g, group in enumerate(groups):
        for at, k in enumerate(group):
            for e in range(parts):
                back = spot - k
                back = jnp.where(back < 0, back + ring, back)
                start = pl.multiple_of(((part ^ e) * ring + back) * rows, rows)
                yield g * parts + e, slice(at * rows, (at + 1) * rows), pl.ds(start, rows)


def prepare_block(b, size, heads, qkv_ref, slope_ref, kaug_ref, qaug_ref):
    rows = block_rows(b, size)
    lane = lax.broadcasted_iota(jnp.int32, (size, HD), 1)
    pos = b * size + lax.broadcasted_iota(jnp.int32, (size, HD), 0)
    ones = jnp.where(lane < 3, 1.0, 0.0).astype(BF)
    for h in range(heads):
        at = h * 3 * HD
        query = qkv_ref[rows, at : at + HD] * jnp.asarray(0.125, BF)
        key = qkv_ref[rows, at + HD : at + 2 * HD]
        offset = pos.astype(F32) * (slope_ref[h] * 0.125)
        high = offset.astype(BF).astype(F32)
        middle = (offset - high).astype(BF).astype(F32)
        low = offset - high - middle
        extra = jnp.where(
            lane == 0, high, jnp.where(lane == 1, middle, jnp.where(lane == 2, low, 0.0))
        ).astype(BF)
        qaug_ref[h, rows, :] = jnp.concatenate([query, ones], axis=1)
        kaug_ref[h, rows, :] = jnp.concatenate([key, extra], axis=1)


def forward_kernel(size, heads, parts, ring, rows, spans, meta_ref, slope_ref, *refs):
    piece_refs = refs[:parts]
    ctx_refs = refs[parts : 2 * parts]
    qkv_ref, out_t_ref, log_ref, kaug_ref, qaug_ref, vt_ref, top_ref, total_ref = refs[2 * parts :]
    length = qkv_ref.shape[0]
    blocks = length // size
    for i, block, dst in true_blocks(meta_ref, parts, ring, rows, together(ring)):
        qkv_ref[dst, :] = piece_refs[i][block, :]
    eye = (
        lax.broadcasted_iota(jnp.int32, (HD, HD), 0) == lax.broadcasted_iota(jnp.int32, (HD, HD), 1)
    ).astype(BF)

    def prepare(b, unused):
        prepare_block(b, size, heads, qkv_ref, slope_ref, kaug_ref, qaug_ref)
        cols = block_rows(b, size)
        for h in range(heads):
            at = h * 3 * HD + 2 * HD
            value = qkv_ref[cols, at : at + HD]
            vt_ref[h, :HD, cols] = dot_nt(eye, value).astype(BF)
            row = lax.broadcasted_iota(jnp.int32, (16, size), 0)
            vt_ref[h, HD:, cols] = jnp.where(row == 0, 1.0, 0.0).astype(BF)
        return unused

    lax.fori_loop(0, blocks, prepare, 0)

    for i in range(blocks):
        rows_i = slice(i * size, (i + 1) * size)
        allowed = allowed_block(i, i, size, meta_ref, spans)
        outs = []
        for h in range(heads):
            query = qaug_ref[h, rows_i, :]
            scores = dot_nt(kaug_ref[h, : (i + 1) * size, :], query)
            own = jnp.where(allowed, scores[i * size :], -1e30)
            top = jnp.max(own, axis=0, keepdims=True)
            if i:
                scores = scores[: i * size]
                top = jnp.maximum(top, jnp.max(scores, axis=0, keepdims=True))
            total = dot(vt_ref[h, :, rows_i], jnp.exp(own - top).astype(BF))
            if i:
                total = total + dot(
                    vt_ref[h, :, : i * size], jnp.exp(scores - top).astype(BF)
                )
            top_ref[h : h + 1, :] = top
            total_ref[h] = total

        if i < blocks - 1:

            @pl.when(crosses(i, size, meta_ref, spans))
            def _(i=i, rows_i=rows_i):
                allowed = allowed_block(i, i + 1, size, meta_ref, spans)
                for h in range(heads):
                    scores = dot_nt(
                        kaug_ref[h, (i + 1) * size : (i + 2) * size, :], qaug_ref[h, rows_i, :]
                    )
                    scores = jnp.where(allowed, scores, -1e30)
                    old_top = top_ref[h : h + 1, :]
                    top = jnp.maximum(old_top, jnp.max(scores, axis=0, keepdims=True))
                    weight = jnp.exp(scores - top).astype(BF)
                    total_ref[h] = total_ref[h] * jnp.exp(old_top - top) + dot(
                        vt_ref[h, :, (i + 1) * size : (i + 2) * size], weight
                    )
                    top_ref[h : h + 1, :] = top

        for h in range(heads):
            total = total_ref[h]
            amount = total[HD : HD + 1]
            outs.append(total[:HD] / amount)
            log_ref[h : h + 1, rows_i] = top_ref[h : h + 1, :] + jnp.log(amount)
        if heads * HD < 128:
            outs.append(jnp.zeros((128 - heads * HD, size), F32))
        out_t_ref[:, rows_i] = jnp.concatenate(outs, axis=0)

    for i, block, true_rows in true_blocks(meta_ref, parts, ring, rows, together(ring)):
        turned = out_t_ref[:, true_rows].T.astype(BF)
        ctx_refs[i][block, :] = turned[:, : heads * HD]


def backward_kernel(size, heads, parts, ring, rows, spans, meta_ref, slope_ref, *refs):
    piece_refs = refs[:parts]
    qkv_ref, out_t_ref, log_ref = refs[parts : parts + 3]
    grad_refs = refs[parts + 3 : 3 * parts + 3]
    (
        g_ref,
        kaug_ref,
        qaug_ref,
        kt_ref,
        gq_ref,
        gg_ref,
        delta_ref,
        dqt_ref,
        dkv_ref,
    ) = refs[3 * parts + 3 :]
    length = qkv_ref.shape[0]
    blocks = length // size
    for i, block, dst in true_blocks(meta_ref, parts, ring, rows, together(ring)):
        g_ref[dst, :] = piece_refs[i][block, :]
    eye = (
        lax.broadcasted_iota(jnp.int32, (HD, HD), 0) == lax.broadcasted_iota(jnp.int32, (HD, HD), 1)
    ).astype(BF)

    def prepare(b, unused):
        prepare_block(b, size, heads, qkv_ref, slope_ref, kaug_ref, qaug_ref)
        cols = block_rows(b, size)
        blank = jnp.zeros((size, HD), BF)
        grad_t = g_ref[cols, :].astype(F32)
        if heads * HD < 128:
            grad_t = jnp.concatenate([grad_t, jnp.zeros((size, 128 - heads * HD), F32)], axis=1)
        product = grad_t.T * out_t_ref[:, cols]
        for h in range(heads):
            at = h * 3 * HD
            kt_ref[h, :, cols] = dot_nt(eye, qkv_ref[cols, at + HD : at + 2 * HD]).astype(BF)
            query = qkv_ref[cols, at : at + HD] * jnp.asarray(0.125, BF)
            gq_ref[h, cols, :] = jnp.concatenate([blank, query], axis=1)
            gg_ref[h, cols, :] = jnp.concatenate([g_ref[cols, h * HD : (h + 1) * HD], blank], axis=1)
            delta_ref[h : h + 1, cols] = jnp.sum(
                product[h * HD : (h + 1) * HD], axis=0, keepdims=True
            )
        return unused

    lax.fori_loop(0, blocks, prepare, 0)

    def part_of(h, keys, queries, allowed):
        at = h * 3 * HD + 2 * HD
        scores = dot_nt(kaug_ref[h, keys, :], qaug_ref[h, queries, :])
        first = jnp.where(allowed, scores[:, :size], -1e30)
        if scores.shape[1] > size:
            scores = jnp.concatenate([first, scores[:, size:]], axis=1)
        else:
            scores = first
        weight = jnp.exp(scores - log_ref[h : h + 1, queries])
        grad_weight = dot_nt(qkv_ref[keys, at : at + HD], g_ref[queries, h * HD : (h + 1) * HD])
        grad_score = (weight * (grad_weight - delta_ref[h : h + 1, queries])).astype(BF)
        dkv = dot(weight.astype(BF), gg_ref[h, queries, :]) + dot(grad_score, gq_ref[h, queries, :])
        return dkv, dot(kt_ref[h, :, keys], grad_score)

    for j in range(blocks):
        keys = slice(j * size, (j + 1) * size)
        queries = slice(j * size, length)
        allowed = allowed_block(j, j, size, meta_ref, spans)
        for h in range(heads):
            dkv, dq = part_of(h, keys, queries, allowed)
            dkv_ref[h, keys, :] = dkv
            rows_h = slice(h * HD, (h + 1) * HD)
            if j:
                dq = dq + dqt_ref[rows_h, queries]
            dqt_ref[rows_h, queries] = dq

        if j:

            @pl.when(crosses(j - 1, size, meta_ref, spans))
            def _(j=j, keys=keys):
                queries = slice((j - 1) * size, j * size)
                allowed = allowed_block(j - 1, j, size, meta_ref, spans)
                for h in range(heads):
                    dkv, dq = part_of(h, keys, queries, allowed)
                    dkv_ref[h, keys, :] += dkv
                    dqt_ref[h * HD : (h + 1) * HD, queries] += dq

    for i, block, true_rows in true_blocks(meta_ref, parts, ring, rows, leaving(ring)):
        columns = []
        grad_q = (dqt_ref[:, true_rows] * 0.125).T
        for h in range(heads):
            dkv = dkv_ref[h, true_rows, :]
            columns += [grad_q[:, h * HD : (h + 1) * HD], dkv[:, HD:], dkv[:, :HD]]
        grad_refs[i][block, :] = jnp.concatenate(columns, axis=1).astype(BF)


def specs(count_smem, count_vmem):
    return [pl.BlockSpec(memory_space=pltpu.SMEM)] * count_smem + [
        pl.BlockSpec(memory_space=pltpu.VMEM)
    ] * count_vmem


def attend_forward(pieces, meta, slopes, ring, rows):
    heads = slopes.shape[0]
    parts = len(pieces)
    length = parts * pieces[0].shape[0]
    wide = max(128, heads * HD)
    outs = pl.pallas_call(
        functools.partial(forward_kernel, FORWARD_BLOCK, heads, parts, ring, rows, meta.shape[0] - 2),
        out_shape=tuple(
            [jax.ShapeDtypeStruct((length // parts, heads * HD), BF)] * parts
            + [
                jax.ShapeDtypeStruct((length, heads * 3 * HD), BF),
                jax.ShapeDtypeStruct((wide, length), F32),
                jax.ShapeDtypeStruct((8, length), F32),
            ]
        ),
        in_specs=specs(2, parts),
        out_specs=tuple(specs(0, parts + 3)),
        scratch_shapes=[
            pltpu.VMEM((heads, length, 128), BF),
            pltpu.VMEM((heads, length, 128), BF),
            pltpu.VMEM((heads, HD + 16, length), BF),
            pltpu.VMEM((8, FORWARD_BLOCK), F32),
            pltpu.VMEM((heads, HD + 16, FORWARD_BLOCK), F32),
        ],
        compiler_params=pltpu.CompilerParams(vmem_limit_bytes=VMEM_BYTES),
        cost_estimate=pl.CostEstimate(
            flops=2 * US, bytes_accessed=length * heads * HD * 20, transcendentals=0
        ),
    )(meta, slopes, *pieces)
    return list(outs[:parts]), *outs[parts:]


def attend_backward(pieces, qkv, out_t, logs, meta, slopes, ring, rows):
    heads = slopes.shape[0]
    parts = len(pieces)
    length = qkv.shape[0]
    wide = max(128, heads * HD)
    outs = pl.pallas_call(
        functools.partial(backward_kernel, BACKWARD_BLOCK, heads, parts, ring, rows, meta.shape[0] - 2),
        out_shape=tuple(
            jax.ShapeDtypeStruct((len(group) * rows, heads * 3 * HD), BF)
            for group in leaving(ring)
            for unused in range(parts)
        ),
        in_specs=specs(2, parts + 3),
        out_specs=tuple(specs(0, 2 * parts)),
        scratch_shapes=[
            pltpu.VMEM((length, heads * HD), BF),
            pltpu.VMEM((heads, length, 128), BF),
            pltpu.VMEM((heads, length, 128), BF),
            pltpu.VMEM((heads, HD, length), BF),
            pltpu.VMEM((heads, length, 128), BF),
            pltpu.VMEM((heads, length, 128), BF),
            pltpu.VMEM((8, length), F32),
            pltpu.VMEM((wide, length), F32),
            pltpu.VMEM((heads, length, 128), F32),
        ],
        compiler_params=pltpu.CompilerParams(vmem_limit_bytes=VMEM_BYTES),
        cost_estimate=pl.CostEstimate(
            flops=2 * US, bytes_accessed=length * heads * HD * 20, transcendentals=0
        ),
    )(meta, slopes, *pieces, qkv, out_t, logs)
    return list(outs[:parts]), list(outs[parts:])


def take_columns(ref, part, e, width):
    def each(use):
        if width % 128 == 0:
            start = pl.multiple_of((part ^ e) * width, width)
            use(ref.at[:, pl.ds(start, width)])
        else:
            for p in range(SEQ_DEVS):

                @pl.when(part == p)
                def _():
                    use(ref.at[:, pl.ds((p ^ e) * width, width)])

    return each


def column_loop(total, body):
    step = min(256, total)

    def one(i, unused):
        body(pl.ds(pl.multiple_of(i * step, step), step))
        return unused

    lax.fori_loop(0, total // step, one, 0)


def in_hbm(pieces):
    return [pltpu.with_memory_space_constraint(piece, pltpu.HBM) for piece in pieces]


def load_weights(w_pieces, w_ref, sems, starts_ref):
    copies = []
    for i, piece in enumerate(w_pieces):
        count = piece.shape[0]
        start = pl.multiple_of(starts_ref[i], min(128, count))
        copy = pltpu.make_async_copy(piece, w_ref.at[pl.ds(start, count), :], sems.at[i])
        copy.start()
        copies.append(copy)
    return copies


def load_shards(w_pieces, w_ref, sems, places_ref):
    copies = []
    for i, piece in enumerate(w_pieces):
        if len(piece.shape) == 3:
            copy = pltpu.make_async_copy(piece, w_ref, sems.at[i])
        else:
            count = piece.shape[0]
            start = pl.multiple_of(places_ref[2 * i + 1], count)
            target = w_ref.at[places_ref[2 * i], pl.ds(start, count), :]
            copy = pltpu.make_async_copy(piece, target, sems.at[i])
        copy.start()
        copies.append(copy)
    return copies


def normed_rows(rows_ref, gain_ref, shift_ref):
    return norm_forward(rows_ref[...].astype(F32), gain_ref[...], shift_ref[...])[0].astype(BF)


def prepare_qkv_kernel(count, starts_ref, *refs):
    h_pieces, refs = refs[:count], refs[count:]
    gain_ref, shift_ref, w_pieces, (w_ref, x_ref, sems) = refs[0], refs[1], refs[2:-3], refs[-3:]
    copies = load_weights(w_pieces, w_ref, sems, starts_ref)
    rows = h_pieces[0].shape[0]
    for k in range(count):
        x_ref[k * rows : (k + 1) * rows, :] = normed_rows(h_pieces[k], gain_ref, shift_ref)
    for copy in copies:
        copy.wait()


def prepare_qkv(h_pieces, gain, shift, w_pieces, starts):
    count, n_w = len(h_pieces), len(w_pieces)
    rows, depth = h_pieces[0].shape
    cols = w_pieces[0].shape[1]
    return pl.pallas_call(
        functools.partial(prepare_qkv_kernel, count),
        out_shape=[pltpu.VMEM((depth, cols), BF), pltpu.VMEM((count * rows, depth), BF)],
        in_specs=specs(1, count + 2) + [pl.BlockSpec(memory_space=pl.ANY)] * n_w,
        out_specs=specs(0, 2),
        scratch_shapes=[pltpu.SemaphoreType.DMA((n_w,))],
        compiler_params=pltpu.CompilerParams(vmem_limit_bytes=SMALL_VMEM_BYTES),
        cost_estimate=pl.CostEstimate(flops=3 * US, bytes_accessed=2**20, transcendentals=0),
    )(starts, *h_pieces, gain, shift, *in_hbm(w_pieces))


def qkv_kernel(meta_ref, first_ref, last_ref, gain_ref, shift_ref, a_ref, b_ref, bias_ref, *refs):
    w_ref, q_refs, (u_ref, x_ref, o_ref) = refs[0], refs[1 : 1 + SEQ_DEVS], refs[1 + SEQ_DEVS :]
    before = first_ref.shape[0]
    x_ref[:before, :] = first_ref[...]
    x_ref[before:, :] = normed_rows(last_ref, gain_ref, shift_ref)
    u_ref[...] = dot_nt(x_ref[...], a_ref[...]).astype(BF)

    def body(cols):
        total = dot(x_ref[...], w_ref[:, cols])
        total = total + FACTOR * dot(u_ref[...], b_ref[:, cols]) + bias_ref[:, cols]
        o_ref[:, cols] = total.astype(BF)

    column_loop(o_ref.shape[1], body)
    for e in range(SEQ_DEVS):

        def store(src, e=e):
            q_refs[e][...] = src[...]

        take_columns(o_ref, meta_ref[0], e, q_refs[e].shape[1])(store)


def qkv_product(first, last, gain, shift, a, b, bias, w, meta):
    count, depth = first.shape[0] + last.shape[0], first.shape[1]
    cols = b.shape[1]
    outs = pl.pallas_call(
        qkv_kernel,
        out_shape=tuple(
            [jax.ShapeDtypeStruct((count, cols // SEQ_DEVS), BF)] * SEQ_DEVS
            + [
                jax.ShapeDtypeStruct((count, a.shape[0]), BF),
                jax.ShapeDtypeStruct((count, depth), BF),
            ]
        ),
        in_specs=specs(1, 8),
        out_specs=tuple(specs(0, SEQ_DEVS + 2)),
        scratch_shapes=[pltpu.VMEM((count, cols), BF)],
        compiler_params=pltpu.CompilerParams(vmem_limit_bytes=SMALL_VMEM_BYTES),
        cost_estimate=pl.CostEstimate(flops=2 * US, bytes_accessed=2**20, transcendentals=0),
    )(meta, first, last, gain, shift, a, b, bias, w)
    return list(outs[:SEQ_DEVS]), outs[SEQ_DEVS], outs[SEQ_DEVS + 1]


def load_kernel(first_ref, second_ref, first_out, second_out, sems):
    shards, half = first_ref.shape[0], first_ref.shape[1]
    depth = second_ref.shape[2]
    chunks = first_out.shape[1] // depth
    copies = []

    def copy(src, dst):
        copies.append(pltpu.make_async_copy(src, dst, sems.at[len(copies)]))

    for i in range(shards):
        copy(first_ref.at[i], first_out.at[pl.ds(2 * i * half, half), :])
        for h in range(chunks):
            copy(
                second_ref.at[i, pl.ds(h * half, half)],
                first_out.at[pl.ds((2 * i + 1) * half, half), pl.ds(h * depth, depth)],
            )
        copy(second_ref.at[i, pl.ds(chunks * half, chunks * depth)], second_out.at[i])
    for each in copies:
        each.start()
    for each in copies:
        each.wait()


def load_to_vmem(first, second):
    shards, half, hidden = first.shape
    chunks = hidden // second.shape[2]
    return pl.pallas_call(
        load_kernel,
        out_shape=[
            pltpu.VMEM((shards * half * 2, hidden), BF),
            pltpu.VMEM((shards, hidden, second.shape[2]), BF),
        ],
        in_specs=[pl.BlockSpec(memory_space=pl.ANY)] * 2,
        out_specs=[pl.BlockSpec(memory_space=pltpu.VMEM)] * 2,
        scratch_shapes=[pltpu.SemaphoreType.DMA((shards * (chunks + 2),))],
        compiler_params=pltpu.CompilerParams(vmem_limit_bytes=2 * 1024 * 1024),
        cost_estimate=pl.CostEstimate(flops=5 * US, bytes_accessed=2**20, transcendentals=0),
    )(*[pltpu.with_memory_space_constraint(w, pltpu.HBM) for w in (first, second)])


def store_rows(refs, cols, total):
    at = 0
    for ref in refs:
        ref[:, cols] = total[at : at + ref.shape[0]]
        at += ref.shape[0]


def out_kernel(ring, n_w, meta_ref, places_ref, *refs):
    c_pieces = refs[:SEQ_DEVS]
    a_ref, b_ref = refs[SEQ_DEVS : SEQ_DEVS + 2]
    w_pieces, refs = refs[SEQ_DEVS + 2 : SEQ_DEVS + 2 + n_w], refs[SEQ_DEVS + 2 + n_w :]
    p_refs = refs[:ring]
    ctx_ref, u_ref, w_ref, sems = refs[ring:]
    copies = load_shards(w_pieces, w_ref, sems, places_ref)
    width = c_pieces[0].shape[1]
    for e in range(SEQ_DEVS):

        def store(dst, e=e):
            dst[...] = c_pieces[e][...]

        take_columns(ctx_ref, meta_ref[0], e, width)(store)
    u_ref[...] = dot_nt(ctx_ref[...], a_ref[...]).astype(BF)
    for copy in copies:
        copy.wait()
    shards, unused, wide = w_ref.shape
    for j in range(shards):
        cols = slice(j * wide, (j + 1) * wide)
        total = dot(ctx_ref[...], w_ref[j]) + FACTOR * dot(u_ref[...], b_ref[:, cols])
        store_rows(p_refs, cols, total.astype(BF))


def paired(pieces):
    return [list(pieces[i : i + 2]) for i in range(0, len(pieces), 2)]


def out_product(c_pieces, a, b, w_pieces, places, meta, ring, shards):
    count, width = c_pieces[0].shape
    rank, depth = b.shape
    n_w = len(w_pieces)
    outs = pl.pallas_call(
        functools.partial(out_kernel, 2 * ring, n_w),
        out_shape=tuple(
            [jax.ShapeDtypeStruct((count // ring // 2, depth), BF)] * (2 * ring)
            + [
                jax.ShapeDtypeStruct((count, width * SEQ_DEVS), BF),
                jax.ShapeDtypeStruct((count, rank), BF),
            ]
        ),
        in_specs=specs(2, SEQ_DEVS + 2) + [pl.BlockSpec(memory_space=pl.ANY)] * n_w,
        out_specs=tuple(specs(0, 2 * ring + 2)),
        scratch_shapes=[
            pltpu.VMEM((shards, width * SEQ_DEVS, depth // shards), BF),
            pltpu.SemaphoreType.DMA((n_w,)),
        ],
        compiler_params=pltpu.CompilerParams(vmem_limit_bytes=VMEM_BYTES),
        cost_estimate=pl.CostEstimate(flops=3 * US, bytes_accessed=2**20, transcendentals=0),
    )(meta, places, *c_pieces, a, b, *w_pieces)
    return paired(outs[: 2 * ring]), outs[2 * ring], outs[2 * ring + 1]


def mlp_kernel(count, add, *refs):
    n2_refs, (gy_ref, a1_ref, b2_ref, b1_ref, a2_ref, bias_ref), refs = (
        refs[:count],
        refs[count : count + 6],
        refs[count + 6 :],
    )
    w1_ref, w2_ref, before, refs = refs[0], refs[1], refs[2 : 2 + add], refs[2 + add :]
    p_refs, m_ref, grads = refs[:count], refs[count], refs[count + 1 : count + 5]
    x_ref, act_ref, slope_ref, gf_ref = refs[count + 5 :]
    shards, hidden, wide = w2_ref.shape
    at = 0
    for ref in n2_refs:
        x_ref[at : at + ref.shape[0], :] = ref[...]
        at += ref.shape[0]
    u3 = dot_nt(x_ref[...], a1_ref[...]).astype(BF)
    gu4 = (FACTOR * dot_nt(gy_ref[...], b2_ref[...])).astype(BF)
    for h in range(0, hidden, wide):
        cols = slice(h, h + wide)
        f = dot(x_ref[...], w1_ref[:, cols])
        f = f + FACTOR * dot(u3, b1_ref[:, cols]) + bias_ref[:, cols]
        act, slope = gelu_and_slope(f)
        act_ref[:, cols] = act.astype(BF)
        slope_ref[:, cols] = slope
    for h in range(0, hidden, wide):
        cols = slice(h, h + wide)
        gact = dot(gu4, a2_ref[:, cols])
        for j in range(shards):
            gact = gact + dot_nt(gy_ref[:, j * wide : (j + 1) * wide], w2_ref[j, cols, :])
        gf_ref[:, cols] = (gact * slope_ref[:, cols]).astype(BF)
    gu3 = (FACTOR * dot_nt(gf_ref[...], b1_ref[...])).astype(BF)
    for j in range(shards):
        cols = slice(j * wide, (j + 1) * wide)
        total = dot_nt(gf_ref[...], w1_ref[cols, :]) + dot(gu3, a1_ref[:, cols])
        store_rows(p_refs, cols, total.astype(BF))
    u4 = dot_nt(act_ref[...], a2_ref[...]).astype(BF)
    for j in range(shards):
        cols = slice(j * wide, (j + 1) * wide)
        total = dot(act_ref[...], w2_ref[j]) + FACTOR * dot(u4, b2_ref[:, cols])
        m_ref[:, cols] = total.astype(BF)
    products = [
        FACTOR * dot_tn(u3, gf_ref[...]),
        dot_tn(gu4, act_ref[...]),
        dot_tn(gu3, x_ref[...]),
        FACTOR * dot_tn(u4, gy_ref[...]),
    ]
    for i, product in enumerate(products):
        grads[i][...] = product + before[i][...] if add else product


def mlp_both_ways(n2_pieces, gy, a1, b1, a2, b2, bias, weights, before):
    count = len(n2_pieces)
    total, depth = gy.shape
    rank, hidden = b1.shape
    outs = pl.pallas_call(
        functools.partial(mlp_kernel, count, len(before)),
        out_shape=(
            [jax.ShapeDtypeStruct(piece.shape, BF) for piece in n2_pieces]
            + [jax.ShapeDtypeStruct((total, depth), BF)]
            + [jax.ShapeDtypeStruct((rank, hidden), F32)] * 2
            + [jax.ShapeDtypeStruct((rank, depth), F32)] * 2
        ),
        in_specs=specs(0, count + 8 + len(before)),
        out_specs=specs(0, count + 5),
        scratch_shapes=[
            pltpu.VMEM((total, depth), BF),
            pltpu.VMEM((total, hidden), BF),
            pltpu.VMEM((total, hidden), F32),
            pltpu.VMEM((total, hidden), BF),
        ],
        compiler_params=pltpu.CompilerParams(vmem_limit_bytes=SMALL_VMEM_BYTES),
        cost_estimate=pl.CostEstimate(
            flops=10 * US, bytes_accessed=4 * depth * hidden, transcendentals=0
        ),
    )(*n2_pieces, gy, a1, b2, b1, a2, bias, *weights, *before)
    return list(outs[:count]), outs[count], list(outs[count + 1 :])


def pack_into(full, own, ring, groups, meta_ref, out_ref):
    part, spot = meta_ref[0], meta_ref[1]
    wide = out_ref.shape[4]
    at = 0
    for ref in full:
        width = ref.shape[1] // (ring * SEQ_DEVS * groups)
        for g in range(groups):
            for p in range(SEQ_DEVS):
                for z in range(ring):
                    k = z - spot
                    k = jnp.where(k < 0, k + ring, k)
                    column = ((g * SEQ_DEVS + p) * ring + z) * width
                    out_ref[part ^ p, k, g, :, at : at + width] = ref[
                        :, column : column + width
                    ].astype(BF)
        at += width
    at = 0
    for ref in own:
        width = ref.shape[1] // (SEQ_DEVS * groups)
        for p in range(SEQ_DEVS):
            for r in range(groups):
                column = (p * groups + r) * width
                out_ref[part ^ p, ring + at // wide, r, :, at % wide : at % wide + width] = ref[
                    :, column : column + width
                ].astype(BF)
        at += width


def pack_shapes(full_cols, own_cols, rank, ring, groups):
    full_widths = [c // (ring * SEQ_DEVS * groups) for c in full_cols]
    own_widths = [c // (SEQ_DEVS * groups) for c in own_cols]
    wide = sum(full_widths)
    rows = ring + sum(own_widths) // wide
    shapes = [jax.ShapeDtypeStruct((SEQ_DEVS, rows, groups, rank, wide), BF)]
    return shapes, full_widths, own_widths


def gctx_kernel(n_g, n_w, meta_ref, places_ref, *refs):
    g_pieces, refs = refs[:n_g], refs[n_g:]
    a_ref, b_ref, ctx_ref, u2_ref = refs[:4]
    w_pieces, refs = refs[4 : 4 + n_w], refs[4 + n_w :]
    c_refs = refs[:SEQ_DEVS]
    gbo_ref, gao_ref, g_ref, o_ref, w_ref, sems = refs[SEQ_DEVS:]
    copies = load_shards(w_pieces, w_ref, sems, places_ref)
    rows = g_pieces[0].shape[0]
    for k in range(n_g):
        g_ref[k * rows : (k + 1) * rows, :] = g_pieces[k][...]
    gu2 = (FACTOR * dot_nt(g_ref[...], b_ref[...])).astype(BF)
    shards, unused, wide = w_ref.shape
    total = dot(gu2, a_ref[...])
    gbo_ref[...] = FACTOR * dot_tn(u2_ref[...], g_ref[...])
    gao_ref[...] = dot_tn(gu2, ctx_ref[...])
    for copy in copies:
        copy.wait()
    for j in range(shards):
        total = total + dot_nt(g_ref[:, j * wide : (j + 1) * wide], w_ref[j])
    o_ref[...] = total.astype(BF)
    for e in range(SEQ_DEVS):

        def store(src, e=e):
            c_refs[e][...] = src[...]

        take_columns(o_ref, meta_ref[0], e, c_refs[e].shape[1])(store)


def gctx_product(g_pieces, a, b, w_pieces, places, ctx, u2, meta, shards):
    n_g, n_w = len(g_pieces), len(w_pieces)
    depth = g_pieces[0].shape[1]
    count, cols = ctx.shape
    rank = a.shape[0]
    outs = pl.pallas_call(
        functools.partial(gctx_kernel, n_g, n_w),
        out_shape=tuple(
            [jax.ShapeDtypeStruct((count, cols // SEQ_DEVS), BF)] * SEQ_DEVS
            + [jax.ShapeDtypeStruct((rank, depth), F32), jax.ShapeDtypeStruct((rank, cols), F32)]
        ),
        in_specs=specs(2, n_g + 4) + [pl.BlockSpec(memory_space=pl.ANY)] * n_w,
        out_specs=tuple(specs(0, SEQ_DEVS + 2)),
        scratch_shapes=[
            pltpu.VMEM((count, depth), BF),
            pltpu.VMEM((count, cols), BF),
            pltpu.VMEM((shards, cols, depth // shards), BF),
            pltpu.SemaphoreType.DMA((n_w,)),
        ],
        compiler_params=pltpu.CompilerParams(vmem_limit_bytes=VMEM_BYTES),
        cost_estimate=pl.CostEstimate(flops=3 * US, bytes_accessed=2**20, transcendentals=0),
    )(meta, places, *g_pieces, a, b, ctx, u2, *w_pieces)
    return list(outs[:SEQ_DEVS]), outs[SEQ_DEVS], outs[SEQ_DEVS + 1]


def near_kernel(starts_ref, *refs):
    w_pieces, w_ref, sems = refs[:-2], refs[-2], refs[-1]
    for copy in load_weights(w_pieces, w_ref, sems, starts_ref):
        copy.wait()


def load_rows_to_vmem(w_pieces, starts, shape):
    n_w = len(w_pieces)
    return pl.pallas_call(
        near_kernel,
        out_shape=pltpu.VMEM(shape, BF),
        in_specs=specs(1, 0) + [pl.BlockSpec(memory_space=pl.ANY)] * n_w,
        out_specs=specs(0, 1)[0],
        scratch_shapes=[pltpu.SemaphoreType.DMA((n_w,))],
        compiler_params=pltpu.CompilerParams(vmem_limit_bytes=2 * 1024 * 1024),
        cost_estimate=pl.CostEstimate(flops=2 * US, bytes_accessed=2**20, transcendentals=0),
    )(starts, *in_hbm(w_pieces))


def gather_columns(q_pieces, q_ref, meta_ref):
    for e in range(SEQ_DEVS):

        def store(dst, e=e):
            dst[...] = q_pieces[e][...]

        take_columns(q_ref, meta_ref[0], e, q_pieces[e].shape[1])(store)


def gn1_rows(q_ref, gu1, a_ref, w_ref, p_refs):
    def body(cols):
        total = dot_nt(q_ref[...], w_ref[cols, :]) + dot(gu1, a_ref[:, cols])
        store_rows(p_refs, cols, total.astype(BF))

    column_loop(w_ref.shape[0], body)


def gn1_first_kernel(meta_ref, *refs):
    q_pieces, (a_ref, b_ref, w_ref), refs = refs[:SEQ_DEVS], refs[SEQ_DEVS : SEQ_DEVS + 3], refs[SEQ_DEVS + 3 :]
    *p_refs, q_ref, gu_ref = refs
    gather_columns(q_pieces, q_ref, meta_ref)
    gu_ref[...] = (FACTOR * dot_nt(q_ref[...], b_ref[...])).astype(BF)
    gn1_rows(q_ref, gu_ref[...], a_ref, w_ref, p_refs)


def gn1_first(q_pieces, a, b, w, meta):
    rows = q_pieces[0].shape[0]
    rank, depth = a.shape
    outs = pl.pallas_call(
        gn1_first_kernel,
        out_shape=[jax.ShapeDtypeStruct((rows // 2, depth), BF)] * 2
        + [jax.ShapeDtypeStruct((rows, b.shape[1]), BF), jax.ShapeDtypeStruct((rows, rank), BF)],
        in_specs=specs(1, SEQ_DEVS + 3),
        out_specs=specs(0, 4),
        compiler_params=pltpu.CompilerParams(vmem_limit_bytes=SMALL_VMEM_BYTES),
        cost_estimate=pl.CostEstimate(flops=3 * US, bytes_accessed=2**20, transcendentals=0),
    )(meta, *q_pieces, a, b, w)
    return list(outs[:2]), outs[2], outs[3]


def gn1_rest_kernel(ring, groups, blocks, meta_ref, *refs):
    q_pieces, refs = refs[:SEQ_DEVS], refs[SEQ_DEVS:]
    q1_ref, gu1_ref, x_ref, u_ref, a_ref, b_ref, w_ref = refs[:7]
    full, own, p_refs, refs = refs[7:10], refs[10:13], refs[13 : 13 + blocks], refs[13 + blocks :]
    out_ref, q_ref, gb_ref, ga_ref = refs
    rows = q1_ref.shape[0]
    gather_columns(q_pieces, q_ref, meta_ref)
    gu1 = (FACTOR * dot_nt(q_ref[...], b_ref[...])).astype(BF)
    gn1_rows(q_ref, gu1, a_ref, w_ref, p_refs)
    here = slice(rows, 2 * rows)
    x = jnp.concatenate([x_ref[2 * rows :, :], x_ref[:rows, :]], axis=0)
    u = jnp.concatenate([u_ref[2 * rows :, :], u_ref[:rows, :]], axis=0)
    gb_ref[...] = FACTOR * (dot_tn(u, q_ref[...]) + dot_tn(u_ref[here, :], q1_ref[...]))
    ga_ref[...] = dot_tn(gu1, x) + dot_tn(gu1_ref[...], x_ref[here, :])
    pack_into([ga_ref, *full], [gb_ref, *own], ring, groups, meta_ref, out_ref)


def gn1_rest(q_pieces, q1, gu1, n1, u1, a, b, w, full, own, meta, ring, groups):
    count = q_pieces[0].shape[0]
    rank, depth = a.shape
    cols = b.shape[1]
    rows = q1.shape[0]
    blocks = 2 * count // rows
    shapes, full_widths, own_widths = pack_shapes(
        [depth] + [g.shape[1] for g in full],
        [cols] + [g.shape[1] for g in own],
        rank,
        ring,
        groups,
    )
    outs = pl.pallas_call(
        functools.partial(gn1_rest_kernel, ring, groups, blocks),
        out_shape=[jax.ShapeDtypeStruct((rows // 2, depth), BF)] * blocks + shapes,
        in_specs=specs(1, SEQ_DEVS + 13),
        out_specs=specs(0, blocks + 1),
        scratch_shapes=[
            pltpu.VMEM((count, cols), BF),
            pltpu.VMEM((rank, cols), F32),
            pltpu.VMEM((rank, depth), F32),
        ],
        compiler_params=pltpu.CompilerParams(vmem_limit_bytes=SMALL_VMEM_BYTES),
        cost_estimate=pl.CostEstimate(flops=6 * US, bytes_accessed=2**20, transcendentals=0),
    )(meta, *q_pieces, q1, gu1, n1, u1, a, b, w, *full, *own)
    stages = functools.partial(
        reduce_stages, full_widths=full_widths, own_widths=own_widths, groups=groups
    )
    return paired(outs[:blocks]), Side(list(outs[blocks:]), stages)


def reduce_stages(packed, full_widths, own_widths, groups):
    ring, n = lax.axis_size("tensor"), lax.axis_size("dp")
    group = lax.axis_index("dp") // SEQ_DEVS
    landed = yield [exchange(packed[e], e) for e in range(1, SEQ_DEVS)]
    total = sum([x.astype(F32) for x in landed], packed[0].astype(F32)).astype(BF)

    def block(array, k):
        return lax.dynamic_index_in_dim(array, (group + k) % groups, -3, keepdims=False)

    flying = [
        lax.ppermute(total[k], "tensor", [(i, (i + k) % ring) for i in range(ring)])
        for k in range(1, ring)
    ]
    for k in range(groups):
        pairs = []
        for i in range(n):
            for z in range(ring):
                r = (i // SEQ_DEVS + k) % groups
                pairs.append((i * ring + z, z * n + (i % SEQ_DEVS) * groups + r))
        flying.append(lax.ppermute(block(total[ring:], k), ("dp", "tensor"), pairs))
    landed = yield flying
    own = list(landed[ring - 1 :])
    total = sum([x.astype(F32) for x in landed[: ring - 1]], total[0].astype(F32)).astype(BF)
    flying = []
    for k in range(1, groups):
        pairs = [(i, (i + k * SEQ_DEVS) % n) for i in range(n)]
        flying.append(lax.ppermute(block(total, k), "dp", pairs))
    landed = yield flying
    return ([block(total, 0)] + list(landed), full_widths), (own, own_widths)


def place_kernel(n_full, n_own, full_widths, own_widths, home_ref, adapter_ref, *refs):
    outs = refs[n_full + n_own :]
    for out in outs:
        out[...] = jnp.zeros(out.shape, F32)
    for i, ref in enumerate(refs[: n_full + n_own]):
        k = i if i < n_full else i - n_full
        sequence = home_ref[int(i >= n_full)] - k
        sequence = jnp.where(sequence < 0, sequence + n_full, sequence)
        slot, at = adapter_ref[sequence], 0
        targets = outs[: len(full_widths)] if i < n_full else outs[len(full_widths) :]
        for out, width in zip(targets, full_widths if i < n_full else own_widths):
            if i < n_full:
                columns = ref[:, at : at + width]
            else:
                wide = ref.shape[2]
                columns = ref[at // wide, :, at % wide : at % wide + width]
            out[slot] = out[slot] + columns.astype(F32)
            at += width


def place(full, full_widths, own, own_widths, home, seq_adapter):
    rank = full[0].shape[0]
    widths = full_widths + own_widths
    return pl.pallas_call(
        functools.partial(place_kernel, len(full), len(own), full_widths, own_widths),
        out_shape=[jax.ShapeDtypeStruct((ADAPTERS, rank, w), F32) for w in widths],
        in_specs=specs(2, len(full) + len(own)),
        out_specs=specs(0, len(widths)),
        compiler_params=pltpu.CompilerParams(vmem_limit_bytes=VMEM_BYTES),
        cost_estimate=pl.CostEstimate(flops=US, bytes_accessed=2**20, transcendentals=0),
    )(home, seq_adapter, *full, *own)


def gather_first(shard, rows_in, data, small):
    n, count = lax.axis_size("dp"), shard.shape[0]
    if n != 8 or lax.axis_size("tensor") != 4:
        whole = lax.all_gather(shard, "dp", axis=0, tiled=True)
        return [whole], [0 * data], ring_gather(rows_in, "tensor"), small
    half = count // 2
    by_x, by_y, by_c = exchange(shard, 2), exchange(shard, 4), exchange(shard, 1)
    ring = [rows_in, shift_one(rows_in, "tensor")]
    by_x, by_y, by_c, ring[1], *small = lax.optimization_barrier(
        (by_x, by_y, by_c, ring[1]) + small
    )
    corner_a, corner_b = exchange(by_x[:half], 4), exchange(by_y[half:], 2)
    by_xc, by_yc = exchange(by_x, 1), exchange(by_y, 1)
    ring.append(shift_one(ring[1], "tensor"))
    corner_a, corner_b, by_xc, by_yc, ring[2], small[:2] = lax.optimization_barrier(
        (corner_a, corner_b, by_xc, by_yc, ring[2], small[:2])
    )
    far_a, far_b = exchange(corner_a, 1), exchange(corner_b, 1)
    ring.append(shift_one(ring[2], "tensor"))
    pieces = [shard, by_c, by_x, by_xc, by_y, by_yc, corner_a, far_a, corner_b, far_b]
    starts = [(data ^ e) * count for e in range(8)]
    starts += [(data ^ e) * count + half for e in (6, 7)]
    return pieces, starts, ring, small


def gather_shards(shard, data):
    stages = shard_stages(data)
    next(stages)
    return stages


def shard_stages(data):
    n = lax.axis_size("dp")
    shard = yield None
    if n != 8:
        landed = yield [lax.all_gather(shard, "dp", axis=0, tiled=False)]
        landed = yield landed
        landed = yield landed
        yield landed
        return
    half = shard.shape[0] // 2
    by_x, by_y, by_c = yield [exchange(shard, 2), exchange(shard, 4), exchange(shard, 1)]
    sent = [exchange(by_x[:half], 4), exchange(by_y[half:], 2), exchange(by_x, 1), exchange(by_y, 1)]
    corner_a, corner_b, by_xc, by_yc = yield sent
    far_a, far_b = yield [exchange(corner_a, 1), exchange(corner_b, 1)]
    pieces = [shard, by_c, by_x, by_xc, by_y, by_yc, corner_a, far_a, corner_b, far_b]
    yield pieces


def shard_places(shard, data):
    if lax.axis_size("dp") != 8:
        return jnp.zeros((2,), jnp.int32)
    half = shard.shape[0] // 2
    places = [(data ^ e, 0 * data) for e in range(8)] + [(data ^ e, 0 * data + half) for e in (6, 7)]
    return jnp.stack([p for place in places for p in place]).astype(jnp.int32)


def swap_start(pieces):
    return [exchange(pieces[2], 2), exchange(pieces[3], 2), exchange(pieces[1], 1)]


def swap_end(pieces, landed):
    across, far, near = landed
    return [pieces[0], near, across, exchange(far, 1)]


def swap_heads(pieces, beside=()):
    across, far, near = exchange(pieces[2], 2), exchange(pieces[3], 2), exchange(pieces[1], 1)
    across, far, near, beside = lax.optimization_barrier((across, far, near, beside))
    return [pieces[0], near, across, exchange(far, 1)], beside


def local(
    hidden_in,
    ln1_gain,
    ln1_bias,
    qkv_weight,
    joined_bias,
    out_weight,
    output_bias,
    ln2_gain,
    ln2_bias,
    fc1_weight,
    first_feed_bias,
    fc2_weight,
    second_feed_bias,
    qkv_down,
    qkv_up,
    out_down,
    out_up,
    fc1_down,
    fc1_up,
    fc2_down,
    fc2_up,
    seq_adapter,
    span_starts,
    cotangent,
):
    spot = lax.axis_index("tensor")
    data = lax.axis_index("dp")
    ring = lax.axis_size("tensor")
    groups = lax.axis_size("dp") // SEQ_DEVS
    group, part = data // SEQ_DEVS, data % SEQ_DEVS
    rows = hidden_in.shape[0]
    slot = lax.dynamic_index_in_dim(seq_adapter, group, 0, keepdims=False)
    starts = lax.dynamic_index_in_dim(span_starts, group, 0, keepdims=False)
    qkv_cols, ctx_cols, hidden_cols = qkv_weight.shape[1], out_weight.shape[0], fc1_weight.shape[1]
    heads = qkv_cols // (3 * HD) // SEQ_DEVS
    meta = jnp.concatenate([jnp.stack([part, spot]), starts]).astype(jnp.int32)
    first_head = (spot * SEQ_DEVS + part) * heads
    slopes = jnp.exp2(
        -8.0 * ((first_head + jnp.arange(heads, dtype=jnp.int32)).astype(F32) + 1.0) / H
    )

    def pick(stack):
        return lax.dynamic_index_in_dim(stack, slot, 0, keepdims=False)

    def own_cols(matrix, count):
        return lax.dynamic_slice_in_dim(matrix, spot * count, count, 1)

    a_q, b_q = pick(qkv_down), own_cols(pick(qkv_up), qkv_cols)
    a_o, b_o = own_cols(pick(out_down), ctx_cols), pick(out_up)
    a_1, b_1 = pick(fc1_down), own_cols(pick(fc1_up), hidden_cols)
    a_2, b_2 = own_cols(pick(fc2_down), hidden_cols), pick(fc2_up)

    n = lax.axis_size("dp")
    shard = fc1_weight.shape[0]
    chunks = hidden_cols // shard
    upper, lower = halves(fc1_weight)
    lower = jnp.transpose(lower.reshape(shard // 2, chunks, shard), (1, 0, 2)).reshape(-1, shard)
    fc_rest = jnp.concatenate([lower, fc2_weight], axis=0)
    places = shard_places(out_weight, data)
    home = jnp.stack([group, (data * ring + spot) % groups]).astype(jnp.int32)
    w_qkv, w_starts, h_pieces, (upper, *small) = gather_first(
        qkv_weight,
        hidden_in,
        data,
        (upper, out_weight, fc_rest, places, home)
        + (a_q, b_q, a_o, b_o, a_1, b_1, a_2, b_2, slopes),
    )
    held_out, fc_rest, places, home, a_q, b_q, a_o, b_o, a_1, b_1, a_2, b_2, slopes = small
    w_fc_first = lax.all_gather(upper, "dp", axis=0, tiled=False)
    w_starts = jnp.stack(w_starts).astype(jnp.int32)
    out_stages = gather_shards(out_weight, data)
    flying = out_stages.send(held_out)

    x = halves(hidden_in.astype(F32))
    w_qkv_near, n1_first = prepare_qkv(
        h_pieces[:-1], ln1_gain[None], ln1_bias[None], w_qkv, w_starts
    )
    h_pieces[-1], cotangent_held, flying, w_qkv_near = lax.optimization_barrier(
        (h_pieces[-1], cotangent, flying, w_qkv_near)
    )
    gy = [cotangent, shift_one(cotangent_held, "tensor")]
    flying = out_stages.send(flying)
    pieces, u1, n1 = qkv_product(
        n1_first,
        h_pieces[-1],
        ln1_gain[None],
        ln1_bias[None],
        a_q,
        b_q,
        joined_bias[None],
        w_qkv_near,
        meta,
    )
    pieces, flying, fc_rest = lax.optimization_barrier((pieces, flying, fc_rest))
    flying = out_stages.send(flying)
    w_fc_second = lax.all_gather(fc_rest, "dp", axis=0, tiled=False)
    pieces, (gy, flying) = swap_heads(pieces, (gy, flying))
    gy.append(shift_one(gy[1], "tensor"))
    pieces, qkv_true, out_t, logs = attend_forward(pieces, meta, slopes, ring, rows)
    pieces, gy = lax.optimization_barrier((pieces, gy))
    gy += ring_gather(gy[-1], "tensor", ring - 3)[1:]
    pieces, unused = swap_heads(pieces)
    pieces, gy = lax.optimization_barrier((pieces, gy))
    w_out = out_stages.send(flying)
    part_out, ctx, u2 = out_product(pieces, a_o, b_o, w_out, places, meta, ring, n)
    weights = [w_fc_first, w_fc_second]

    def load_beside(hop, moved):
        if hop == ring - 3:
            moved, weights[:] = lax.optimization_barrier((moved, weights))
        if hop == ring - 2:
            moved, weights[:] = lax.optimization_barrier((moved, load_to_vmem(*weights)))
        return moved

    summed = ring_scatter(part_out, "tensor", load_beside)
    mid = [rows_in + (term + output_bias) for rows_in, term in zip(x, summed)]

    normed2 = [norm_forward(m, ln2_gain, ln2_bias) for m in mid]
    block = [normed.astype(BF) for normed, unused, unused in normed2]
    part_in2, part_mlp, fc_grads = [], [], []
    for k in range(ring):
        following = shift_all(block if k < ring - 1 else part_in2[1], "tensor")
        grad_pieces, out_piece, fc_grads = mlp_both_ways(
            block, gy[k], a_1, b_1, a_2, b_2, first_feed_bias[None], weights, fc_grads
        )
        part_in2.append(grad_pieces)
        part_mlp.append(out_piece)
        block, part_in2[1:], fc_grads = lax.optimization_barrier(
            (following, part_in2[1:], fc_grads)
        )
    g_b1, g_a2, g_a1, g_b2 = fc_grads
    grad_n2 = ring_scatter(part_in2, "tensor", moved=block)
    grad_mid = [
        top.astype(F32) + norm_backward(grad, unit, inverse, ln2_gain)
        for top, grad, (unused, unit, inverse) in zip(halves(cotangent), grad_n2, normed2)
    ]
    gm = [[g.astype(BF) for g in grad_mid]]
    for k in range(ring):
        if k < ring - 1:
            gm.append(shift_all(gm[-1], "tensor"))
    gm = [half for pair in gm for half in pair]

    mlp_total, gm = lax.optimization_barrier((part_mlp[1], gm))
    mlp_total = shift_one(mlp_total, "tensor")
    pieces, g_bo, g_ao = gctx_product(gm, a_o, b_o, w_out, places, ctx, u2, meta, n)
    pieces, mlp_total = swap_heads(pieces, mlp_total)
    (mlp_total,) = add_terms([mlp_total], part_mlp[2:3], BF)
    mlp_total = shift_one(mlp_total, "tensor")
    first, second = attend_backward(pieces, qkv_true, out_t, logs, meta, slopes, ring, rows)
    first, second, mlp_total = lax.optimization_barrier((first, second, mlp_total))
    (mlp_total,) = add_terms([mlp_total], (part_mlp[3:] + part_mlp[:1])[:1], BF)
    mlp_total = shift_one(mlp_total, "tensor")
    landed = swap_start(first)
    w_near = load_rows_to_vmem(w_qkv, w_starts, (qkv_down.shape[2], qkv_cols))
    landed, w_near, second = lax.optimization_barrier((landed, w_near, second))
    first = swap_end(first, landed)
    landed = swap_start(second)
    part_first, q1, gu1 = gn1_first(first, a_q, b_q, w_near, meta)
    for terms in (part_mlp[3:] + part_mlp[:1])[1:]:
        (mlp_total,) = add_terms([mlp_total], [terms], F32)
        if terms is not part_mlp[0]:
            mlp_total = shift_one(mlp_total.astype(BF), "tensor")
    moved = shift_all(part_first, "tensor")
    second = swap_end(second, landed)
    part_rest, late = gn1_rest(
        second,
        q1,
        gu1,
        n1,
        u1,
        a_q,
        b_q,
        w_near,
        [g_bo, g_a1, g_b2],
        [g_ao, g_b1, g_a2],
        meta,
        ring,
        groups,
    )
    moved, part_rest, mlp_total = lax.optimization_barrier((moved, part_rest, mlp_total))
    late.step(())
    part_in1 = part_rest[-1:] + [part_first] + part_rest[:-1]

    def reduce_beside(hop, moved):
        late.step(moved[0])
        return moved

    grad_n1 = ring_scatter(part_in1, "tensor", reduce_beside, moved)
    while late.result is None:
        late.step(())
    layer_output = jnp.concatenate(
        [(m + (t + second_feed_bias)).astype(BF) for m, t in zip(mid, halves(mlp_total))], axis=0
    )
    normed1 = [norm_forward(rows_in, ln1_gain, ln1_bias) for rows_in in x]
    hidden_grad = jnp.concatenate(
        [
            g + norm_backward(grad, unit, inverse, ln1_gain)
            for g, grad, (unused, unit, inverse) in zip(grad_mid, grad_n1, normed1)
        ],
        axis=0,
    )

    (full, full_widths), (own, own_widths) = late.result
    g_aq, g_bo, g_a1, g_b2, g_bq, g_ao, g_b1, g_a2 = place(
        full, full_widths, own, own_widths, home, seq_adapter
    )
    return (layer_output, hidden_grad, g_aq, g_bq, g_ao, g_bo, g_a1, g_b1, g_a2, g_b2)


def solution(mesh):
    rows, cols = P(("dp", "tensor"), None), P(None, None, ("dp", "tensor"))
    placed = (
        rows,
        P(),
        P(),
        P("dp", "tensor"),
        P("tensor"),
        P("tensor", "dp"),
        P(),
        P(),
        P(),
        P("dp", "tensor"),
        P("tensor"),
        P("tensor", "dp"),
    ) + (P(),) * 11 + (rows,)
    return jax.shard_map(
        local,
        mesh=mesh,
        in_specs=placed,
        out_specs=(rows, rows) + (cols,) * 8,
        check_vma=False,
    )
```
